256 devices in a mesh: dp: 16 (over y, x), pass: 8 (over z), tensor: 2 (over core).
Axes of the slice: x: 4, y: 4, z: 8, core: 2. Of those that a mesh axis runs over, the one named last changes fastest.
Arguments:
- question_q: bfloat16 [512, 32, 4096], P(('dp', 'pass'), None, 'tensor'), may hold values from -4.5 to 4.5
- question_grad: bfloat16 [512, 32, 4096], P(('dp', 'pass'), None, 'tensor'), may hold values from -6 to 6
- question_kv: bfloat16 [512, 32, 2, 512], P(('dp', 'pass'), None, None, 'tensor'), may hold values from -4.5 to 4.5
- passage_kv: bfloat16 [256, 256, 2, 512], P(('dp', 'pass'), None, None, 'tensor'), may hold values from -6 to 6
- question_hidden: bfloat16 [512, 32, 4096], P(('dp', 'pass'), 'tensor'), may hold values from -24 to 24
- passage_hidden: bfloat16 [256, 256, 4096], P(('dp', 'pass'), 'tensor'), may hold values from -24 to 24
- reuse: int32 [16, 8, 16], P(None, 'pass'), may hold values from 0 to 31, as said below
- passage_blocks: int32 [16, 8, 2], P(None, 'pass'), may hold values from 1 to 2
Outputs:
- question_dq: bfloat16 [512, 32, 4096], P(('dp', 'pass'), None, 'tensor')
- question_dkv: bfloat16 [512, 32, 2, 512], P(('dp', 'pass'), None, None, 'tensor')
- passage_dkv: bfloat16 [256, 256, 2, 512], P(('dp', 'pass'), None, None, 'tensor')
- weight_grad: float32 [4096, 2, 512], P(('dp', 'pass', 'tensor'))
The draws below stay inside these ranges and needn't reach their ends.
Inputs may be any that keep to these rules, and one draw needn't show every extreme that they name: `reuse`: an entry is owner * 2 + slot, owner being the dp index of the owning device within the same pass group. The 16 entries of one reading device name every owner of its pass group exactly once; entry j belongs to that device's sample j // 4.
All inputs are finite; a program needn't handle non-finite values.
Results may differ from the reference program's by a relative error of at most 0.0068.
Values may be sent and summed in bfloat16 or wider, within the bound.
No kernel may reach another device: no remote copies, remote signals or barrier semaphores. Data moves between devices by JAX's collectives and lax.ppermute only.
A program may use at most 128 MiB of HBM per device.

```python
import jax
import jax.numpy as jnp
from jax import lax

DMODEL = 4096
QH = 32
KVH = 4
HD = 128
BLOCK = 128
LB = 2
PS = 2
RPS = 4
QLEN = 32
NSAMP = 4
SAMPLES = 512
PASSAGES = 256
LPAD = 256
N_DP = 16
N_PASS = 8


def draw_question_q(key, part):
    key = jax.random.fold_in(key, 11)
    base = jnp.clip(jax.random.normal(key, (SAMPLES, QLEN, QH, HD), jnp.float32), -4.5, 4.5)
    return base.reshape(SAMPLES, QLEN, QH * HD).astype(jnp.bfloat16)


def draw_question_kv(key, part):
    key = jax.random.fold_in(key, 12)
    base = jnp.clip(jax.random.normal(key, (SAMPLES, QLEN, 2, KVH, HD), jnp.float32), -4.5, 4.5)
    return base.reshape(SAMPLES, QLEN, 2, KVH * HD).astype(jnp.bfloat16)


def draw_reuse(key, part):
    key = jax.random.fold_in(key, 13)
    keys_all = jax.random.split(key, 5)
    readers = NSAMP * RPS
    order_keys = jax.random.split(keys_all[0], readers * N_PASS)
    order = jax.vmap(lambda single: jax.random.permutation(single, readers))(order_keys).reshape(readers, N_PASS, readers)
    order = order.astype(jnp.int32)
    hot_slot = jax.random.randint(keys_all[1], (N_PASS, readers), 0, PS)
    coin = jax.random.randint(keys_all[2], (readers, N_PASS, readers), 0, 4)
    other_slot = jax.random.randint(keys_all[3], (readers, N_PASS, readers), 0, PS)
    forced = jax.random.randint(keys_all[4], (N_PASS, readers), 0, readers)
    reader_ids = jnp.arange(readers, dtype=jnp.int32)[:, None, None]
    chosen = jnp.where(coin < 3, hot_slot[None], other_slot)
    chosen = jnp.where(reader_ids == (forced[None] + 1) % readers, 0, chosen)
    chosen = jnp.where(reader_ids == forced[None], PS - 1, chosen)
    slot_taken = jnp.take_along_axis(chosen, order, axis=2)
    return (order * PS + slot_taken).astype(jnp.int32)


def set_ends(values, rng, low, largest):
    dims = values.shape
    index_at = [jax.random.randint(jax.random.fold_in(rng, axis), (), 0, dims[axis]) for axis in range(len(dims))]
    values = values.at[tuple(index_at)].set(low)
    longest = dims.index(max(dims))
    index_at[longest] = (index_at[longest] + 1) % dims[longest]
    return values.at[tuple(index_at)].set(largest)


def raised(values, own_key, source, target, parts, factor):
    owner, partner = [(jnp.arange(values.shape[dim]) // (values.shape[dim] // parts)).reshape([-1 if axis == dim else 1 for axis in range(values.ndim)]) for dim in (source, target)]
    chosen = jax.random.permutation(own_key, parts)[partner]
    strong = (owner == chosen) | (owner == (partner + parts // 2) % parts)
    return jnp.where(strong, factor * values, values)


def shard_levels(rng, shape, shards, least, largest):
    loudness, own = 1.0, jax.random.fold_in(rng, 6)
    for dim, blocks in shards:
        heights = jnp.exp(jax.random.uniform(jax.random.fold_in(own, dim), (blocks,), jnp.float32, least / len(shards), largest / len(shards)))
        loudness = loudness * jnp.repeat(heights, shape[dim] // blocks).reshape([-1 if axis == dim else 1 for axis in range(len(shape))])
    return loudness


def scatter_about(key, extent, width, limit, cuts=(), held_as=jnp.bfloat16):
    gain = shard_levels(key, extent, cuts, -0.22, 0.18) if cuts else 1.0
    values = jax.random.normal(key, extent, jnp.float32) * width * gain
    return jnp.minimum(jnp.maximum(values, -limit), limit).astype(held_as)


def noise_with(own_key, extent, deviation, reach, pieces, heavy, kind=jnp.bfloat16):
    drawn = deviation * jax.random.normal(own_key, extent, jnp.float32)
    if pieces:
        drawn = drawn * shard_levels(own_key, extent, pieces, -0.22, 0.18)
    return jnp.clip(raised(drawn, jax.random.fold_in(own_key, 3), *heavy), -reach, reach).astype(kind)


def setup_inputs(seed: int = 0) -> dict:
    key_list = jax.random.split(jax.random.key(seed), 9)
    return {
        "question_q": draw_question_q(jax.random.fold_in(key_list[8], 71), 0),
        "question_grad": scatter_about(key_list[1], (SAMPLES, QLEN, QH * HD), 1.0, 6.0, ((0, 128), (2, 2))),
        "question_kv": draw_question_kv(jax.random.fold_in(key_list[8], 71), 0),
        "passage_kv": scatter_about(key_list[3], (PASSAGES, LPAD, 2, KVH * HD), 1.0, 6.0, ((0, 128), (3, 2))),
        "question_hidden": noise_with(key_list[4], (SAMPLES, QLEN, DMODEL), 1.0, 24.0, ((0, 128), (1, 2)), (0, 2, 128, 5.5)),
        "passage_hidden": noise_with(key_list[5], (PASSAGES, LPAD, DMODEL), 1.0, 24.0, ((0, 128), (1, 2)), (0, 2, 128, 5.5)),
        "reuse": draw_reuse(jax.random.fold_in(key_list[8], 71), 0),
        "passage_blocks": set_ends(jax.random.randint(key_list[7], (N_DP, N_PASS, PS), 1, LB + 1), jax.random.fold_in(key_list[7], 1), 1, LB).astype(jnp.int32),
    }


NEG_FILL = -1.0e30


def key_valid(block_counts, query_len, slot_len):
    position = jnp.arange(slot_len, dtype=jnp.int32)
    passage_ok = (position[None, :] < block_counts[:, None] * BLOCK).reshape(-1)
    query_rows = jnp.arange(query_len, dtype=jnp.int32)
    own_ok = jnp.arange(BLOCK, dtype=jnp.int32)[None, :] <= query_rows[:, None]
    spread = jnp.broadcast_to(passage_ok[None, :], (query_len, passage_ok.shape[0]))
    return jnp.concatenate([spread, own_ok], axis=1)


def attend(queries, out_grad, key_rows, key_ok):
    query_len = queries.shape[0]
    key_count = key_rows.shape[0]
    kv_heads = key_rows.shape[2] // HD
    group_size = queries.shape[1] // HD // kv_heads
    score_scale = HD ** -0.5
    query_heads = queries.reshape(query_len, kv_heads, group_size, HD).astype(jnp.float32)
    grad_heads = out_grad.reshape(query_len, kv_heads, group_size, HD).astype(jnp.float32)
    key_heads = key_rows[:, 0].reshape(key_count, kv_heads, HD).astype(jnp.float32)
    value_heads = key_rows[:, 1].reshape(key_count, kv_heads, HD).astype(jnp.float32)
    scores = jnp.einsum("qgrd,kgd->grqk", query_heads, key_heads) * score_scale
    scores = jnp.where(key_ok[None, None], scores, NEG_FILL)
    row_top = jnp.max(scores, axis=-1, keepdims=True)
    shifted_exp = jnp.exp(scores - row_top)
    attn_prob = shifted_exp / jnp.sum(shifted_exp, axis=-1, keepdims=True)
    prob_low = lax.optimization_barrier(attn_prob.astype(jnp.bfloat16)).astype(jnp.float32)
    prob_grad = jnp.einsum("qgrd,kgd->grqk", grad_heads, value_heads)
    row_delta = jnp.sum(attn_prob * prob_grad, axis=-1, keepdims=True)
    dscore = (attn_prob * (prob_grad - row_delta) * score_scale).astype(jnp.bfloat16)
    dscore = lax.optimization_barrier(dscore).astype(jnp.float32)
    query_grad = jnp.einsum("grqk,kgd->qgrd", dscore, key_heads)
    key_grad = jnp.einsum("grqk,qgrd->kgd", dscore, query_heads)
    value_grad = jnp.einsum("grqk,qgrd->kgd", prob_low, grad_heads)
    stacked = jnp.stack([key_grad.reshape(key_count, kv_heads * HD), value_grad.reshape(key_count, kv_heads * HD)], axis=1)
    return query_grad.reshape(query_len, -1).astype(jnp.bfloat16), stacked.astype(jnp.bfloat16)


def reference(question_q, question_grad, question_kv, passage_kv, question_hidden, passage_hidden, reuse, passage_blocks):
    sample_ids = jnp.arange(SAMPLES, dtype=jnp.int32)
    group_ids = (sample_ids // NSAMP) % N_PASS
    local_refs = reuse.reshape(SAMPLES, RPS)
    global_refs = ((local_refs // PS) * N_PASS + group_ids[:, None]) * PS + local_refs % PS
    block_table = passage_blocks.reshape(PASSAGES)
    pad_rows = jnp.zeros((BLOCK - QLEN, 2, KVH * HD), jnp.bfloat16)

    def sample_step(running, item):
        queries, out_grad, own_rows, ref_ids = item
        passage_rows = passage_kv[ref_ids].reshape(RPS * LPAD, 2, KVH * HD)
        key_rows = jnp.concatenate([passage_rows, own_rows, pad_rows], axis=0)
        query_grad, key_grads = attend(queries, out_grad, key_rows, key_valid(block_table[ref_ids], QLEN, LPAD))
        partial_value = key_grads[:RPS * LPAD].reshape(RPS, LPAD, 2, KVH * HD).astype(jnp.float32)
        running = running.at[ref_ids].add(partial_value)
        return running, (query_grad, key_grads[RPS * LPAD:RPS * LPAD + QLEN])

    start_total = jnp.zeros((PASSAGES, LPAD, 2, KVH * HD), jnp.float32)
    running, (question_dq, question_dkv) = lax.scan(sample_step, start_total, (question_q, question_grad, question_kv, global_refs))
    passage_dkv = running.astype(jnp.bfloat16)
    contract = (((0,), (0,)), ((), ()))
    weight_grad = lax.dot_general(passage_hidden.reshape(PASSAGES * LPAD, DMODEL), passage_dkv.reshape(PASSAGES * LPAD, 2 * KVH * HD), contract, preferred_element_type=jnp.float32)
    weight_grad = weight_grad + lax.dot_general(question_hidden.reshape(SAMPLES * QLEN, DMODEL), question_dkv.reshape(SAMPLES * QLEN, 2 * KVH * HD), contract, preferred_element_type=jnp.float32)
    return question_dq, question_dkv, passage_dkv, weight_grad.reshape(DMODEL, 2, KVH * HD)
```

```python
import functools

import jax
import jax.numpy as jnp
from jax import lax
from jax.experimental import pallas as pl
from jax.experimental.pallas import tpu as pltpu
from jax.sharding import PartitionSpec as P

HD = 128
BLOCK = 128
NEG_FILL = -1e30
SCALE = HD ** (-0.5)
VMEM_LIMIT = 48 * 1024 * 1024
NT = (((1,), (1,)), ((), ()))
TN = (((0,), (0,)), ((), ()))
F32 = jnp.float32
BF16 = jnp.bfloat16


def params():
    return pltpu.CompilerParams(vmem_limit_bytes=VMEM_LIMIT)


def whole():
    return pl.BlockSpec(memory_space=pltpu.VMEM)


def smem():
    return pl.BlockSpec(memory_space=pltpu.SMEM)


def cost(flops, nbytes, trans=0):
    return pl.CostEstimate(flops=flops, bytes_accessed=nbytes, transcendentals=trans)


def head_rows(block, head, group):
    first = head * group
    return jnp.concatenate(
        [block[:, (first + r) * HD : (first + r + 1) * HD] for r in range(group)], axis=0
    )


def send_kernel(slots, refs, me, q_ref, g_ref, out_ref, sems):
    peers = out_ref.shape[0]
    rows = q_ref.shape[1]
    per = peers // q_ref.shape[0]
    copies = []
    for j in range(peers):
        dest = refs[me[0], j] // slots
        for part, src in enumerate((q_ref, g_ref)):
            copy = pltpu.make_async_copy(
                src.at[j // per],
                out_ref.at[dest, pl.ds(part * rows, rows)],
                sems.at[j, part],
            )
            copy.start()
            copies.append(copy)
    for copy in copies:
        copy.wait()


def pack_queries(refs, me, question_q, question_grad, slots):
    samples, rows, width = question_q.shape
    peers = refs.shape[0]
    return pl.pallas_call(
        functools.partial(send_kernel, slots),
        out_shape=jax.ShapeDtypeStruct((peers, 2 * rows, width), BF16),
        in_specs=[smem(), smem(), whole(), whole()],
        out_specs=pl.BlockSpec(memory_space=pl.ANY),
        scratch_shapes=[pltpu.SemaphoreType.DMA((peers, 2))],
        compiler_params=params(),
        cost_estimate=cost(0, 6 * 2**20),
        name="pack_queries",
    )(refs, me, question_q, question_grad)


def scores_t(keys, queries, valid):
    scores = lax.dot_general(keys, queries, NT, preferred_element_type=F32) * SCALE
    return jnp.where(valid, scores, NEG_FILL)


def put_stats(out_ref, index, head, heads, scores, prob_grad):
    top = jnp.max(scores, axis=0, keepdims=True)
    shifted = jnp.exp(scores - top)
    total = jnp.sum(shifted, axis=0, keepdims=True)
    weighted = jnp.sum(shifted * prob_grad, axis=0, keepdims=True)
    out_ref[index, head : head + 1] = top + jnp.log(total)
    out_ref[index, heads + head : heads + head + 1] = weighted / total


def owner_stats_kernel(group, slot_of, blocks, got_ref, k_ref, v_ref, out_ref):
    slot = slot_of[pl.program_id(0)]
    rows = got_ref.shape[1] // 2
    slot_len = k_ref.shape[1]
    heads = k_ref.shape[2] // HD
    shape = (slot_len, group * rows)
    valid = lax.broadcasted_iota(jnp.int32, shape, 0) < blocks[slot] * BLOCK
    for head in range(heads):
        lanes = slice(head * HD, (head + 1) * HD)
        queries = head_rows(got_ref[0, :rows], head, group)
        grads = head_rows(got_ref[0, rows:], head, group)
        scores = scores_t(k_ref[slot, :, lanes], queries, valid)
        prob_grad = lax.dot_general(v_ref[slot, :, lanes], grads, NT, preferred_element_type=F32)
        put_stats(out_ref, 0, head, heads, scores, prob_grad)


def owner_stats(slot_of, blocks, got, keys, values, group):
    peers, both, width = got.shape
    heads = keys.shape[2] // HD
    columns = group * both // 2
    return pl.pallas_call(
        functools.partial(owner_stats_kernel, group),
        out_shape=jax.ShapeDtypeStruct((peers, 2 * heads, columns), F32),
        grid_spec=pltpu.PrefetchScalarGridSpec(
            num_scalar_prefetch=2,
            grid=(peers,),
            in_specs=[
                pl.BlockSpec((1, both, width), lambda r, s, b: (r, 0, 0)),
                whole(),
                whole(),
            ],
            out_specs=pl.BlockSpec((1, 2 * heads, columns), lambda r, s, b: (r, 0, 0)),
        ),
        compiler_params=params(),
        cost_estimate=cost(2 * 10**9, 5 * 2**20, 2 * 10**6),
        name="owner_stats",
    )(slot_of, blocks, got, keys, values)


def own_valid(own_rows, rows, group):
    shape = (own_rows, group * rows)
    key_row = lax.broadcasted_iota(jnp.int32, shape, 0)
    query_row = lax.rem(lax.broadcasted_iota(jnp.int32, shape, 1), jnp.int32(rows))
    return key_row <= query_row


def own_stats_kernel(group, q_ref, g_ref, k_ref, v_ref, out_ref):
    samples, rows, _ = q_ref.shape
    heads = k_ref.shape[2] // HD
    valid = own_valid(rows, rows, group)
    for sample in range(samples):
        for head in range(heads):
            lanes = slice(head * HD, (head + 1) * HD)
            queries = head_rows(q_ref[sample], head, group)
            grads = head_rows(g_ref[sample], head, group)
            scores = scores_t(k_ref[sample, :, lanes], queries, valid)
            prob_grad = lax.dot_general(
                v_ref[sample, :, lanes], grads, NT, preferred_element_type=F32
            )
            put_stats(out_ref, sample, head, heads, scores, prob_grad)


def own_stats(question_q, question_grad, keys, values, group):
    samples, rows, _ = question_q.shape
    heads = keys.shape[2] // HD
    return pl.pallas_call(
        functools.partial(own_stats_kernel, group),
        out_shape=jax.ShapeDtypeStruct((samples, 2 * heads, group * rows), F32),
        in_specs=[whole()] * 4,
        out_specs=whole(),
        compiler_params=params(),
        cost_estimate=cost(10**8, 2**20, 10**5),
        name="own_stats",
    )(question_q, question_grad, keys, values)


def merge_kernel(slots, refs, me, st_ref, own_ref, back_ref, merged_ref):
    samples, stat_rows, _ = own_ref.shape
    heads = stat_rows // 2
    per = st_ref.shape[0] // samples
    for sample in range(samples):
        owners = [refs[me[0], sample * per + k] // slots for k in range(per)]
        parts = [own_ref[sample]] + [st_ref[owner] for owner in owners]
        logs = [part[:heads] for part in parts]
        top = functools.reduce(jnp.maximum, logs)
        total = sum(jnp.exp(one - top) for one in logs)
        joint = top + jnp.log(total)
        delta = sum(jnp.exp(one - joint) * part[heads:] for one, part in zip(logs, parts))
        both = jnp.concatenate([joint, delta], axis=0)
        merged_ref[sample] = both
        for owner in owners:
            back_ref[owner] = both


def merge(refs, me, stats, own, slots):
    return pl.pallas_call(
        functools.partial(merge_kernel, slots),
        out_shape=(
            jax.ShapeDtypeStruct(stats.shape, F32),
            jax.ShapeDtypeStruct(own.shape, F32),
        ),
        in_specs=[smem(), smem(), whole(), whole()],
        out_specs=(whole(), whole()),
        compiler_params=params(),
        cost_estimate=cost(10**5, 2**17, 10**4),
        name="merge_stats",
    )(refs, me, stats, own)


def probs_and_dscore(scores, prob_grad, joint, delta):
    probs = jnp.exp(scores - joint)
    dscore = (probs * (prob_grad - delta) * SCALE).astype(BF16)
    return probs.astype(BF16), dscore


def owner_grads_kernel(
    group, slot_of, blocks, got_ref, joint_ref, k_ref, v_ref, grad_ref, dq_ref, acc_ref
):
    step = pl.program_id(0)
    slot = slot_of[step]
    rows = got_ref.shape[1] // 2
    slot_len = k_ref.shape[1]
    width = k_ref.shape[2]
    heads = width // HD
    shape = (slot_len, group * rows)
    valid = lax.broadcasted_iota(jnp.int32, shape, 0) < blocks[slot] * BLOCK

    @pl.when(step == 0)
    def _():
        acc_ref[...] = jnp.zeros_like(acc_ref)

    for head in range(heads):
        lanes = slice(head * HD, (head + 1) * HD)
        value_lanes = slice(width + head * HD, width + (head + 1) * HD)
        queries = head_rows(got_ref[0, :rows], head, group)
        grads = head_rows(got_ref[0, rows:], head, group)
        keys = k_ref[slot, :, lanes]
        scores = scores_t(keys, queries, valid)
        prob_grad = lax.dot_general(v_ref[slot, :, lanes], grads, NT, preferred_element_type=F32)
        joint = joint_ref[0, head : head + 1]
        delta = joint_ref[0, heads + head : heads + head + 1]
        probs, dscore = probs_and_dscore(scores, prob_grad, joint, delta)
        acc_ref[slot, :, lanes] += jnp.dot(dscore, queries, preferred_element_type=F32)
        acc_ref[slot, :, value_lanes] += jnp.dot(probs, grads, preferred_element_type=F32)
        dq = lax.dot_general(dscore, keys, TN, preferred_element_type=F32).astype(BF16)
        for r in range(group):
            column = (head * group + r) * HD
            dq_ref[0, :, column : column + HD] = dq[r * rows : (r + 1) * rows]

    @pl.when(step == pl.num_programs(0) - 1)
    def _():
        for one in range(acc_ref.shape[0]):
            grad_ref[one * slot_len : (one + 1) * slot_len] = acc_ref[one].astype(BF16)


def owner_grads(slot_of, blocks, got, joint, keys, values, group):
    peers, both, width = got.shape
    slots, slot_len, key_width = keys.shape
    stat_rows, columns = joint.shape[1:]
    return pl.pallas_call(
        functools.partial(owner_grads_kernel, group),
        out_shape=(
            jax.ShapeDtypeStruct((slots * slot_len, 2 * key_width), BF16),
            jax.ShapeDtypeStruct((peers, both // 2, width), BF16),
        ),
        grid_spec=pltpu.PrefetchScalarGridSpec(
            num_scalar_prefetch=2,
            grid=(peers,),
            in_specs=[
                pl.BlockSpec((1, both, width), lambda r, s, b: (r, 0, 0)),
                pl.BlockSpec((1, stat_rows, columns), lambda r, s, b: (r, 0, 0)),
                whole(),
                whole(),
            ],
            out_specs=(
                pl.BlockSpec((slots * slot_len, 2 * key_width), lambda r, s, b: (0, 0)),
                pl.BlockSpec((1, both // 2, width), lambda r, s, b: (r, 0, 0)),
            ),
            scratch_shapes=[pltpu.VMEM((slots, slot_len, 2 * key_width), F32)],
        ),
        compiler_params=params(),
        cost_estimate=cost(5 * 10**9, 8 * 2**20, 2 * 10**6),
        name="owner_grads",
    )(slot_of, blocks, got, joint, keys, values)


def own_grads_kernel(group, q_ref, g_ref, k_ref, v_ref, joint_ref, grad_ref, dq_ref):
    samples, rows, _ = q_ref.shape
    width = k_ref.shape[2]
    heads = width // HD
    valid = own_valid(rows, rows, group)
    for sample in range(samples):
        token = slice(sample * rows, (sample + 1) * rows)
        for head in range(heads):
            lanes = slice(head * HD, (head + 1) * HD)
            value_lanes = slice(width + head * HD, width + (head + 1) * HD)
            queries = head_rows(q_ref[sample], head, group)
            grads = head_rows(g_ref[sample], head, group)
            keys = k_ref[sample, :, lanes]
            scores = scores_t(keys, queries, valid)
            prob_grad = lax.dot_general(
                v_ref[sample, :, lanes], grads, NT, preferred_element_type=F32
            )
            joint = joint_ref[sample, head : head + 1]
            delta = joint_ref[sample, heads + head : heads + head + 1]
            probs, dscore = probs_and_dscore(scores, prob_grad, joint, delta)
            key_grad = jnp.dot(dscore, queries, preferred_element_type=F32)
            value_grad = jnp.dot(probs, grads, preferred_element_type=F32)
            grad_ref[token, lanes] = key_grad.astype(BF16)
            grad_ref[token, value_lanes] = value_grad.astype(BF16)
            dq = lax.dot_general(dscore, keys, TN, preferred_element_type=F32)
            for r in range(group):
                column = (head * group + r) * HD
                dq_ref[sample, :, column : column + HD] = dq[r * rows : (r + 1) * rows]


def own_grads(question_q, question_grad, keys, values, joint, group):
    samples, rows, width = question_q.shape
    key_width = keys.shape[2]
    return pl.pallas_call(
        functools.partial(own_grads_kernel, group),
        out_shape=(
            jax.ShapeDtypeStruct((samples * rows, 2 * key_width), BF16),
            jax.ShapeDtypeStruct((samples, rows, width), F32),
        ),
        in_specs=[whole()] * 5,
        out_specs=(whole(), whole()),
        compiler_params=params(),
        cost_estimate=cost(3 * 10**8, 3 * 2**20, 10**5),
        name="own_grads",
    )(question_q, question_grad, keys, values, joint)


def sum_dq_kernel(owners, *refs):
    out_ref = refs[-1]
    total = refs[-2][0]
    for ref in refs[:-2]:
        total = total + ref[0].astype(F32)
    out_ref[0] = total.astype(BF16)


def sum_dq(owners, returned, own):
    samples, rows, width = own.shape
    per = returned.shape[0] // samples

    def from_owner(k):
        return pl.BlockSpec((1, rows, width), lambda s, o: (o[s * per + k], 0, 0))

    return pl.pallas_call(
        sum_dq_kernel,
        out_shape=jax.ShapeDtypeStruct((samples, rows, width), BF16),
        grid_spec=pltpu.PrefetchScalarGridSpec(
            num_scalar_prefetch=1,
            grid=(samples,),
            in_specs=[from_owner(k) for k in range(per)]
            + [pl.BlockSpec((1, rows, width), lambda s, o: (s, 0, 0))],
            out_specs=pl.BlockSpec((1, rows, width), lambda s, o: (s, 0, 0)),
        ),
        compiler_params=params(),
        cost_estimate=cost(2 * 10**6, 4 * 2**20),
        name="sum_dq",
    )(owners, *([returned] * per), own)


def transpose_kernel(p_ref, q_ref, out_ref):
    split = p_ref.shape[0]
    out_ref[:, :split] = p_ref[...].T
    out_ref[:, split:] = q_ref[...].T


def transpose_hidden(flat_pass, flat_query):
    count, width = flat_pass.shape
    extra = flat_query.shape[0]
    tile = 512
    return pl.pallas_call(
        transpose_kernel,
        out_shape=jax.ShapeDtypeStruct((width, count + extra), BF16),
        grid=(width // tile,),
        in_specs=[
            pl.BlockSpec((count, tile), lambda i: (0, i)),
            pl.BlockSpec((extra, tile), lambda i: (0, i)),
        ],
        out_specs=pl.BlockSpec((tile, count + extra), lambda i: (i, 0)),
        compiler_params=params(),
        cost_estimate=cost(0, 12 * 2**20),
        name="transpose_hidden",
    )(flat_pass, flat_query)


def weight_kernel(h_ref, p_ref, q_ref, out_ref):
    split = p_ref.shape[0]
    groups, owners, rows, width = out_ref.shape
    total = jnp.dot(h_ref[:, :split], p_ref[...], preferred_element_type=F32)
    total = total + jnp.dot(h_ref[:, split:], q_ref[...], preferred_element_type=F32)
    total = total.astype(BF16)
    for owner in range(owners):
        for group in range(groups):
            first = (owner * groups + group) * rows
            out_ref[group, owner] = total[first : first + rows]


def weight_terms(hidden_t, grads_pass, grads_query, owners, groups):
    model_width, tokens = hidden_t.shape
    width = grads_pass.shape[1]
    rows = model_width // (owners * groups)
    per = 2
    return pl.pallas_call(
        weight_kernel,
        out_shape=jax.ShapeDtypeStruct((groups, owners, rows, width), BF16),
        grid=(owners // per,),
        in_specs=[
            pl.BlockSpec((per * groups * rows, tokens), lambda i: (i, 0)),
            whole(),
            whole(),
        ],
        out_specs=pl.BlockSpec((groups, per, rows, width), lambda i: (0, i, 0, 0)),
        compiler_params=params(),
        cost_estimate=cost(2 * model_width * tokens * width, 10 * 2**20),
        name="weight_terms",
    )(hidden_t, grads_pass, grads_query)


def finish_kernel(x_ref, out_ref):
    owners, cores, rows, width = x_ref.shape
    half = width // 2
    for core in range(cores):
        total = x_ref[0, core].astype(F32)
        for owner in range(1, owners):
            total = total + x_ref[owner, core].astype(F32)
        lanes = slice(core * half, (core + 1) * half)
        out_ref[:, 0, lanes] = total[:, :half]
        out_ref[:, 1, lanes] = total[:, half:]


def finish_weights(parts):
    owners, cores, rows, width = parts.shape
    return pl.pallas_call(
        finish_kernel,
        out_shape=jax.ShapeDtypeStruct((rows, 2, cores * width // 2), F32),
        in_specs=[whole()],
        out_specs=whole(),
        compiler_params=params(),
        cost_estimate=cost(10**6, 2**20),
        name="finish_weights",
    )(parts)


def local(
    question_q,
    question_grad,
    question_kv,
    passage_kv,
    question_hidden,
    passage_hidden,
    reuse,
    passage_blocks,
):
    me = lax.axis_index("dp")
    me_array = me.reshape(1)
    peers = lax.axis_size("dp")
    groups = lax.axis_size("pass")
    cores = lax.axis_size("tensor")
    slots, slot_len, _, channels = passage_kv.shape
    samples, rows, width = question_q.shape
    group = width // channels
    refs = reuse.reshape(reuse.shape[0], reuse.shape[2])

    def exchange(x):
        return lax.all_to_all(x, "dp", split_axis=0, concat_axis=0, tiled=True)

    packed = pack_queries(refs, me_array, question_q, question_grad, slots)
    got = exchange(packed)

    slot_of = jnp.sum(jnp.where(refs // slots == me, refs % slots, 0), axis=1)
    owners = lax.dynamic_index_in_dim(refs, me, 0, keepdims=False) // slots
    blocks = lax.dynamic_index_in_dim(passage_blocks, me, 0, keepdims=False).reshape(slots)
    keys, values = passage_kv[:, :, 0], passage_kv[:, :, 1]
    own_keys, own_values = question_kv[:, :, 0], question_kv[:, :, 1]
    own = own_stats(question_q, question_grad, own_keys, own_values, group)

    full_pass = lax.all_gather(passage_hidden, "tensor", axis=1, tiled=True)
    full_query = lax.all_gather(question_hidden, "tensor", axis=1, tiled=True)
    model_width = passage_hidden.shape[2]
    hidden_t = transpose_hidden(
        full_pass.reshape(-1, model_width), full_query.reshape(-1, model_width)
    )

    stats = owner_stats(slot_of, blocks, got, keys, values, group)
    back, merged = merge(refs, me_array, exchange(stats), own, slots)
    joint = exchange(back)
    grads_query, own_dq = own_grads(
        question_q, question_grad, own_keys, own_values, merged, group
    )
    grads_pass, dq_parts = owner_grads(slot_of, blocks, got, joint, keys, values, group)

    terms = weight_terms(hidden_t, grads_pass, grads_query, peers, groups)
    summed = lax.psum_scatter(terms, "pass", scatter_dimension=0, tiled=False)
    question_dq = sum_dq(owners, exchange(dq_parts), own_dq)

    share = summed.shape[1] // cores
    parts = lax.all_to_all(
        summed.reshape(peers * cores, share, -1),
        ("dp", "tensor"),
        split_axis=0,
        concat_axis=0,
        tiled=True,
    )
    weight_grad = finish_weights(parts.reshape(peers, cores, share, -1))
    question_dkv = grads_query.reshape(samples, rows, 2, channels)
    passage_dkv = grads_pass.reshape(slots, slot_len, 2, channels)
    return (question_dq, question_dkv, passage_dkv, weight_grad)


def solution(mesh):
    in_specs = (
        P(("dp", "pass"), None, "tensor"),
        P(("dp", "pass"), None, "tensor"),
        P(("dp", "pass"), None, None, "tensor"),
        P(("dp", "pass"), None, None, "tensor"),
        P(("dp", "pass"), "tensor", None),
        P(("dp", "pass"), "tensor", None),
        P(None, "pass", None),
        P(None, "pass", None),
    )
    out_specs = (
        P(("dp", "pass"), None, "tensor"),
        P(("dp", "pass"), None, None, "tensor"),
        P(("dp", "pass"), None, None, "tensor"),
        P(("dp", "pass", "tensor"), None, None),
    )
    return jax.shard_map(local, mesh=mesh, in_specs=in_specs, out_specs=out_specs, check_vma=False)
```

```python
import functools
import math

import jax
import jax.numpy as jnp
from jax import lax
from jax.experimental import pallas as pl
from jax.experimental.pallas import tpu as pltpu
from jax.sharding import PartitionSpec as P

HD = 128
BLOCK = 128
NEG_FILL = -1e30
SCALE = HD ** (-0.5)
SCALE_LOG2 = SCALE * math.log2(math.e)
VMEM_LIMIT = 48 * 1024 * 1024
NT = (((1,), (1,)), ((), ()))
TN = (((0,), (0,)), ((), ()))
F32 = jnp.float32
BF16 = jnp.bfloat16


def params():
    return pltpu.CompilerParams(vmem_limit_bytes=VMEM_LIMIT)


def whole():
    return pl.BlockSpec(memory_space=pltpu.VMEM)


def smem():
    return pl.BlockSpec(memory_space=pltpu.SMEM)


def anywhere():
    return pl.BlockSpec(memory_space=pl.ANY)


def cost(flops, nbytes, trans=0):
    return pl.CostEstimate(flops=flops, bytes_accessed=nbytes, transcendentals=trans)


def quotient(value, divisor):
    return lax.div(value, jnp.int32(divisor))


def head_rows(block, head, group):
    first = head * group
    return jnp.concatenate(
        [block[:, (first + r) * HD : (first + r + 1) * HD] for r in range(group)], axis=0
    )


def pack_kernel(slots, refs, me, q_ref, g_ref, out_ref, held, load_sems, sems):
    peers = out_ref.shape[0]
    samples, rows, _ = q_ref.shape
    per = peers // samples
    loads = []
    for sample in range(samples):
        pair = []
        for part, src in enumerate((q_ref, g_ref)):
            pair.append(
                pltpu.make_async_copy(
                    src.at[sample],
                    held.at[sample, pl.ds(part * rows, rows)],
                    load_sems.at[sample, part],
                )
            )
            pair[-1].start()
        loads.append(pair)
    copies = []
    for j in range(peers):
        sample = j // per
        if j % per == 0:
            for copy in loads[sample]:
                copy.wait()
        dest = quotient(refs[me[0], j], slots)
        copy = pltpu.make_async_copy(held.at[sample], out_ref.at[dest], sems.at[j])
        copy.start()
        copies.append(copy)
    for copy in copies:
        copy.wait()


def pack_queries(refs, me, question_q, question_grad, slots):
    samples, rows, width = question_q.shape
    peers = refs.shape[0]
    return pl.pallas_call(
        functools.partial(pack_kernel, slots),
        out_shape=jax.ShapeDtypeStruct((peers, 2 * rows, width), BF16),
        in_specs=[smem(), smem(), anywhere(), anywhere()],
        out_specs=anywhere(),
        scratch_shapes=[
            pltpu.VMEM((samples, 2 * rows, width), BF16),
            pltpu.SemaphoreType.DMA((samples, 2)),
            pltpu.SemaphoreType.DMA((peers,)),
        ],
        compiler_params=params(),
        cost_estimate=cost(0, 6 * 2**20),
        name="pack_queries",
    )(refs, me, question_q, question_grad)


def scores_t(keys, queries, valid):
    scores = lax.dot_general(keys, queries, NT, preferred_element_type=F32) * SCALE_LOG2
    return jnp.where(valid, scores, NEG_FILL)


def part_stats(scores, prob_grad):
    top = jnp.max(scores, axis=0, keepdims=True)
    shifted = jnp.exp2(scores - top)
    total = jnp.sum(shifted, axis=0, keepdims=True)
    weighted = jnp.sum(shifted * prob_grad, axis=0, keepdims=True)
    return top + jnp.log2(total), weighted / total


def passage_valid(blocks, slot, slot_len, columns):
    shape = (slot_len, columns)
    return lax.broadcasted_iota(jnp.int32, shape, 0) < blocks[slot] * BLOCK


def owner_stats_kernel(group, slot_of, blocks, got_ref, k_ref, v_ref, own_ref, out_ref):
    step = pl.program_id(0)
    last = pl.num_programs(0) - 1
    per, both, _ = got_ref.shape
    rows = both // 2
    peers = out_ref.shape[0]
    slot_len = k_ref.shape[1]
    heads = k_ref.shape[2] // HD
    columns = group * rows

    @pl.when(step < last)
    def _():
        for one in range(per):
            slot = slot_of[step * per + one]
            valid = passage_valid(blocks, slot, slot_len, columns)
            logs, deltas = [], []
            for head in range(heads):
                lanes = slice(head * HD, (head + 1) * HD)
                queries = head_rows(got_ref[one, :rows], head, group)
                grads = head_rows(got_ref[one, rows:], head, group)
                scores = scores_t(k_ref[slot, :, lanes], queries, valid)
                prob_grad = lax.dot_general(
                    v_ref[slot, :, lanes], grads, NT, preferred_element_type=F32
                )
                log, delta = part_stats(scores, prob_grad)
                logs.append(log)
                deltas.append(delta)
            both_stats = jnp.concatenate(logs + deltas, axis=0)
            for peer in range(peers):
                out_ref[peer, one] = both_stats

    @pl.when(step == last)
    def _():
        for peer in range(peers):
            out_ref[peer] = own_ref[...]


def owner_stats(slot_of, blocks, got, keys, values, own, group):
    peers, both, width = got.shape
    samples, stat_rows, columns = own.shape
    steps = peers // samples
    return pl.pallas_call(
        functools.partial(owner_stats_kernel, group),
        out_shape=jax.ShapeDtypeStruct((peers, peers + samples, stat_rows, columns), F32),
        grid_spec=pltpu.PrefetchScalarGridSpec(
            num_scalar_prefetch=2,
            grid=(steps + 1,),
            in_specs=[
                pl.BlockSpec(
                    (samples, both, width), lambda r, s, b: (jnp.minimum(r, steps - 1), 0, 0)
                ),
                whole(),
                whole(),
                whole(),
            ],
            out_specs=pl.BlockSpec(
                (peers, samples, stat_rows, columns), lambda r, s, b: (0, r, 0, 0)
            ),
        ),
        compiler_params=params(),
        cost_estimate=cost(2 * 10**9, 6 * 2**20, 2 * 10**6),
        name="owner_stats",
    )(slot_of, blocks, got, keys, values, own)


def own_valid(own_rows, rows, group):
    shape = (own_rows, group * rows)
    key_row = lax.broadcasted_iota(jnp.int32, shape, 0)
    query_row = lax.rem(lax.broadcasted_iota(jnp.int32, shape, 1), jnp.int32(rows))
    return key_row <= query_row


def own_stats_kernel(group, q_ref, g_ref, k_ref, v_ref, out_ref):
    samples, rows, _ = q_ref.shape
    heads = k_ref.shape[2] // HD
    valid = own_valid(rows, rows, group)
    for sample in range(samples):
        logs, deltas = [], []
        for head in range(heads):
            lanes = slice(head * HD, (head + 1) * HD)
            queries = head_rows(q_ref[sample], head, group)
            grads = head_rows(g_ref[sample], head, group)
            scores = scores_t(k_ref[sample, :, lanes], queries, valid)
            prob_grad = lax.dot_general(
                v_ref[sample, :, lanes], grads, NT, preferred_element_type=F32
            )
            log, delta = part_stats(scores, prob_grad)
            logs.append(log)
            deltas.append(delta)
        out_ref[sample] = jnp.concatenate(logs + deltas, axis=0)


def own_stats(question_q, question_grad, keys, values, group):
    samples, rows, _ = question_q.shape
    heads = keys.shape[2] // HD
    return pl.pallas_call(
        functools.partial(own_stats_kernel, group),
        out_shape=jax.ShapeDtypeStruct((samples, 2 * heads, group * rows), F32),
        in_specs=[whole()] * 4,
        out_specs=whole(),
        compiler_params=params(),
        cost_estimate=cost(10**8, 2**20, 10**5),
        name="own_stats",
    )(question_q, question_grad, keys, values)


def joint_stats(all_ref, refs, reader, sample, per, slots, head, heads):
    peers = all_ref.shape[0]
    parts = [all_ref[reader, peers + sample]]
    for k in range(per):
        parts.append(all_ref[quotient(refs[reader, sample * per + k], slots), reader])
    logs = [part[head : head + 1] for part in parts]
    deltas = [part[heads + head : heads + head + 1] for part in parts]
    top = functools.reduce(jnp.maximum, logs)
    weights = [jnp.exp2(log - top) for log in logs]
    total = sum(weights)
    delta = sum(weight * one for weight, one in zip(weights, deltas)) / total
    return top + jnp.log2(total), delta


def probs_and_dscore(scores, prob_grad, joint, delta):
    probs = jnp.exp2(scores - joint)
    dscore = (probs * (prob_grad - delta) * SCALE).astype(BF16)
    return probs.astype(BF16), dscore


def owner_grads_kernel(
    group,
    slots,
    head,
    slot_of,
    blocks,
    refs,
    entry_of,
    got_ref,
    all_ref,
    k_ref,
    v_ref,
    grad_ref,
    dq_ref,
    acc_ref,
):
    step = pl.program_id(0)
    per, both, _ = got_ref.shape
    rows = both // 2
    slot_len = k_ref.shape[1]
    heads = k_ref.shape[2] // HD
    peers = all_ref.shape[0]
    entries = peers // (all_ref.shape[1] - peers)
    lanes = slice(head * HD, (head + 1) * HD)

    @pl.when(step == 0)
    def _():
        acc_ref[...] = jnp.zeros_like(acc_ref)

    for one in range(per):
        reader = step * per + one
        slot = slot_of[reader]
        sample = quotient(entry_of[reader], entries)
        joint, delta = joint_stats(all_ref, refs, reader, sample, entries, slots, head, heads)
        valid = passage_valid(blocks, slot, slot_len, group * rows)
        queries = head_rows(got_ref[one, :rows], 0, group)
        grads = head_rows(got_ref[one, rows:], 0, group)
        keys = k_ref[slot, :, lanes]
        scores = scores_t(keys, queries, valid)
        prob_grad = lax.dot_general(v_ref[slot, :, lanes], grads, NT, preferred_element_type=F32)
        probs, dscore = probs_and_dscore(scores, prob_grad, joint, delta)
        acc_ref[slot, :, :HD] += jnp.dot(dscore, queries, preferred_element_type=F32)
        acc_ref[slot, :, HD:] += jnp.dot(probs, grads, preferred_element_type=F32)
        dq = lax.dot_general(dscore, keys, TN, preferred_element_type=F32).astype(BF16)
        for r in range(group):
            dq_ref[one, :, r * HD : (r + 1) * HD] = dq[r * rows : (r + 1) * rows]

    @pl.when(step == pl.num_programs(0) - 1)
    def _():
        for one in range(acc_ref.shape[0]):
            grad_ref[one * slot_len : (one + 1) * slot_len] = acc_ref[one].astype(BF16)


def owner_grads(head, slot_of, blocks, refs, entry_of, got, stats, keys, values, group):
    peers, both, _ = got.shape
    slots, slot_len, _ = keys.shape
    per = stats.shape[1] - peers
    width = group * HD
    return pl.pallas_call(
        functools.partial(owner_grads_kernel, group, slots, head),
        out_shape=(
            jax.ShapeDtypeStruct((slots * slot_len, 2 * HD), BF16),
            jax.ShapeDtypeStruct((peers, both // 2, width), BF16),
        ),
        grid_spec=pltpu.PrefetchScalarGridSpec(
            num_scalar_prefetch=4,
            grid=(peers // per,),
            in_specs=[
                pl.BlockSpec((per, both, width), lambda r, *_: (r, 0, head)),
                whole(),
                whole(),
                whole(),
            ],
            out_specs=(
                pl.BlockSpec((slots * slot_len, 2 * HD), lambda r, *_: (0, 0)),
                pl.BlockSpec((per, both // 2, width), lambda r, *_: (r, 0, 0)),
            ),
            scratch_shapes=[pltpu.VMEM((slots, slot_len, 2 * HD), F32)],
        ),
        compiler_params=params(),
        cost_estimate=cost(5 * 10**9, 8 * 2**20, 2 * 10**6),
        name=f"owner_grads_{head}",
    )(slot_of, blocks, refs, entry_of, got, stats, keys, values)


def own_grads_kernel(
    group, slots, refs, me, q_ref, g_ref, k_ref, v_ref, all_ref, grad_ref, dq_ref
):
    samples, rows, _ = q_ref.shape
    heads = k_ref.shape[2] // HD
    entries = all_ref.shape[0] // samples
    valid = own_valid(rows, rows, group)
    for sample in range(samples):
        token = slice(sample * rows, (sample + 1) * rows)
        for head in range(heads):
            lanes = slice(head * HD, (head + 1) * HD)
            joint, delta = joint_stats(all_ref, refs, me[0], sample, entries, slots, head, heads)
            queries = head_rows(q_ref[sample], head, group)
            grads = head_rows(g_ref[sample], head, group)
            keys = k_ref[sample, :, lanes]
            scores = scores_t(keys, queries, valid)
            prob_grad = lax.dot_general(
                v_ref[sample, :, lanes], grads, NT, preferred_element_type=F32
            )
            probs, dscore = probs_and_dscore(scores, prob_grad, joint, delta)
            key_grad = jnp.dot(dscore, queries, preferred_element_type=F32)
            value_grad = jnp.dot(probs, grads, preferred_element_type=F32)
            grad_ref[head, token, :HD] = key_grad.astype(BF16)
            grad_ref[head, token, HD:] = value_grad.astype(BF16)
            dq = lax.dot_general(dscore, keys, TN, preferred_element_type=F32)
            for r in range(group):
                column = (head * group + r) * HD
                dq_ref[sample, :, column : column + HD] = dq[r * rows : (r + 1) * rows]


def own_grads(refs, me, question_q, question_grad, keys, values, stats, group, slots):
    samples, rows, width = question_q.shape
    heads = keys.shape[2] // HD
    return pl.pallas_call(
        functools.partial(own_grads_kernel, group, slots),
        out_shape=(
            jax.ShapeDtypeStruct((heads, samples * rows, 2 * HD), BF16),
            jax.ShapeDtypeStruct((samples, rows, width), F32),
        ),
        in_specs=[smem(), smem()] + [whole()] * 5,
        out_specs=(whole(), whole()),
        compiler_params=params(),
        cost_estimate=cost(3 * 10**8, 3 * 2**20, 10**5),
        name="own_grads",
    )(refs, me, question_q, question_grad, keys, values, stats)


def sum_dq_kernel(heads, owners, *refs):
    out_ref = refs[-1]
    own_ref = refs[-2]
    per = (len(refs) - 2) // heads
    width = refs[0].shape[2]
    for head in range(heads):
        lanes = slice(head * width, (head + 1) * width)
        total = own_ref[0, :, lanes]
        for ref in refs[head * per : (head + 1) * per]:
            total = total + ref[0].astype(F32)
        out_ref[0, :, lanes] = total.astype(BF16)


def sum_dq(owners, returned, own):
    samples, rows, width = own.shape
    per = owners.shape[0] // samples
    heads = len(returned)

    def from_owner(k):
        return pl.BlockSpec((1, rows, width // heads), lambda s, o: (o[s * per + k], 0, 0))

    return pl.pallas_call(
        functools.partial(sum_dq_kernel, heads),
        out_shape=jax.ShapeDtypeStruct((samples, rows, width), BF16),
        grid_spec=pltpu.PrefetchScalarGridSpec(
            num_scalar_prefetch=1,
            grid=(samples,),
            in_specs=[from_owner(k) for k in range(per)] * heads
            + [pl.BlockSpec((1, rows, width), lambda s, o: (s, 0, 0))],
            out_specs=pl.BlockSpec((1, rows, width), lambda s, o: (s, 0, 0)),
        ),
        compiler_params=params(),
        cost_estimate=cost(2 * 10**6, 4 * 2**20),
        name="sum_dq",
    )(owners, *[one for one in returned for _ in range(per)], own)


def transpose_kernel(slots, samples, owners, core, mine_p, other_p, mine_q, other_q, out_ref):
    groups, share, _ = out_ref.shape
    lower = core[0] == 0
    first_p = jnp.where(lower, mine_p[...], other_p[...])
    second_p = jnp.where(lower, other_p[...], mine_p[...])
    first_q = jnp.where(lower, mine_q[...], other_q[...])
    second_q = jnp.where(lower, other_q[...], mine_q[...])
    half = first_p.shape[0] // slots
    part = first_q.shape[0] // samples
    pieces = []
    for slot in range(slots):
        pieces.append(first_p[slot * half : (slot + 1) * half])
        pieces.append(second_p[slot * half : (slot + 1) * half])
    for sample in range(samples):
        pieces.append(first_q[sample * part : (sample + 1) * part])
        pieces.append(second_q[sample * part : (sample + 1) * part])
    turned = jnp.concatenate(pieces, axis=0).T
    rows = share // owners
    for owner in range(owners):
        for group in range(groups):
            first = (owner * groups + group) * rows
            out_ref[group, owner * rows : (owner + 1) * rows] = turned[first : first + rows]


def transpose_hidden(core, mine_p, other_p, mine_q, other_q, slots, samples, owners, groups):
    width = mine_p.shape[1]
    tokens = 2 * (mine_p.shape[0] + mine_q.shape[0])
    per = 2
    tile = per * width // owners
    return pl.pallas_call(
        functools.partial(transpose_kernel, slots, samples, per),
        out_shape=jax.ShapeDtypeStruct((groups, width // groups, tokens), BF16),
        grid_spec=pltpu.PrefetchScalarGridSpec(
            num_scalar_prefetch=1,
            grid=(width // tile,),
            in_specs=[
                pl.BlockSpec((one.shape[0], tile), lambda i, c: (0, i))
                for one in (mine_p, other_p, mine_q, other_q)
            ],
            out_specs=pl.BlockSpec((groups, tile // groups, tokens), lambda i, c: (0, i, 0)),
        ),
        compiler_params=params(),
        cost_estimate=cost(0, 12 * 2**20),
        name="transpose_hidden",
    )(core, mine_p, other_p, mine_q, other_q)


def weight_kernel(h_ref, p_ref, q_ref, out_ref):
    split = p_ref.shape[0]
    for one in range(h_ref.shape[0]):
        total = jnp.dot(h_ref[one, :, :split], p_ref[...], preferred_element_type=F32)
        total = total + jnp.dot(h_ref[one, :, split:], q_ref[...], preferred_element_type=F32)
        out_ref[one] = total.astype(BF16)


def weight_terms(hidden_t, grads_pass, grads_query, head):
    groups, share, tokens = hidden_t.shape
    width = grads_pass.shape[1]
    per = 2
    return pl.pallas_call(
        weight_kernel,
        out_shape=jax.ShapeDtypeStruct((groups, share, width), BF16),
        grid=(groups // per,),
        in_specs=[
            pl.BlockSpec((per, share, tokens), lambda i: (i, 0, 0)),
            whole(),
            whole(),
        ],
        out_specs=pl.BlockSpec((per, share, width), lambda i: (i, 0, 0)),
        compiler_params=params(),
        cost_estimate=cost(2 * groups * share * tokens * width, 8 * 2**20),
        name=f"weight_terms_{head}",
    )(hidden_t, grads_pass, grads_query)


def add_low(one, other):
    return (one.astype(F32) + other.astype(F32)).astype(BF16)


def reduce_over_pass(sets):
    me = lax.axis_index("pass")
    count = lax.axis_size("pass")
    right = [(i, (i + 1) % count) for i in range(count)]
    left = [(i, (i - 1) % count) for i in range(count)]
    far = count // 2

    def pick(one, distance):
        return lax.dynamic_index_in_dim(one, lax.rem(me + distance + count, count), 0, False)

    ahead = [pick(one, far) for one in sets]
    behind = [pick(one, 1 - far) for one in sets]
    for distance in range(far - 1, -1, -1):
        for i, one in enumerate(sets):
            ahead[i] = lax.ppermute(ahead[i], "pass", right)
            if distance:
                ahead[i] = add_low(ahead[i], pick(one, distance))
            if distance < far - 1:
                behind[i] = lax.ppermute(behind[i], "pass", left)
                if distance:
                    behind[i] = add_low(behind[i], pick(one, -distance))
    return [
        (a.astype(F32) + b.astype(F32) + pick(one, 0).astype(F32)).astype(BF16)
        for a, b, one in zip(ahead, behind, sets)
    ]


def finish_kernel(heads, x_ref, out_ref):
    owners, cores, _, _ = x_ref.shape
    for core in range(cores):
        total = x_ref[0, core].astype(F32)
        for owner in range(1, owners):
            total = total + x_ref[owner, core].astype(F32)
        for head in range(heads):
            lanes = slice((core * heads + head) * HD, (core * heads + head + 1) * HD)
            for part in range(2):
                first = (head * 2 + part) * HD
                out_ref[:, part, lanes] = total[:, first : first + HD]


def finish_weights(parts):
    owners, cores, rows, width = parts.shape
    return pl.pallas_call(
        functools.partial(finish_kernel, width // (2 * HD)),
        out_shape=jax.ShapeDtypeStruct((rows, 2, cores * width // 2), F32),
        in_specs=[whole()],
        out_specs=whole(),
        compiler_params=params(),
        cost_estimate=cost(10**6, 2**20),
        name="finish_weights",
    )(parts)


def local(
    question_q,
    question_grad,
    question_kv,
    passage_kv,
    question_hidden,
    passage_hidden,
    reuse,
    passage_blocks,
):
    me = lax.axis_index("dp")
    me_array = me.reshape(1)
    peers = lax.axis_size("dp")
    groups = lax.axis_size("pass")
    cores = lax.axis_size("tensor")
    slots, slot_len, _, channels = passage_kv.shape
    samples, rows, width = question_q.shape
    heads = channels // HD
    group = width // channels
    refs = reuse.reshape(reuse.shape[0], reuse.shape[2])
    model_width = passage_hidden.shape[2]

    def exchange(x):
        return lax.all_to_all(x, "dp", split_axis=0, concat_axis=0, tiled=True)

    def from_partner(x):
        return lax.ppermute(x, "tensor", [(i, cores - 1 - i) for i in range(cores)])

    packed = pack_queries(refs, me_array, question_q, question_grad, slots)
    got = exchange(packed)

    hit = quotient(refs, slots) == me
    slot_of = jnp.sum(jnp.where(hit, lax.rem(refs, jnp.int32(slots)), 0), axis=1)
    order = jnp.arange(refs.shape[1], dtype=jnp.int32)
    entry_of = jnp.sum(jnp.where(hit, order[None, :], 0), axis=1)
    owners = quotient(lax.dynamic_index_in_dim(refs, me, 0, keepdims=False), slots)
    blocks = lax.dynamic_index_in_dim(passage_blocks, me, 0, keepdims=False).reshape(slots)
    keys, values = passage_kv[:, :, 0], passage_kv[:, :, 1]
    own_keys, own_values = question_kv[:, :, 0], question_kv[:, :, 1]
    own = own_stats(question_q, question_grad, own_keys, own_values, group)
    hidden_t = transpose_hidden(
        lax.axis_index("tensor").reshape(1),
        passage_hidden.reshape(-1, model_width),
        from_partner(passage_hidden).reshape(-1, model_width),
        question_hidden.reshape(-1, model_width),
        from_partner(question_hidden).reshape(-1, model_width),
        slots,
        samples,
        peers,
        groups,
    )
    got, hidden_t, own, keys, values = lax.optimization_barrier(
        (got, hidden_t, own, keys, values)
    )

    stats = exchange(owner_stats(slot_of, blocks, got, keys, values, own, group))
    grads_query, own_dq = own_grads(
        refs, me_array, question_q, question_grad, own_keys, own_values, stats, group, slots
    )
    grads_pass, dq_parts, terms = [], [], []
    for head in range(heads):
        one, dq = owner_grads(
            head, slot_of, blocks, refs, entry_of, got, stats, keys, values, group
        )
        grads_pass.append(one)
        dq_parts.append(dq)
        terms.append(weight_terms(hidden_t, one, grads_query[head], head))
    summed = jnp.concatenate(reduce_over_pass(terms), axis=-1)
    returned = exchange(jnp.concatenate(dq_parts, axis=-1))
    question_dq = sum_dq(owners, [returned], own_dq)

    share = summed.shape[0] // (peers * cores)
    parts = lax.all_to_all(
        summed.reshape(peers * cores, share, -1),
        ("dp", "tensor"),
        split_axis=0,
        concat_axis=0,
        tiled=True,
    )
    weight_grad = finish_weights(parts.reshape(peers, cores, share, -1))
    question_dkv = jnp.concatenate(
        [grads_query[head].reshape(samples, rows, 2, HD) for head in range(heads)], axis=-1
    )
    passage_dkv = jnp.concatenate(
        [one.reshape(slots, slot_len, 2, HD) for one in grads_pass], axis=-1
    )
    return (question_dq, question_dkv, passage_dkv, weight_grad)


def solution(mesh):
    in_specs = (
        P(("dp", "pass"), None, "tensor"),
        P(("dp", "pass"), None, "tensor"),
        P(("dp", "pass"), None, None, "tensor"),
        P(("dp", "pass"), None, None, "tensor"),
        P(("dp", "pass"), "tensor", None),
        P(("dp", "pass"), "tensor", None),
        P(None, "pass", None),
        P(None, "pass", None),
    )
    out_specs = (
        P(("dp", "pass"), None, "tensor"),
        P(("dp", "pass"), None, None, "tensor"),
        P(("dp", "pass"), None, None, "tensor"),
        P(("dp", "pass", "tensor"), None, None),
    )
    return jax.shard_map(local, mesh=mesh, in_specs=in_specs, out_specs=out_specs, check_vma=False)
```

```python
import functools
import math

import jax
import jax.numpy as jnp
from jax import lax
from jax.experimental import pallas as pl
from jax.experimental.pallas import tpu as pltpu
from jax.sharding import PartitionSpec as P

HD = 128
BLOCK = 128
NEG_FILL = -1e30
SCALE = HD ** (-0.5)
SCALE_LOG2 = SCALE * math.log2(math.e)
VMEM_LIMIT = 24 * 1024 * 1024
NT = (((1,), (1,)), ((), ()))
TN = (((0,), (0,)), ((), ()))
F32 = jnp.float32
BF16 = jnp.bfloat16


def params(limit=VMEM_LIMIT):
    return pltpu.CompilerParams(vmem_limit_bytes=limit)


def whole():
    return pl.BlockSpec(memory_space=pltpu.VMEM)


def smem():
    return pl.BlockSpec(memory_space=pltpu.SMEM)


def in_hbm():
    return pl.BlockSpec(memory_space=pltpu.HBM)


def cost(flops, nbytes, trans=0):
    return pl.CostEstimate(flops=flops, bytes_accessed=nbytes, transcendentals=trans)


def quotient(value, divisor):
    return lax.div(value, jnp.int32(divisor))


def head_rows(block, head, group):
    first = head * group
    return jnp.concatenate(
        [block[:, (first + r) * HD : (first + r + 1) * HD] for r in range(group)], axis=0
    )


def pack_kernel(slots, refs, q_ref, g_ref, out_ref, held, load_sems, sems):
    peers = out_ref.shape[0]
    samples, rows, _ = q_ref.shape
    per = peers // samples
    me = lax.axis_index("dp")
    loads = []
    for sample in range(samples):
        pair = []
        for part, src in enumerate((q_ref, g_ref)):
            pair.append(
                pltpu.make_async_copy(
                    src.at[sample],
                    held.at[sample, pl.ds(part * rows, rows)],
                    load_sems.at[sample, part],
                )
            )
            pair[-1].start()
        loads.append(pair)
    copies = []
    for j in range(peers):
        sample = j // per
        if j % per == 0:
            for copy in loads[sample]:
                copy.wait()
        dest = quotient(refs[me, j], slots)
        copy = pltpu.make_async_copy(held.at[sample], out_ref.at[dest], sems.at[j])
        copy.start()
        copies.append(copy)
    for copy in copies:
        copy.wait()


def pack_queries(refs, question_q, question_grad, slots):
    samples, rows, width = question_q.shape
    peers = refs.shape[0]
    return pl.pallas_call(
        functools.partial(pack_kernel, slots),
        out_shape=jax.ShapeDtypeStruct((peers, 2 * rows, width), BF16),
        in_specs=[smem(), in_hbm(), in_hbm()],
        out_specs=in_hbm(),
        scratch_shapes=[
            pltpu.VMEM((samples, 2 * rows, width), BF16),
            pltpu.SemaphoreType.DMA((samples, 2)),
            pltpu.SemaphoreType.DMA((peers,)),
        ],
        compiler_params=params(60 * 1024 * 1024),
        cost_estimate=cost(0, 6 * 2**20),
        name="pack_queries",
    )(refs, question_q, question_grad)


def scores_t(keys, queries, valid):
    scores = lax.dot_general(keys, queries, NT, preferred_element_type=F32) * SCALE_LOG2
    return jnp.where(valid, scores, NEG_FILL)


def part_stats(scores, prob_grad):
    top = jnp.max(scores, axis=0, keepdims=True)
    shifted = jnp.exp2(scores - top)
    total = jnp.sum(shifted, axis=0, keepdims=True)
    weighted = jnp.sum(shifted * prob_grad, axis=0, keepdims=True)
    return top + jnp.log2(total), weighted / total


def passage_valid(blocks, slot, slot_len, columns):
    shape = (slot_len, columns)
    return lax.broadcasted_iota(jnp.int32, shape, 0) < blocks[slot] * BLOCK


def owner_stats_kernel(group, slot_of, blocks, got_ref, k_ref, v_ref, out_ref):
    step = pl.program_id(0)
    per, both, _ = got_ref.shape
    rows = both // 2
    slot_len = k_ref.shape[1]
    heads = k_ref.shape[2] // HD
    columns = group * rows
    for one in range(per):
        slot = slot_of[step * per + one]
        valid = passage_valid(blocks, slot, slot_len, columns)
        logs, deltas = [], []
        for head in range(heads):
            lanes = slice(head * HD, (head + 1) * HD)
            queries = head_rows(got_ref[one, :rows], head, group)
            grads = head_rows(got_ref[one, rows:], head, group)
            scores = scores_t(k_ref[slot, :, lanes], queries, valid)
            prob_grad = lax.dot_general(
                v_ref[slot, :, lanes], grads, NT, preferred_element_type=F32
            )
            log, delta = part_stats(scores, prob_grad)
            logs.append(log)
            deltas.append(delta)
        out_ref[one] = jnp.concatenate(logs + deltas, axis=0)


def owner_stats(slot_of, blocks, got, keys, values, group):
    peers, both, width = got.shape
    heads = keys.shape[2] // HD
    columns = group * both // 2
    per = 4
    return pl.pallas_call(
        functools.partial(owner_stats_kernel, group),
        out_shape=jax.ShapeDtypeStruct((peers, 2 * heads, columns), F32),
        grid_spec=pltpu.PrefetchScalarGridSpec(
            num_scalar_prefetch=2,
            grid=(peers // per,),
            in_specs=[
                pl.BlockSpec((per, both, width), lambda r, s, b: (r, 0, 0)),
                whole(),
                whole(),
            ],
            out_specs=pl.BlockSpec((per, 2 * heads, columns), lambda r, s, b: (r, 0, 0)),
        ),
        compiler_params=params(),
        cost_estimate=cost(2 * 10**9, 6 * 2**20, 2 * 10**6),
        name="owner_stats",
    )(slot_of, blocks, got, keys, values)


def own_valid(own_rows, rows, group):
    shape = (own_rows, group * rows)
    key_row = lax.broadcasted_iota(jnp.int32, shape, 0)
    query_row = lax.rem(lax.broadcasted_iota(jnp.int32, shape, 1), jnp.int32(rows))
    return key_row <= query_row


def own_stats_kernel(group, q_ref, g_ref, k_ref, v_ref, out_ref):
    samples, rows, _ = q_ref.shape
    heads = k_ref.shape[2] // HD
    valid = own_valid(rows, rows, group)
    for sample in range(samples):
        logs, deltas = [], []
        for head in range(heads):
            lanes = slice(head * HD, (head + 1) * HD)
            queries = head_rows(q_ref[sample], head, group)
            grads = head_rows(g_ref[sample], head, group)
            scores = scores_t(k_ref[sample, :, lanes], queries, valid)
            prob_grad = lax.dot_general(
                v_ref[sample, :, lanes], grads, NT, preferred_element_type=F32
            )
            log, delta = part_stats(scores, prob_grad)
            logs.append(log)
            deltas.append(delta)
        out_ref[sample] = jnp.concatenate(logs + deltas, axis=0)


def own_stats(question_q, question_grad, keys, values, group):
    samples, rows, _ = question_q.shape
    heads = keys.shape[2] // HD
    return pl.pallas_call(
        functools.partial(own_stats_kernel, group),
        out_shape=jax.ShapeDtypeStruct((samples, 2 * heads, group * rows), F32),
        in_specs=[whole()] * 4,
        out_specs=whole(),
        compiler_params=params(),
        cost_estimate=cost(10**8, 2**20, 10**5),
        name="own_stats",
    )(question_q, question_grad, keys, values)


def merge_kernel(slots, refs, st_ref, own_ref, back_ref, merged_ref):
    samples, stat_rows, _ = own_ref.shape
    heads = stat_rows // 2
    per = st_ref.shape[0] // samples
    me = lax.axis_index("dp")
    for sample in range(samples):
        owners = [quotient(refs[me, sample * per + k], slots) for k in range(per)]
        parts = [own_ref[sample]] + [st_ref[owner] for owner in owners]
        logs = [part[:heads] for part in parts]
        top = functools.reduce(jnp.maximum, logs)
        weights = [jnp.exp2(log - top) for log in logs]
        total = sum(weights)
        delta = sum(weight * part[heads:] for weight, part in zip(weights, parts)) / total
        joint = jnp.concatenate([top + jnp.log2(total), delta], axis=0)
        merged_ref[sample] = joint
        for owner in owners:
            back_ref[owner] = joint


def merge(refs, stats, own, slots):
    return pl.pallas_call(
        functools.partial(merge_kernel, slots),
        out_shape=(
            jax.ShapeDtypeStruct(stats.shape, F32),
            jax.ShapeDtypeStruct(own.shape, F32),
        ),
        in_specs=[smem(), whole(), whole()],
        out_specs=(whole(), whole()),
        compiler_params=params(),
        cost_estimate=cost(10**5, 2**17, 10**4),
        name="merge_stats",
    )(refs, stats, own)


def probs_and_dscore(scores, prob_grad, joint, delta):
    probs = jnp.exp2(scores - joint)
    dscore = (probs * (prob_grad - delta) * SCALE).astype(BF16)
    return probs.astype(BF16), dscore


def owner_grads_kernel(group, head, slot_of, blocks, got_ref, joint_ref, k_ref, v_ref, *rest):
    grad_ref, dq_ref, acc_ref = rest[-3:]
    step = pl.program_id(0)
    per, both, _ = got_ref.shape
    rows = both // 2
    slot_len = k_ref.shape[1]
    heads = k_ref.shape[2] // HD
    lanes = slice(head * HD, (head + 1) * HD)

    @pl.when(step == 0)
    def _():
        acc_ref[...] = jnp.zeros_like(acc_ref)

    for one in range(per):
        slot = slot_of[step * per + one]
        valid = passage_valid(blocks, slot, slot_len, group * rows)
        queries = head_rows(got_ref[one, :rows], 0, group)
        grads = head_rows(got_ref[one, rows:], 0, group)
        keys = k_ref[slot, :, lanes]
        scores = scores_t(keys, queries, valid)
        prob_grad = lax.dot_general(v_ref[slot, :, lanes], grads, NT, preferred_element_type=F32)
        joint = joint_ref[one, head : head + 1]
        delta = joint_ref[one, heads + head : heads + head + 1]
        probs, dscore = probs_and_dscore(scores, prob_grad, joint, delta)
        acc_ref[slot, :, :HD] += jnp.dot(dscore, queries, preferred_element_type=F32)
        acc_ref[slot, :, HD:] += jnp.dot(probs, grads, preferred_element_type=F32)
        dq = lax.dot_general(dscore, keys, TN, preferred_element_type=F32).astype(BF16)
        for r in range(group):
            dq_ref[one, :, r * HD : (r + 1) * HD] = dq[r * rows : (r + 1) * rows]

    @pl.when(step == pl.num_programs(0) - 1)
    def _():
        for one in range(acc_ref.shape[0]):
            grad_ref[one * slot_len : (one + 1) * slot_len] = acc_ref[one].astype(BF16)


def owner_grads(head, slot_of, blocks, got, joint, keys, values, dq, group):
    peers, both, width = got.shape
    slots, slot_len, _ = keys.shape
    stat_rows, columns = joint.shape[1:]
    per = 4
    lanes = group * HD
    operands = [slot_of, blocks, got, joint, keys, values]
    in_specs = [
        pl.BlockSpec((per, both, lanes), lambda r, *_: (r, 0, head)),
        pl.BlockSpec((per, stat_rows, columns), lambda r, *_: (r, 0, 0)),
        whole(),
        whole(),
    ]
    aliases = {}
    if dq is not None:
        aliases = {len(operands): 1}
        operands.append(dq)
        in_specs.append(in_hbm())
    return pl.pallas_call(
        functools.partial(owner_grads_kernel, group, head),
        out_shape=(
            jax.ShapeDtypeStruct((slots * slot_len, 2 * HD), BF16),
            jax.ShapeDtypeStruct((peers, both // 2, width), BF16),
        ),
        grid_spec=pltpu.PrefetchScalarGridSpec(
            num_scalar_prefetch=2,
            grid=(peers // per,),
            in_specs=in_specs,
            out_specs=(
                pl.BlockSpec((slots * slot_len, 2 * HD), lambda r, *_: (0, 0)),
                pl.BlockSpec((per, both // 2, lanes), lambda r, *_: (r, 0, head)),
            ),
            scratch_shapes=[pltpu.VMEM((slots, slot_len, 2 * HD), F32)],
        ),
        input_output_aliases=aliases,
        compiler_params=params(),
        cost_estimate=cost(5 * 10**9, 8 * 2**20, 2 * 10**6),
        name=f"owner_grads_{head}",
    )(*operands)


def own_grads_kernel(group, q_ref, g_ref, k_ref, v_ref, joint_ref, grad_ref, dq_ref):
    samples, rows, _ = q_ref.shape
    heads = k_ref.shape[2] // HD
    valid = own_valid(rows, rows, group)
    for sample in range(samples):
        token = slice(sample * rows, (sample + 1) * rows)
        for head in range(heads):
            lanes = slice(head * HD, (head + 1) * HD)
            joint = joint_ref[sample, head : head + 1]
            delta = joint_ref[sample, heads + head : heads + head + 1]
            queries = head_rows(q_ref[sample], head, group)
            grads = head_rows(g_ref[sample], head, group)
            keys = k_ref[sample, :, lanes]
            scores = scores_t(keys, queries, valid)
            prob_grad = lax.dot_general(
                v_ref[sample, :, lanes], grads, NT, preferred_element_type=F32
            )
            probs, dscore = probs_and_dscore(scores, prob_grad, joint, delta)
            key_grad = jnp.dot(dscore, queries, preferred_element_type=F32)
            value_grad = jnp.dot(probs, grads, preferred_element_type=F32)
            grad_ref[head, token, :HD] = key_grad.astype(BF16)
            grad_ref[head, token, HD:] = value_grad.astype(BF16)
            dq = lax.dot_general(dscore, keys, TN, preferred_element_type=F32)
            for r in range(group):
                column = (head * group + r) * HD
                dq_ref[sample, :, column : column + HD] = dq[r * rows : (r + 1) * rows]


def own_grads(question_q, question_grad, keys, values, joint, group):
    samples, rows, width = question_q.shape
    heads = keys.shape[2] // HD
    return pl.pallas_call(
        functools.partial(own_grads_kernel, group),
        out_shape=(
            jax.ShapeDtypeStruct((heads, samples * rows, 2 * HD), BF16),
            jax.ShapeDtypeStruct((samples, rows, width), F32),
        ),
        in_specs=[whole()] * 5,
        out_specs=(whole(), whole()),
        compiler_params=params(),
        cost_estimate=cost(3 * 10**8, 3 * 2**20, 10**5),
        name="own_grads",
    )(question_q, question_grad, keys, values, joint)


def sum_dq_kernel(heads, owners, *refs):
    out_ref = refs[-1]
    own_ref = refs[-2]
    per = (len(refs) - 2) // heads
    width = refs[0].shape[2]
    for head in range(heads):
        lanes = slice(head * width, (head + 1) * width)
        total = own_ref[0, :, lanes]
        for ref in refs[head * per : (head + 1) * per]:
            total = total + ref[0].astype(F32)
        out_ref[0, :, lanes] = total.astype(BF16)


def sum_dq(owners, returned, own):
    samples, rows, width = own.shape
    per = owners.shape[0] // samples
    heads = len(returned)

    def from_owner(k):
        return pl.BlockSpec((1, rows, width // heads), lambda s, o: (o[s * per + k], 0, 0))

    return pl.pallas_call(
        functools.partial(sum_dq_kernel, heads),
        out_shape=jax.ShapeDtypeStruct((samples, rows, width), BF16),
        grid_spec=pltpu.PrefetchScalarGridSpec(
            num_scalar_prefetch=1,
            grid=(samples,),
            in_specs=[from_owner(k) for k in range(per)] * heads
            + [pl.BlockSpec((1, rows, width), lambda s, o: (s, 0, 0))],
            out_specs=pl.BlockSpec((1, rows, width), lambda s, o: (s, 0, 0)),
        ),
        compiler_params=params(),
        cost_estimate=cost(2 * 10**6, 4 * 2**20),
        name="sum_dq",
    )(owners, *[one for one in returned for _ in range(per)], own)


def transpose_kernel(slots, samples, owners, core, mine_p, other_p, mine_q, other_q, out_ref):
    groups, share, _ = out_ref.shape
    lower = core[0] == 0
    first_p = jnp.where(lower, mine_p[...], other_p[...])
    second_p = jnp.where(lower, other_p[...], mine_p[...])
    first_q = jnp.where(lower, mine_q[...], other_q[...])
    second_q = jnp.where(lower, other_q[...], mine_q[...])
    half = first_p.shape[0] // slots
    part = first_q.shape[0] // samples
    pieces = []
    for slot in range(slots):
        pieces.append(first_p[slot * half : (slot + 1) * half])
        pieces.append(second_p[slot * half : (slot + 1) * half])
    for sample in range(samples):
        pieces.append(first_q[sample * part : (sample + 1) * part])
        pieces.append(second_q[sample * part : (sample + 1) * part])
    turned = jnp.concatenate(pieces, axis=0).T
    rows = share // owners
    for owner in range(owners):
        for group in range(groups):
            first = (owner * groups + group) * rows
            out_ref[group, owner * rows : (owner + 1) * rows] = turned[first : first + rows]


def transpose_hidden(core, mine_p, other_p, mine_q, other_q, slots, samples, owners, groups):
    width = mine_p.shape[1]
    tokens = 2 * (mine_p.shape[0] + mine_q.shape[0])
    per = 2
    tile = per * width // owners
    return pl.pallas_call(
        functools.partial(transpose_kernel, slots, samples, per),
        out_shape=jax.ShapeDtypeStruct((groups, width // groups, tokens), BF16),
        grid_spec=pltpu.PrefetchScalarGridSpec(
            num_scalar_prefetch=1,
            grid=(width // tile,),
            in_specs=[
                pl.BlockSpec((one.shape[0], tile), lambda i, c: (0, i))
                for one in (mine_p, other_p, mine_q, other_q)
            ],
            out_specs=pl.BlockSpec((groups, tile // groups, tokens), lambda i, c: (0, i, 0)),
        ),
        compiler_params=params(),
        cost_estimate=cost(0, 12 * 2**20),
        name="transpose_hidden",
    )(core, mine_p, other_p, mine_q, other_q)


def weight_block(h_ref, place, p_ref, q_ref, sums):
    count, _, _ = h_ref.shape
    split = p_ref.shape[0]
    group = lax.rem(lax.axis_index("pass") + (place + count), count)
    total = jnp.dot(h_ref[group, :, :split], p_ref[...], preferred_element_type=F32)
    total = total + jnp.dot(h_ref[group, :, split:], q_ref[...], preferred_element_type=F32)
    for one in sums:
        total = total + one[...].astype(F32)
    return total.astype(BF16)


def weight_kernel(places, arrived, h_ref, p_ref, q_ref, *refs):
    sums, outs = list(refs[: -len(places)]), refs[-len(places) :]
    for place, extra, out_ref in zip(places, arrived, outs):
        out_ref[...] = weight_block(h_ref, place, p_ref, q_ref, [sums.pop(0) for _ in range(extra)])


def weight_blocks(hidden_t, grads_pass, grads_query, places, arrived, name):
    _, share, tokens = hidden_t.shape
    width = grads_pass.shape[1]
    count = len(places)
    extras = [one for block in arrived for one in block]
    return pl.pallas_call(
        functools.partial(weight_kernel, places, tuple(len(block) for block in arrived)),
        out_shape=tuple(jax.ShapeDtypeStruct((share, width), BF16) for _ in range(count)),
        in_specs=[whole()] * (3 + len(extras)),
        out_specs=tuple(whole() for _ in range(count)),
        compiler_params=params(),
        cost_estimate=cost(2 * count * share * tokens * width, 2 * count * share * 2 * width),
        name=name,
    )(hidden_t, grads_pass, grads_query, *extras)


def last_kernel(h_ref, *refs):
    out_ref = refs[-1]
    per = 4
    for head in range((len(refs) - 1) // per):
        p_ref, q_ref, ahead, behind = refs[head * per : (head + 1) * per]
        width = p_ref.shape[1]
        out_ref[:, head * width : (head + 1) * width] = weight_block(
            h_ref, 0, p_ref, q_ref, [ahead, behind]
        )


def last_blocks(hidden_t, chains):
    _, share, tokens = hidden_t.shape
    width = sum(chain[0].shape[1] for chain in chains)
    operands = [one for chain in chains for one in chain]
    return pl.pallas_call(
        last_kernel,
        out_shape=jax.ShapeDtypeStruct((share, width), BF16),
        in_specs=[whole()] * (1 + len(operands)),
        out_specs=whole(),
        compiler_params=params(),
        cost_estimate=cost(2 * share * tokens * width, 2 * share * 3 * width),
        name="weights_last",
    )(hidden_t, *operands)


def ring(head):
    count = lax.axis_size("pass")
    sign = 1 if head % 2 == 0 else -1
    ahead_to = [(i, (i + sign) % count) for i in range(count)]
    behind_to = [(i, (i - sign) % count) for i in range(count)]
    return sign, ahead_to, behind_to


def farthest(hidden_t, grads_pass, grads_query, head):
    sign, ahead_to, _ = ring(head)
    far = lax.axis_size("pass") // 2
    (block,) = weight_blocks(
        hidden_t, grads_pass, grads_query, (sign * far,), ([],), f"weights_{head}_{far}"
    )
    return block, lax.ppermute(block, "pass", ahead_to)


def sums_over_pass(hidden_t, grads_pass, grads_query, ahead, head):
    sign, ahead_to, behind_to = ring(head)
    behind = []
    for distance in range(lax.axis_size("pass") // 2 - 1, 0, -1):
        sums = weight_blocks(
            hidden_t,
            grads_pass,
            grads_query,
            (sign * distance, -sign * distance),
            ([ahead], behind),
            f"weights_{head}_{distance}",
        )
        ahead = lax.ppermute(sums[0], "pass", ahead_to)
        behind = [lax.ppermute(sums[1], "pass", behind_to)]
    return ahead, behind[0]


def finish_kernel(heads, x_ref, out_ref):
    owners, cores, _, _ = x_ref.shape
    for core in range(cores):
        total = x_ref[0, core].astype(F32)
        for owner in range(1, owners):
            total = total + x_ref[owner, core].astype(F32)
        for head in range(heads):
            lanes = slice((core * heads + head) * HD, (core * heads + head + 1) * HD)
            for part in range(2):
                first = (head * 2 + part) * HD
                out_ref[:, part, lanes] = total[:, first : first + HD]


def finish_weights(parts):
    owners, cores, rows, width = parts.shape
    return pl.pallas_call(
        functools.partial(finish_kernel, width // (2 * HD)),
        out_shape=jax.ShapeDtypeStruct((rows, 2, cores * width // 2), F32),
        in_specs=[whole()],
        out_specs=whole(),
        compiler_params=params(),
        cost_estimate=cost(10**6, 2**20),
        name="finish_weights",
    )(parts)


def local(
    question_q,
    question_grad,
    question_kv,
    passage_kv,
    question_hidden,
    passage_hidden,
    reuse,
    passage_blocks,
):
    me = lax.axis_index("dp")
    peers = lax.axis_size("dp")
    groups = lax.axis_size("pass")
    cores = lax.axis_size("tensor")
    slots, slot_len, _, channels = passage_kv.shape
    samples, rows, width = question_q.shape
    heads = channels // HD
    group = width // channels
    refs = reuse.reshape(reuse.shape[0], reuse.shape[2])
    model_width = passage_hidden.shape[2]

    def exchange(x):
        return lax.all_to_all(x, "dp", split_axis=0, concat_axis=0, tiled=True)

    def from_partner(x):
        return lax.ppermute(x, "tensor", [(i, cores - 1 - i) for i in range(cores)])

    packed = pack_queries(refs, question_q, question_grad, slots)
    got = exchange(packed)

    hit = quotient(refs, slots) == me
    slot_of = jnp.sum(jnp.where(hit, lax.rem(refs, jnp.int32(slots)), 0), axis=1)
    owners = quotient(lax.dynamic_index_in_dim(refs, me, 0, keepdims=False), slots)
    blocks = lax.dynamic_index_in_dim(passage_blocks, me, 0, keepdims=False).reshape(slots)
    keys, values = passage_kv[:, :, 0], passage_kv[:, :, 1]
    own_keys, own_values = question_kv[:, :, 0], question_kv[:, :, 1]
    own = own_stats(question_q, question_grad, own_keys, own_values, group)
    hidden_t = transpose_hidden(
        lax.axis_index("tensor").reshape(1),
        passage_hidden.reshape(-1, model_width),
        from_partner(passage_hidden).reshape(-1, model_width),
        question_hidden.reshape(-1, model_width),
        from_partner(question_hidden).reshape(-1, model_width),
        slots,
        samples,
        peers,
        groups,
    )
    got, hidden_t, own = lax.optimization_barrier((got, hidden_t, own))

    stats = exchange(owner_stats(slot_of, blocks, got, keys, values, group))
    back, merged = merge(refs, stats, own, slots)
    joint = exchange(back)
    grads_query, own_dq = own_grads(
        question_q, question_grad, own_keys, own_values, merged, group
    )
    joint, grads_query, own_dq = lax.optimization_barrier((joint, grads_query, own_dq))
    grads_pass, first = [], []
    dq_parts = None
    for head in range(heads):
        one, dq_parts = owner_grads(
            head, slot_of, blocks, got, joint, keys, values, dq_parts, group
        )
        grads_pass.append(one)
        block, ahead = farthest(hidden_t, one, grads_query[head], head)
        first.append(ahead)
        dq_parts, _ = lax.optimization_barrier((dq_parts, block))
    returned = exchange(dq_parts)
    chains = []
    for head in range(heads):
        ends = sums_over_pass(
            hidden_t, grads_pass[head], grads_query[head], first[head], head
        )
        chains.append((grads_pass[head], grads_query[head], *ends))
    summed = last_blocks(hidden_t, chains)
    summed, returned = lax.optimization_barrier((summed, returned))
    question_dq = sum_dq(owners, [returned], own_dq)

    share = summed.shape[0] // (peers * cores)
    parts = lax.all_to_all(
        summed.reshape(peers * cores, share, -1),
        ("dp", "tensor"),
        split_axis=0,
        concat_axis=0,
        tiled=True,
    )
    weight_grad = finish_weights(parts.reshape(peers, cores, share, -1))
    question_dkv = jnp.concatenate(
        [grads_query[head].reshape(samples, rows, 2, HD) for head in range(heads)], axis=-1
    )
    passage_dkv = jnp.concatenate(
        [one.reshape(slots, slot_len, 2, HD) for one in grads_pass], axis=-1
    )
    return (question_dq, question_dkv, passage_dkv, weight_grad)


def solution(mesh):
    in_specs = (
        P(("dp", "pass"), None, "tensor"),
        P(("dp", "pass"), None, "tensor"),
        P(("dp", "pass"), None, None, "tensor"),
        P(("dp", "pass"), None, None, "tensor"),
        P(("dp", "pass"), "tensor", None),
        P(("dp", "pass"), "tensor", None),
        P(None, "pass", None),
        P(None, "pass", None),
    )
    out_specs = (
        P(("dp", "pass"), None, "tensor"),
        P(("dp", "pass"), None, None, "tensor"),
        P(("dp", "pass"), None, None, "tensor"),
        P(("dp", "pass", "tensor"), None, None),
    )
    return jax.shard_map(local, mesh=mesh, in_specs=in_specs, out_specs=out_specs, check_vma=False)
```

```python
import functools
import math

import jax
import jax.numpy as jnp
from jax import lax
from jax.experimental import pallas as pl
from jax.experimental.pallas import tpu as pltpu
from jax.sharding import PartitionSpec as P

HD = 128
BLOCK = 128
NEG_FILL = -1e30
SCALE = HD ** (-0.5)
SCALE_LOG2 = SCALE * math.log2(math.e)
VMEM_LIMIT = 24 * 1024 * 1024
VMEM_MOST = 60 * 1024 * 1024
NT = (((1,), (1,)), ((), ()))
TN = (((0,), (0,)), ((), ()))
F32 = jnp.float32
BF16 = jnp.bfloat16


def params(limit=VMEM_LIMIT):
    return pltpu.CompilerParams(vmem_limit_bytes=limit)


def whole():
    return pl.BlockSpec(memory_space=pltpu.VMEM)


def smem():
    return pl.BlockSpec(memory_space=pltpu.SMEM)


def in_hbm():
    return pl.BlockSpec(memory_space=pltpu.HBM)


def cost(flops, nbytes, trans=0):
    return pl.CostEstimate(flops=flops, bytes_accessed=nbytes, transcendentals=trans)


def quotient(value, divisor):
    return lax.div(value, jnp.int32(divisor))


def head_rows(block, head, group):
    first = head * group
    return jnp.concatenate(
        [block[:, (first + r) * HD : (first + r + 1) * HD] for r in range(group)], axis=0
    )


def pack_kernel(slots, refs, q_ref, g_ref, out_ref, held, load_sems, sems):
    peers = out_ref.shape[0]
    samples, rows, _ = q_ref.shape
    per = peers // samples
    me = lax.axis_index("dp")
    loads = []
    for sample in range(samples):
        pair = []
        for part, src in enumerate((q_ref, g_ref)):
            pair.append(
                pltpu.make_async_copy(
                    src.at[sample],
                    held.at[sample, pl.ds(part * rows, rows)],
                    load_sems.at[sample, part],
                )
            )
            pair[-1].start()
        loads.append(pair)
    copies = []
    for j in range(peers):
        sample = j // per
        if j % per == 0:
            for copy in loads[sample]:
                copy.wait()
        dest = quotient(refs[me, j], slots)
        copy = pltpu.make_async_copy(held.at[sample], out_ref.at[dest], sems.at[j])
        copy.start()
        copies.append(copy)
    for copy in copies:
        copy.wait()


def pack_queries(refs, question_q, question_grad, slots):
    samples, rows, width = question_q.shape
    peers = refs.shape[0]
    return pl.pallas_call(
        functools.partial(pack_kernel, slots),
        out_shape=jax.ShapeDtypeStruct((peers, 2 * rows, width), BF16),
        in_specs=[smem(), in_hbm(), in_hbm()],
        out_specs=in_hbm(),
        scratch_shapes=[
            pltpu.VMEM((samples, 2 * rows, width), BF16),
            pltpu.SemaphoreType.DMA((samples, 2)),
            pltpu.SemaphoreType.DMA((peers,)),
        ],
        compiler_params=params(VMEM_MOST),
        cost_estimate=cost(0, 6 * 2**20),
        name="pack_queries",
    )(refs, question_q, question_grad)


def scores_t(keys, queries, valid):
    scores = lax.dot_general(keys, queries, NT, preferred_element_type=F32) * SCALE_LOG2
    return jnp.where(valid, scores, NEG_FILL)


def part_stats(scores, prob_grad):
    top = jnp.max(scores, axis=0, keepdims=True)
    shifted = jnp.exp2(scores - top)
    total = jnp.sum(shifted, axis=0, keepdims=True)
    weighted = jnp.sum(shifted * prob_grad, axis=0, keepdims=True)
    return top + jnp.log2(total), weighted / total


def passage_valid(blocks, slot_len, columns):
    shape = (slot_len, columns)
    return lax.broadcasted_iota(jnp.int32, shape, 0) < blocks * BLOCK


def owner_stats_kernel(group, table, got_ref, kv_ref, out_ref):
    step = pl.program_id(0)
    per, both, _ = got_ref.shape
    peers = per * pl.num_programs(0)
    rows = both // 2
    slot_len = kv_ref.shape[2]
    heads = kv_ref.shape[3] // HD
    columns = group * rows
    for one in range(per):
        slot = table[step * per + one]
        valid = passage_valid(table[peers + slot], slot_len, columns)
        logs, deltas = [], []
        for head in range(heads):
            lanes = slice(head * HD, (head + 1) * HD)
            queries = head_rows(got_ref[one, :rows], head, group)
            grads = head_rows(got_ref[one, rows:], head, group)
            scores = scores_t(kv_ref[0, slot, :, lanes], queries, valid)
            prob_grad = lax.dot_general(
                kv_ref[1, slot, :, lanes], grads, NT, preferred_element_type=F32
            )
            log, delta = part_stats(scores, prob_grad)
            logs.append(log)
            deltas.append(delta)
        out_ref[one] = jnp.concatenate(logs + deltas, axis=0)


def owner_stats(table, got, kv, group):
    peers, both, width = got.shape
    heads = kv.shape[3] // HD
    columns = group * both // 2
    per = 4
    return pl.pallas_call(
        functools.partial(owner_stats_kernel, group),
        out_shape=jax.ShapeDtypeStruct((peers, 2 * heads, columns), F32),
        grid_spec=pltpu.PrefetchScalarGridSpec(
            num_scalar_prefetch=1,
            grid=(peers // per,),
            in_specs=[pl.BlockSpec((per, both, width), lambda r, t: (r, 0, 0)), whole()],
            out_specs=pl.BlockSpec((per, 2 * heads, columns), lambda r, t: (r, 0, 0)),
        ),
        compiler_params=params(VMEM_MOST),
        cost_estimate=cost(2 * 10**9, 6 * 2**20, 2 * 10**6),
        name="owner_stats",
    )(table, got, kv)


def own_valid(own_rows, rows, group):
    shape = (own_rows, group * rows)
    key_row = lax.broadcasted_iota(jnp.int32, shape, 0)
    query_row = lax.rem(lax.broadcasted_iota(jnp.int32, shape, 1), jnp.int32(rows))
    return key_row <= query_row


def own_stats_kernel(group, q_ref, g_ref, k_ref, v_ref, out_ref):
    samples, rows, _ = q_ref.shape
    heads = k_ref.shape[2] // HD
    valid = own_valid(rows, rows, group)
    for sample in range(samples):
        logs, deltas = [], []
        for head in range(heads):
            lanes = slice(head * HD, (head + 1) * HD)
            queries = head_rows(q_ref[sample], head, group)
            grads = head_rows(g_ref[sample], head, group)
            scores = scores_t(k_ref[sample, :, lanes], queries, valid)
            prob_grad = lax.dot_general(
                v_ref[sample, :, lanes], grads, NT, preferred_element_type=F32
            )
            log, delta = part_stats(scores, prob_grad)
            logs.append(log)
            deltas.append(delta)
        out_ref[sample] = jnp.concatenate(logs + deltas, axis=0)


def own_stats(question_q, question_grad, keys, values, group):
    samples, rows, _ = question_q.shape
    heads = keys.shape[2] // HD
    return pl.pallas_call(
        functools.partial(own_stats_kernel, group),
        out_shape=jax.ShapeDtypeStruct((samples, 2 * heads, group * rows), F32),
        in_specs=[whole()] * 4,
        out_specs=whole(),
        compiler_params=params(),
        cost_estimate=cost(10**8, 2**20, 10**5),
        name="own_stats",
    )(question_q, question_grad, keys, values)


def merge_kernel(slots, refs, st_ref, own_ref, back_ref, merged_ref):
    samples, stat_rows, _ = own_ref.shape
    heads = stat_rows // 2
    per = st_ref.shape[0] // samples
    me = lax.axis_index("dp")
    for sample in range(samples):
        owners = [quotient(refs[me, sample * per + k], slots) for k in range(per)]
        parts = [own_ref[sample]] + [st_ref[owner] for owner in owners]
        logs = [part[:heads] for part in parts]
        top = functools.reduce(jnp.maximum, logs)
        weights = [jnp.exp2(log - top) for log in logs]
        total = sum(weights)
        delta = sum(weight * part[heads:] for weight, part in zip(weights, parts)) / total
        joint = jnp.concatenate([top + jnp.log2(total), delta], axis=0)
        merged_ref[sample] = joint
        for owner in owners:
            back_ref[owner] = joint


def merge(refs, stats, own, slots):
    return pl.pallas_call(
        functools.partial(merge_kernel, slots),
        out_shape=(
            jax.ShapeDtypeStruct(stats.shape, F32),
            jax.ShapeDtypeStruct(own.shape, F32),
        ),
        in_specs=[smem(), whole(), whole()],
        out_specs=(whole(), whole()),
        compiler_params=params(),
        cost_estimate=cost(10**5, 2**17, 10**4),
        name="merge_stats",
    )(refs, stats, own)


def probs_and_dscore(scores, prob_grad, joint, delta):
    probs = jnp.exp2(scores - joint)
    dscore = (probs * (prob_grad - delta) * SCALE).astype(BF16)
    return probs.astype(BF16), dscore


def owner_grads_kernel(
    group, head, places, table, got_ref, joint_ref, kv_ref, own_ref, hidden_ref, *rest
):
    grad_ref, dq_ref, *block_refs, acc_ref, h_ref, h_sem = rest[-5 - len(places) :]
    load = pltpu.make_async_copy(hidden_ref, h_ref, h_sem)
    step = pl.program_id(0)
    per, both, _ = got_ref.shape
    peers = per * pl.num_programs(0)
    rows = both // 2
    slot_len = kv_ref.shape[2]
    heads = kv_ref.shape[3] // HD
    lanes = slice(head * HD, (head + 1) * HD)

    @pl.when(step == 0)
    def _():
        load.start()
        acc_ref[...] = jnp.zeros_like(acc_ref)

    for one in range(per):
        slot = table[step * per + one]
        valid = passage_valid(table[peers + slot], slot_len, group * rows)
        queries = head_rows(got_ref[one, :rows], 0, group)
        grads = head_rows(got_ref[one, rows:], 0, group)
        keys = kv_ref[0, slot, :, lanes]
        scores = scores_t(keys, queries, valid)
        prob_grad = lax.dot_general(
            kv_ref[1, slot, :, lanes], grads, NT, preferred_element_type=F32
        )
        joint = joint_ref[one, head : head + 1]
        delta = joint_ref[one, heads + head : heads + head + 1]
        probs, dscore = probs_and_dscore(scores, prob_grad, joint, delta)
        acc_ref[slot, :, :HD] += jnp.dot(dscore, queries, preferred_element_type=F32)
        acc_ref[slot, :, HD:] += jnp.dot(probs, grads, preferred_element_type=F32)
        dq = lax.dot_general(dscore, keys, TN, preferred_element_type=F32).astype(BF16)
        for r in range(group):
            dq_ref[one, :, r * HD : (r + 1) * HD] = dq[r * rows : (r + 1) * rows]

    @pl.when(step == pl.num_programs(0) - 1)
    def _():
        for one in range(acc_ref.shape[0]):
            grad_ref[one * slot_len : (one + 1) * slot_len] = acc_ref[one].astype(BF16)
        load.wait()
        for place, block_ref in zip(places, block_refs):
            block_ref[...] = weight_block(h_ref, place, grad_ref, own_ref, head)


def owner_grads(head, places, table, got, joint, kv, hidden_t, grads_query, dq, group):
    peers, both, width = got.shape
    _, slots, slot_len, _ = kv.shape
    stat_rows, columns = joint.shape[1:]
    share = hidden_t.shape[1]
    per = 4
    lanes = group * HD
    operands = [table, got, joint, kv, grads_query, hidden_t]
    in_specs = [
        pl.BlockSpec((per, both, lanes), lambda r, t: (r, 0, head)),
        pl.BlockSpec((per, stat_rows, columns), lambda r, t: (r, 0, 0)),
        whole(),
        whole(),
        in_hbm(),
    ]
    aliases = {}
    if dq is not None:
        aliases = {len(operands): 1}
        operands.append(dq)
        in_specs.append(in_hbm())
    return pl.pallas_call(
        functools.partial(owner_grads_kernel, group, head, places),
        out_shape=(
            jax.ShapeDtypeStruct((slots * slot_len, 2 * HD), BF16),
            jax.ShapeDtypeStruct((peers, both // 2, width), BF16),
            *[jax.ShapeDtypeStruct((share, 2 * HD), BF16) for _ in places],
        ),
        grid_spec=pltpu.PrefetchScalarGridSpec(
            num_scalar_prefetch=1,
            grid=(peers // per,),
            in_specs=in_specs,
            out_specs=(
                pl.BlockSpec((slots * slot_len, 2 * HD), lambda r, t: (0, 0)),
                pl.BlockSpec((per, both // 2, lanes), lambda r, t: (r, 0, head)),
                *[pl.BlockSpec((share, 2 * HD), lambda r, t: (0, 0)) for _ in places],
            ),
            scratch_shapes=[
                pltpu.VMEM((slots, slot_len, 2 * HD), F32),
                pltpu.VMEM(hidden_t.shape, BF16),
                pltpu.SemaphoreType.DMA,
            ],
        ),
        input_output_aliases=aliases,
        compiler_params=params(VMEM_MOST),
        cost_estimate=cost(5 * 10**9, 8 * 2**20, 2 * 10**6),
        name=f"owner_grads_{head}",
    )(*operands)


def own_grads_kernel(group, q_ref, g_ref, k_ref, v_ref, joint_ref, grad_ref, dq_ref):
    samples, rows, _ = q_ref.shape
    heads = k_ref.shape[2] // HD
    valid = own_valid(rows, rows, group)
    for sample in range(samples):
        token = slice(sample * rows, (sample + 1) * rows)
        for head in range(heads):
            lanes = slice(head * HD, (head + 1) * HD)
            joint = joint_ref[sample, head : head + 1]
            delta = joint_ref[sample, heads + head : heads + head + 1]
            queries = head_rows(q_ref[sample], head, group)
            grads = head_rows(g_ref[sample], head, group)
            keys = k_ref[sample, :, lanes]
            scores = scores_t(keys, queries, valid)
            prob_grad = lax.dot_general(
                v_ref[sample, :, lanes], grads, NT, preferred_element_type=F32
            )
            probs, dscore = probs_and_dscore(scores, prob_grad, joint, delta)
            key_grad = jnp.dot(dscore, queries, preferred_element_type=F32)
            value_grad = jnp.dot(probs, grads, preferred_element_type=F32)
            grad_ref[head, token, :HD] = key_grad.astype(BF16)
            grad_ref[head, token, HD:] = value_grad.astype(BF16)
            dq = lax.dot_general(dscore, keys, TN, preferred_element_type=F32)
            for r in range(group):
                column = (head * group + r) * HD
                dq_ref[sample, :, column : column + HD] = dq[r * rows : (r + 1) * rows]


def own_grads(question_q, question_grad, keys, values, joint, group):
    samples, rows, width = question_q.shape
    heads = keys.shape[2] // HD
    return pl.pallas_call(
        functools.partial(own_grads_kernel, group),
        out_shape=(
            jax.ShapeDtypeStruct((heads, samples * rows, 2 * HD), BF16),
            jax.ShapeDtypeStruct((samples, rows, width), F32),
        ),
        in_specs=[whole()] * 5,
        out_specs=(whole(), whole()),
        compiler_params=params(),
        cost_estimate=cost(3 * 10**8, 3 * 2**20, 10**5),
        name="own_grads",
    )(question_q, question_grad, keys, values, joint)


def sum_dq_kernel(heads, owners, *refs):
    out_ref = refs[-1]
    own_ref = refs[-2]
    per = (len(refs) - 2) // heads
    width = refs[0].shape[2]
    for head in range(heads):
        lanes = slice(head * width, (head + 1) * width)
        total = own_ref[0, :, lanes]
        for ref in refs[head * per : (head + 1) * per]:
            total = total + ref[0].astype(F32)
        out_ref[0, :, lanes] = total.astype(BF16)


def sum_dq(owners, returned, own):
    samples, rows, width = own.shape
    per = owners.shape[0] // samples
    heads = len(returned)

    def from_owner(k):
        return pl.BlockSpec((1, rows, width // heads), lambda s, o: (o[s * per + k], 0, 0))

    return pl.pallas_call(
        functools.partial(sum_dq_kernel, heads),
        out_shape=jax.ShapeDtypeStruct((samples, rows, width), BF16),
        grid_spec=pltpu.PrefetchScalarGridSpec(
            num_scalar_prefetch=1,
            grid=(samples,),
            in_specs=[from_owner(k) for k in range(per)] * heads
            + [pl.BlockSpec((1, rows, width), lambda s, o: (s, 0, 0))],
            out_specs=pl.BlockSpec((1, rows, width), lambda s, o: (s, 0, 0)),
        ),
        compiler_params=params(),
        cost_estimate=cost(2 * 10**6, 4 * 2**20),
        name="sum_dq",
    )(owners, *[one for one in returned for _ in range(per)], own)


def transpose_kernel(slots, samples, owners, core, mine_p, other_p, mine_q, other_q, out_ref):
    groups, share, _ = out_ref.shape
    lower = core[0] == 0
    first_p = jnp.where(lower, mine_p[...], other_p[...])
    second_p = jnp.where(lower, other_p[...], mine_p[...])
    first_q = jnp.where(lower, mine_q[...], other_q[...])
    second_q = jnp.where(lower, other_q[...], mine_q[...])
    half = first_p.shape[0] // slots
    part = first_q.shape[0] // samples
    pieces = []
    for slot in range(slots):
        pieces.append(first_p[slot * half : (slot + 1) * half])
        pieces.append(second_p[slot * half : (slot + 1) * half])
    for sample in range(samples):
        pieces.append(first_q[sample * part : (sample + 1) * part])
        pieces.append(second_q[sample * part : (sample + 1) * part])
    turned = jnp.concatenate(pieces, axis=0).T
    rows = share // owners
    for owner in range(owners):
        for group in range(groups):
            first = (owner * groups + group) * rows
            out_ref[group, owner * rows : (owner + 1) * rows] = turned[first : first + rows]


def transpose_hidden(core, mine_p, other_p, mine_q, other_q, slots, samples, owners, groups):
    width = mine_p.shape[1]
    tokens = 2 * (mine_p.shape[0] + mine_q.shape[0])
    per = 2
    tile = per * width // owners
    return pl.pallas_call(
        functools.partial(transpose_kernel, slots, samples, per),
        out_shape=jax.ShapeDtypeStruct((groups, width // groups, tokens), BF16),
        grid_spec=pltpu.PrefetchScalarGridSpec(
            num_scalar_prefetch=1,
            grid=(width // tile,),
            in_specs=[
                pl.BlockSpec((one.shape[0], tile), lambda i, c: (0, i))
                for one in (mine_p, other_p, mine_q, other_q)
            ],
            out_specs=pl.BlockSpec((groups, tile // groups, tokens), lambda i, c: (0, i, 0)),
        ),
        compiler_params=params(VMEM_MOST),
        cost_estimate=cost(0, 12 * 2**20),
        name="transpose_hidden",
    )(core, mine_p, other_p, mine_q, other_q)


def weight_block(h_ref, place, p_ref, q_ref, head):
    count, _, _ = h_ref.shape
    split = p_ref.shape[0]
    group = lax.rem(lax.axis_index("pass") + (place + count), count)
    total = jnp.dot(h_ref[group, :, :split], p_ref[...], preferred_element_type=F32)
    total = total + jnp.dot(h_ref[group, :, split:], q_ref[head], preferred_element_type=F32)
    return total.astype(BF16)


def add_kernel(*refs):
    outs = refs[2 * (len(refs) // 3) + 1 :]
    for k, out_ref in enumerate(outs):
        total = refs[2 * k][...].astype(F32) + refs[2 * k + 1][...].astype(F32)
        out_ref[...] = total.astype(BF16)


def add_arrived(blocks, arrived, after, name):
    return pl.pallas_call(
        add_kernel,
        out_shape=tuple(jax.ShapeDtypeStruct(one.shape, BF16) for one in blocks),
        in_specs=[whole()] * (2 * len(blocks)) + [pl.BlockSpec(memory_space=pl.ANY)],
        out_specs=tuple(whole() for _ in blocks),
        compiler_params=params(),
        cost_estimate=cost(8 * 10**9, 2**20),
        name=name,
    )(*[one for pair in zip(blocks, arrived) for one in pair], after)


def last_kernel(*refs):
    out_ref = refs[-1]
    per = 3
    for head in range((len(refs) - 1) // per):
        total = sum(ref[...].astype(F32) for ref in refs[head * per : (head + 1) * per])
        width = total.shape[1]
        out_ref[:, head * width : (head + 1) * width] = total.astype(BF16)


def last_sums(chains):
    share, width = chains[0][0].shape
    return pl.pallas_call(
        last_kernel,
        out_shape=jax.ShapeDtypeStruct((share, len(chains) * width), BF16),
        in_specs=[whole()] * (3 * len(chains)),
        out_specs=whole(),
        compiler_params=params(),
        cost_estimate=cost(10**6, 2**21),
        name="weights_last",
    )(*[one for chain in chains for one in chain])


def travel(blocks, head):
    count = lax.axis_size("pass")
    ways = [direction(head), -direction(head)]
    return [
        lax.ppermute(block, "pass", [(i, (i + way) % count) for i in range(count)])
        for block, way in zip(blocks, ways)
    ]


def direction(head):
    return 1 if head % 2 == 0 else -1


def finish_kernel(heads, x_ref, out_ref):
    owners, cores, _, _ = x_ref.shape
    for core in range(cores):
        total = x_ref[0, core].astype(F32)
        for owner in range(1, owners):
            total = total + x_ref[owner, core].astype(F32)
        for head in range(heads):
            lanes = slice((core * heads + head) * HD, (core * heads + head + 1) * HD)
            for part in range(2):
                first = (head * 2 + part) * HD
                out_ref[:, part, lanes] = total[:, first : first + HD]


def finish_weights(parts):
    owners, cores, rows, width = parts.shape
    return pl.pallas_call(
        functools.partial(finish_kernel, width // (2 * HD)),
        out_shape=jax.ShapeDtypeStruct((rows, 2, cores * width // 2), F32),
        in_specs=[whole()],
        out_specs=whole(),
        compiler_params=params(),
        cost_estimate=cost(10**6, 2**20),
        name="finish_weights",
    )(parts)


def local(
    question_q,
    question_grad,
    question_kv,
    passage_kv,
    question_hidden,
    passage_hidden,
    reuse,
    passage_blocks,
):
    me = lax.axis_index("dp")
    peers = lax.axis_size("dp")
    groups = lax.axis_size("pass")
    cores = lax.axis_size("tensor")
    slots, slot_len, _, channels = passage_kv.shape
    samples, rows, width = question_q.shape
    heads = channels // HD
    group = width // channels
    refs = reuse.reshape(reuse.shape[0], reuse.shape[2])
    model_width = passage_hidden.shape[2]

    def exchange(x):
        return lax.all_to_all(x, "dp", split_axis=0, concat_axis=0, tiled=True)

    def from_partner(x):
        return lax.ppermute(x, "tensor", [(i, cores - 1 - i) for i in range(cores)])

    packed = pack_queries(refs, question_q, question_grad, slots)
    got = exchange(packed)

    hit = quotient(refs, slots) == me
    slot_of = jnp.sum(jnp.where(hit, lax.rem(refs, jnp.int32(slots)), 0), axis=1)
    owners = quotient(lax.dynamic_index_in_dim(refs, me, 0, keepdims=False), slots)
    blocks = lax.dynamic_index_in_dim(passage_blocks, me, 0, keepdims=False).reshape(slots)
    table = jnp.concatenate([slot_of, blocks])
    kv = jnp.transpose(passage_kv, (2, 0, 1, 3))
    own_keys, own_values = question_kv[:, :, 0], question_kv[:, :, 1]
    own = own_stats(question_q, question_grad, own_keys, own_values, group)
    hidden_t = transpose_hidden(
        lax.axis_index("tensor").reshape(1),
        passage_hidden.reshape(-1, model_width),
        from_partner(passage_hidden).reshape(-1, model_width),
        question_hidden.reshape(-1, model_width),
        from_partner(question_hidden).reshape(-1, model_width),
        slots,
        samples,
        peers,
        groups,
    )
    got, hidden_t, own = lax.optimization_barrier((got, hidden_t, own))

    stats = exchange(owner_stats(table, got, kv, group))
    back, merged = merge(refs, stats, own, slots)
    joint = exchange(back)
    grads_query, own_dq = own_grads(
        question_q, question_grad, own_keys, own_values, merged, group
    )
    joint, grads_query, own_dq = lax.optimization_barrier((joint, grads_query, own_dq))
    far = groups // 2
    distances = list(range(far, 0, -1))
    grads_pass, blocks_of, sums = [], [], []
    dq_parts = None
    for head in range(heads):
        way = direction(head)
        places = [way * one for one in distances] + [-way * one for one in distances[1:]] + [0]
        one, dq_parts, *weights = owner_grads(
            head, tuple(places), table, got, joint, kv, hidden_t, grads_query, dq_parts, group
        )
        grads_pass.append(one)
        blocks_of.append(dict(zip([place * way for place in places], weights)))
        sums.append(travel([blocks_of[head][far], blocks_of[head][1 - far]], head))
    ends = [None] * heads
    after = grads_pass[-1]
    for distance in distances[1:]:
        for head in range(heads):
            places = [distance, 1 - distance]
            if distance == 1:
                places = places[:1]
                ends[head] = sums[head][1]
            added = add_arrived(
                [blocks_of[head][place] for place in places],
                sums[head][: len(places)],
                after,
                f"add_{head}_{distance}",
            )
            after = added[0]
            sums[head] = travel(added, head)
        if distance == far - 1:
            dq_parts, after = lax.optimization_barrier((dq_parts, after))
    returned = exchange(dq_parts)
    summed = last_sums([(blocks_of[h][0], sums[h][0], ends[h]) for h in range(heads)])
    summed, returned = lax.optimization_barrier((summed, returned))
    question_dq = sum_dq(owners, [returned], own_dq)

    share = summed.shape[0] // (peers * cores)
    parts = lax.all_to_all(
        summed.reshape(peers * cores, share, -1),
        ("dp", "tensor"),
        split_axis=0,
        concat_axis=0,
        tiled=True,
    )
    weight_grad = finish_weights(parts.reshape(peers, cores, share, -1))
    question_dkv = jnp.concatenate(
        [grads_query[head].reshape(samples, rows, 2, HD) for head in range(heads)], axis=-1
    )
    passage_dkv = jnp.concatenate(
        [one.reshape(slots, slot_len, 2, HD) for one in grads_pass], axis=-1
    )
    return (question_dq, question_dkv, passage_dkv, weight_grad)


def solution(mesh):
    in_specs = (
        P(("dp", "pass"), None, "tensor"),
        P(("dp", "pass"), None, "tensor"),
        P(("dp", "pass"), None, None, "tensor"),
        P(("dp", "pass"), None, None, "tensor"),
        P(("dp", "pass"), "tensor", None),
        P(("dp", "pass"), "tensor", None),
        P(None, "pass", None),
        P(None, "pass", None),
    )
    out_specs = (
        P(("dp", "pass"), None, "tensor"),
        P(("dp", "pass"), None, None, "tensor"),
        P(("dp", "pass"), None, None, "tensor"),
        P(("dp", "pass", "tensor"), None, None),
    )
    return jax.shard_map(local, mesh=mesh, in_specs=in_specs, out_specs=out_specs, check_vma=False)
```

```python
import functools
import math

import jax
import jax.numpy as jnp
from jax import lax
from jax.experimental import pallas as pl
from jax.experimental.pallas import tpu as pltpu
from jax.sharding import PartitionSpec as P

HD = 128
BLOCK = 128
NEG_FILL = -1e30
SCALE = HD ** (-0.5)
SCALE_LOG2 = SCALE * math.log2(math.e)
VMEM_LIMIT = 24 * 1024 * 1024
VMEM_MOST = 60 * 1024 * 1024
NT = (((1,), (1,)), ((), ()))
TN = (((0,), (0,)), ((), ()))
F32 = jnp.float32
BF16 = jnp.bfloat16


def params(limit=VMEM_LIMIT):
    return pltpu.CompilerParams(vmem_limit_bytes=limit)


def whole():
    return pl.BlockSpec(memory_space=pltpu.VMEM)


def smem():
    return pl.BlockSpec(memory_space=pltpu.SMEM)


def in_hbm():
    return pl.BlockSpec(memory_space=pltpu.HBM)


def cost(flops, nbytes, trans=0):
    return pl.CostEstimate(flops=flops, bytes_accessed=nbytes, transcendentals=trans)


def quotient(value, divisor):
    return lax.div(value, jnp.int32(divisor))


def head_rows(block, head, group):
    first = head * group
    return jnp.concatenate(
        [block[:, (first + r) * HD : (first + r + 1) * HD] for r in range(group)], axis=0
    )


def pack_kernel(slots, refs, q_ref, g_ref, out_ref, held, load_sems, sems):
    peers = out_ref.shape[0]
    samples, rows, _ = q_ref.shape
    per = peers // samples
    me = lax.axis_index("dp")
    loads = []
    for sample in range(samples):
        pair = []
        for part, src in enumerate((q_ref, g_ref)):
            pair.append(
                pltpu.make_async_copy(
                    src.at[sample],
                    held.at[sample, pl.ds(part * rows, rows)],
                    load_sems.at[sample, part],
                )
            )
            pair[-1].start()
        loads.append(pair)
    copies = []
    for j in range(peers):
        sample = j // per
        if j % per == 0:
            for copy in loads[sample]:
                copy.wait()
        dest = quotient(refs[me, j], slots)
        copy = pltpu.make_async_copy(held.at[sample], out_ref.at[dest], sems.at[j])
        copy.start()
        copies.append(copy)
    for copy in copies:
        copy.wait()


def pack_queries(refs, question_q, question_grad, slots):
    samples, rows, width = question_q.shape
    peers = refs.shape[0]
    return pl.pallas_call(
        functools.partial(pack_kernel, slots),
        out_shape=jax.ShapeDtypeStruct((peers, 2 * rows, width), BF16),
        in_specs=[smem(), in_hbm(), in_hbm()],
        out_specs=in_hbm(),
        scratch_shapes=[
            pltpu.VMEM((samples, 2 * rows, width), BF16),
            pltpu.SemaphoreType.DMA((samples, 2)),
            pltpu.SemaphoreType.DMA((peers,)),
        ],
        compiler_params=params(VMEM_MOST),
        cost_estimate=cost(0, 6 * 2**20),
        name="pack_queries",
    )(refs, question_q, question_grad)


def scores_t(keys, queries, valid):
    scores = lax.dot_general(keys, queries, NT, preferred_element_type=F32) * SCALE_LOG2
    return jnp.where(valid, scores, NEG_FILL)


def part_stats(scores, prob_grad):
    top = jnp.max(scores, axis=0, keepdims=True)
    shifted = jnp.exp2(scores - top)
    total = jnp.sum(shifted, axis=0, keepdims=True)
    weighted = jnp.sum(shifted * prob_grad, axis=0, keepdims=True)
    return top + jnp.log2(total), weighted / total


def passage_valid(blocks, slot_len, columns):
    shape = (slot_len, columns)
    return lax.broadcasted_iota(jnp.int32, shape, 0) < blocks * BLOCK


def load_groups(src, held, sems):
    count = sems.shape[0]
    per = src.shape[0] // count
    return [
        pltpu.make_async_copy(
            src.at[pl.ds(i * per, per)], held.at[pl.ds(i * per, per)], sems.at[i]
        )
        for i in range(count)
    ]


def wait_group(i, src, held, sems):
    per = src.shape[0] // sems.shape[0]
    rows = pl.ds(i * per, per)
    pltpu.make_async_copy(src.at[rows], held.at[rows], sems.at[i]).wait()


def owner_stats_kernel(group, table, got_hbm, kv_ref, out_ref, got_ref, sems):
    peers, both, _ = got_ref.shape
    steps = sems.shape[0]
    per = peers // steps
    rows = both // 2
    slot_len = kv_ref.shape[2]
    heads = kv_ref.shape[3] // HD
    columns = group * rows
    for load in load_groups(got_hbm, got_ref, sems):
        load.start()

    @pl.loop(0, steps)
    def _(step):
        wait_group(step, got_hbm, got_ref, sems)
        for one in range(per):
            reader = step * per + one
            slot = table[reader]
            valid = passage_valid(table[peers + slot], slot_len, columns)
            logs, deltas = [], []
            for head in range(heads):
                lanes = slice(head * HD, (head + 1) * HD)
                queries = head_rows(got_ref[reader, :rows], head, group)
                grads = head_rows(got_ref[reader, rows:], head, group)
                scores = scores_t(kv_ref[0, slot, :, lanes], queries, valid)
                prob_grad = lax.dot_general(
                    kv_ref[1, slot, :, lanes], grads, NT, preferred_element_type=F32
                )
                log, delta = part_stats(scores, prob_grad)
                logs.append(log)
                deltas.append(delta)
            out_ref[reader] = jnp.concatenate(logs + deltas, axis=0)


def owner_stats(table, got, kv, group):
    peers, both, width = got.shape
    heads = kv.shape[3] // HD
    columns = group * both // 2
    return pl.pallas_call(
        functools.partial(owner_stats_kernel, group),
        out_shape=jax.ShapeDtypeStruct((peers, 2 * heads, columns), F32),
        in_specs=[smem(), in_hbm(), whole()],
        out_specs=whole(),
        scratch_shapes=[pltpu.VMEM(got.shape, BF16), pltpu.SemaphoreType.DMA((4,))],
        compiler_params=params(VMEM_MOST),
        cost_estimate=cost(2 * 10**9, 6 * 2**20, 2 * 10**6),
        name="owner_stats",
    )(table, got, kv)


def own_valid(own_rows, rows, group):
    shape = (own_rows, group * rows)
    key_row = lax.broadcasted_iota(jnp.int32, shape, 0)
    query_row = lax.rem(lax.broadcasted_iota(jnp.int32, shape, 1), jnp.int32(rows))
    return key_row <= query_row


def own_stats_kernel(group, q_ref, g_ref, k_ref, v_ref, out_ref):
    samples, rows, _ = q_ref.shape
    heads = k_ref.shape[2] // HD
    valid = own_valid(rows, rows, group)
    for sample in range(samples):
        logs, deltas = [], []
        for head in range(heads):
            lanes = slice(head * HD, (head + 1) * HD)
            queries = head_rows(q_ref[sample], head, group)
            grads = head_rows(g_ref[sample], head, group)
            scores = scores_t(k_ref[sample, :, lanes], queries, valid)
            prob_grad = lax.dot_general(
                v_ref[sample, :, lanes], grads, NT, preferred_element_type=F32
            )
            log, delta = part_stats(scores, prob_grad)
            logs.append(log)
            deltas.append(delta)
        out_ref[sample] = jnp.concatenate(logs + deltas, axis=0)


def own_stats(question_q, question_grad, keys, values, group):
    samples, rows, _ = question_q.shape
    heads = keys.shape[2] // HD
    return pl.pallas_call(
        functools.partial(own_stats_kernel, group),
        out_shape=jax.ShapeDtypeStruct((samples, 2 * heads, group * rows), F32),
        in_specs=[whole()] * 4,
        out_specs=whole(),
        compiler_params=params(),
        cost_estimate=cost(10**8, 2**20, 10**5),
        name="own_stats",
    )(question_q, question_grad, keys, values)


def merge_kernel(slots, refs, st_ref, own_ref, back_ref, merged_ref):
    samples, stat_rows, _ = own_ref.shape
    heads = stat_rows // 2
    per = st_ref.shape[0] // samples
    me = lax.axis_index("dp")
    for sample in range(samples):
        owners = [quotient(refs[me, sample * per + k], slots) for k in range(per)]
        parts = [own_ref[sample]] + [st_ref[owner] for owner in owners]
        logs = [part[:heads] for part in parts]
        top = functools.reduce(jnp.maximum, logs)
        weights = [jnp.exp2(log - top) for log in logs]
        total = sum(weights)
        delta = sum(weight * part[heads:] for weight, part in zip(weights, parts)) / total
        joint = jnp.concatenate([top + jnp.log2(total), delta], axis=0)
        merged_ref[sample] = joint
        for owner in owners:
            back_ref[owner] = joint


def merge(refs, stats, own, slots):
    return pl.pallas_call(
        functools.partial(merge_kernel, slots),
        out_shape=(
            jax.ShapeDtypeStruct(stats.shape, F32),
            jax.ShapeDtypeStruct(own.shape, F32),
        ),
        in_specs=[smem(), whole(), whole()],
        out_specs=(whole(), whole()),
        compiler_params=params(),
        cost_estimate=cost(10**5, 2**17, 10**4),
        name="merge_stats",
    )(refs, stats, own)


def probs_and_dscore(scores, prob_grad, joint, delta):
    probs = jnp.exp2(scores - joint)
    dscore = (probs * (prob_grad - delta) * SCALE).astype(BF16)
    return probs.astype(BF16), dscore


def owner_grads_kernel(
    group,
    places,
    table,
    got_hbm,
    joint_ref,
    kv_ref,
    turned_ref,
    own_ref,
    hidden_ref,
    grad_out,
    dq_out,
    *rest,
):
    outs = rest[:-11]
    acc_ref, got_ref, h_ref, grad_ref, dq_ref, block_ref = rest[-11:-5]
    got_sems, h_sem, grad_sem, dq_sems, sems = rest[-5:]
    peers, both, _ = got_ref.shape
    steps = got_sems.shape[0]
    per = peers // steps
    rows = both // 2
    slot_len = kv_ref.shape[2]
    heads = kv_ref.shape[3] // HD
    for load in load_groups(got_hbm, got_ref, got_sems):
        load.start()
    hidden_load = pltpu.make_async_copy(hidden_ref, h_ref, h_sem)
    hidden_load.start()
    acc_ref[...] = jnp.zeros_like(acc_ref)

    @pl.loop(0, steps)
    def _(step):
        wait_group(step, got_hbm, got_ref, got_sems)
        for one in range(per):
            reader = step * per + one
            slot = table[reader]
            valid = passage_valid(table[peers + slot], slot_len, group * rows)
            for head in range(heads):
                lanes = slice(head * HD, (head + 1) * HD)
                key_lanes = slice(2 * head * HD, (2 * head + 1) * HD)
                value_lanes = slice((2 * head + 1) * HD, (2 * head + 2) * HD)
                queries = head_rows(got_ref[reader, :rows], head, group)
                grads = head_rows(got_ref[reader, rows:], head, group)
                scores = scores_t(kv_ref[0, slot, :, lanes], queries, valid)
                prob_grad = lax.dot_general(
                    kv_ref[1, slot, :, lanes], grads, NT, preferred_element_type=F32
                )
                joint = joint_ref[reader, head : head + 1]
                delta = joint_ref[reader, heads + head : heads + head + 1]
                probs, dscore = probs_and_dscore(scores, prob_grad, joint, delta)
                acc_ref[slot, :, key_lanes] += jnp.dot(
                    dscore, queries, preferred_element_type=F32
                )
                acc_ref[slot, :, value_lanes] += jnp.dot(
                    probs, grads, preferred_element_type=F32
                )
                dq = jnp.dot(turned_ref[slot, lanes], dscore, preferred_element_type=F32)
                dq = dq.astype(BF16).T
                for r in range(group):
                    column = (head * group + r) * HD
                    dq_ref[reader, :, column : column + HD] = dq[r * rows : (r + 1) * rows]
        part = pl.ds(step * per, per)
        pltpu.make_async_copy(dq_ref.at[part], dq_out.at[part], dq_sems.at[step]).start()

    for one in range(acc_ref.shape[0]):
        grad_ref[one * slot_len : (one + 1) * slot_len] = acc_ref[one].astype(BF16)
    copies = [pltpu.make_async_copy(grad_ref, grad_out, grad_sem)]
    copies[0].start()
    hidden_load.wait()
    count = h_ref.shape[0]
    tokens = grad_ref.shape[0]
    k = 0
    for place, uses in places:
        pass_group = lax.rem(lax.axis_index("pass") + (place + count), count)
        total = jnp.dot(h_ref[pass_group, :, :tokens], grad_ref[...], preferred_element_type=F32)
        total = total + jnp.dot(
            h_ref[pass_group, :, tokens:], own_ref[...], preferred_element_type=F32
        )
        for head, out, row in uses:
            lanes = slice(2 * head * HD, 2 * (head + 1) * HD)
            block_ref[k] = total[:, lanes].astype(BF16)
            copies.append(
                pltpu.make_async_copy(block_ref.at[k], outs[out].at[row], sems.at[k])
            )
            copies[-1].start()
            k += 1
    for copy in copies:
        copy.wait()
    for step in range(steps):
        wait_group(step, dq_ref, dq_out, dq_sems)


def owner_grads(places, depths, table, got, joint, kv, turned, hidden_t, grads_query):
    peers, both, width = got.shape
    _, slots, slot_len, channels = kv.shape
    columns = joint.shape[2]
    share = hidden_t.shape[1]
    count = sum(depths)
    grads = jax.ShapeDtypeStruct((slots * slot_len, 2 * channels), BF16)
    dq = jax.ShapeDtypeStruct((peers, both // 2, width), BF16)
    return pl.pallas_call(
        functools.partial(owner_grads_kernel, 2 * columns // both, places),
        out_shape=(
            grads,
            dq,
            *[jax.ShapeDtypeStruct((depth, share, 2 * HD), BF16) for depth in depths],
        ),
        in_specs=[smem(), in_hbm(), whole(), whole(), whole(), whole(), in_hbm()],
        out_specs=tuple(in_hbm() for _ in range(2 + len(depths))),
        scratch_shapes=[
            pltpu.VMEM((slots, slot_len, 2 * channels), F32),
            pltpu.VMEM(got.shape, BF16),
            pltpu.VMEM(hidden_t.shape, BF16),
            pltpu.VMEM(grads.shape, BF16),
            pltpu.VMEM(dq.shape, BF16),
            pltpu.VMEM((count, share, 2 * HD), BF16),
            pltpu.SemaphoreType.DMA((4,)),
            pltpu.SemaphoreType.DMA,
            pltpu.SemaphoreType.DMA,
            pltpu.SemaphoreType.DMA((4,)),
            pltpu.SemaphoreType.DMA((count,)),
        ],
        compiler_params=params(VMEM_MOST),
        cost_estimate=cost(16 * 10**9, 24 * 2**20, 2 * 10**6),
        name="owner_grads",
    )(table, got, joint, kv, turned, grads_query, hidden_t)


def own_grads_kernel(group, q_ref, g_ref, k_ref, v_ref, joint_ref, grad_ref, dq_ref):
    samples, rows, _ = q_ref.shape
    heads = k_ref.shape[2] // HD
    valid = own_valid(rows, rows, group)
    for sample in range(samples):
        token = slice(sample * rows, (sample + 1) * rows)
        for head in range(heads):
            lanes = slice(head * HD, (head + 1) * HD)
            joint = joint_ref[sample, head : head + 1]
            delta = joint_ref[sample, heads + head : heads + head + 1]
            queries = head_rows(q_ref[sample], head, group)
            grads = head_rows(g_ref[sample], head, group)
            keys = k_ref[sample, :, lanes]
            scores = scores_t(keys, queries, valid)
            prob_grad = lax.dot_general(
                v_ref[sample, :, lanes], grads, NT, preferred_element_type=F32
            )
            probs, dscore = probs_and_dscore(scores, prob_grad, joint, delta)
            key_grad = jnp.dot(dscore, queries, preferred_element_type=F32)
            value_grad = jnp.dot(probs, grads, preferred_element_type=F32)
            key_lanes = slice(2 * head * HD, (2 * head + 1) * HD)
            value_lanes = slice((2 * head + 1) * HD, (2 * head + 2) * HD)
            grad_ref[token, key_lanes] = key_grad.astype(BF16)
            grad_ref[token, value_lanes] = value_grad.astype(BF16)
            dq = lax.dot_general(dscore, keys, TN, preferred_element_type=F32).astype(BF16)
            for r in range(group):
                column = (head * group + r) * HD
                dq_ref[sample, :, column : column + HD] = dq[r * rows : (r + 1) * rows]


def own_grads(question_q, question_grad, keys, values, joint, group):
    samples, rows, width = question_q.shape
    heads = keys.shape[2] // HD
    return pl.pallas_call(
        functools.partial(own_grads_kernel, group),
        out_shape=(
            jax.ShapeDtypeStruct((samples * rows, 2 * heads * HD), BF16),
            jax.ShapeDtypeStruct((samples, rows, width), BF16),
        ),
        in_specs=[whole()] * 5,
        out_specs=(whole(), whole()),
        compiler_params=params(),
        cost_estimate=cost(3 * 10**8, 3 * 2**20, 10**5),
        name="own_grads",
    )(question_q, question_grad, keys, values, joint)


def sum_dq_kernel(heads, owners, *refs):
    out_ref = refs[-1]
    own_ref = refs[-2]
    per = (len(refs) - 2) // heads
    width = refs[0].shape[2]
    for head in range(heads):
        lanes = slice(head * width, (head + 1) * width)
        total = own_ref[0, :, lanes].astype(F32)
        for ref in refs[head * per : (head + 1) * per]:
            total = total + ref[0].astype(F32)
        out_ref[0, :, lanes] = total.astype(BF16)


def sum_dq(owners, returned, own):
    samples, rows, width = own.shape
    per = owners.shape[0] // samples
    heads = len(returned)

    def from_owner(k):
        return pl.BlockSpec((1, rows, width // heads), lambda s, o: (o[s * per + k], 0, 0))

    return pl.pallas_call(
        functools.partial(sum_dq_kernel, heads),
        out_shape=jax.ShapeDtypeStruct((samples, rows, width), BF16),
        grid_spec=pltpu.PrefetchScalarGridSpec(
            num_scalar_prefetch=1,
            grid=(samples,),
            in_specs=[from_owner(k) for k in range(per)] * heads
            + [pl.BlockSpec((1, rows, width), lambda s, o: (s, 0, 0))],
            out_specs=pl.BlockSpec((1, rows, width), lambda s, o: (s, 0, 0)),
        ),
        compiler_params=params(),
        cost_estimate=cost(2 * 10**6, 4 * 2**20),
        name="sum_dq",
    )(owners, *[one for one in returned for _ in range(per)], own)


def transpose_kernel(slots, samples, owners, core, mine_p, other_p, mine_q, other_q, out_ref):
    groups, share, _ = out_ref.shape
    lower = core[0] == 0
    first_p = jnp.where(lower, mine_p[...], other_p[...])
    second_p = jnp.where(lower, other_p[...], mine_p[...])
    first_q = jnp.where(lower, mine_q[...], other_q[...])
    second_q = jnp.where(lower, other_q[...], mine_q[...])
    half = first_p.shape[0] // slots
    part = first_q.shape[0] // samples
    pieces = []
    for slot in range(slots):
        pieces.append(first_p[slot * half : (slot + 1) * half])
        pieces.append(second_p[slot * half : (slot + 1) * half])
    for sample in range(samples):
        pieces.append(first_q[sample * part : (sample + 1) * part])
        pieces.append(second_q[sample * part : (sample + 1) * part])
    turned = jnp.concatenate(pieces, axis=0).T
    rows = share // owners
    for owner in range(owners):
        for group in range(groups):
            first = (owner * groups + group) * rows
            out_ref[group, owner * rows : (owner + 1) * rows] = turned[first : first + rows]


def transpose_hidden(core, mine_p, other_p, mine_q, other_q, slots, samples, owners, groups):
    width = mine_p.shape[1]
    tokens = 2 * (mine_p.shape[0] + mine_q.shape[0])
    per = 2
    tile = per * width // owners
    return pl.pallas_call(
        functools.partial(transpose_kernel, slots, samples, per),
        out_shape=jax.ShapeDtypeStruct((groups, width // groups, tokens), BF16),
        grid_spec=pltpu.PrefetchScalarGridSpec(
            num_scalar_prefetch=1,
            grid=(width // tile,),
            in_specs=[
                pl.BlockSpec((one.shape[0], tile), lambda i, c: (0, i))
                for one in (mine_p, other_p, mine_q, other_q)
            ],
            out_specs=pl.BlockSpec((groups, tile // groups, tokens), lambda i, c: (0, i, 0)),
        ),
        compiler_params=params(VMEM_MOST),
        cost_estimate=cost(0, 12 * 2**20),
        name="transpose_hidden",
    )(core, mine_p, other_p, mine_q, other_q)


def add_kernel(count, blocks_ref, *refs):
    outs = refs[len(refs) - count :]
    for k, (arrived, out_ref) in enumerate(zip(refs, outs)):
        out_ref[...] = (blocks_ref[k].astype(F32) + arrived[...].astype(F32)).astype(BF16)


def add_arrived(blocks, arrived, after, name):
    count = len(arrived)
    return pl.pallas_call(
        functools.partial(add_kernel, count),
        out_shape=tuple(jax.ShapeDtypeStruct(one.shape, BF16) for one in arrived),
        in_specs=[whole()] * (1 + count) + [pl.BlockSpec(memory_space=pl.ANY)],
        out_specs=(whole(),) * count,
        compiler_params=params(),
        cost_estimate=cost(8 * 10**9, 2**20),
        name=name,
    )(blocks, *arrived, after)


def last_kernel(heads, blocks_ref, *refs):
    out_ref = refs[-1]
    for head in range(heads):
        total = blocks_ref[head].astype(F32)
        for ref in refs[2 * head : 2 * head + 2]:
            total = total + ref[...].astype(F32)
        width = total.shape[1]
        out_ref[:, head * width : (head + 1) * width] = total.astype(BF16)


def last_sums(blocks, arrived):
    heads, share, width = blocks.shape
    return pl.pallas_call(
        functools.partial(last_kernel, heads),
        out_shape=jax.ShapeDtypeStruct((share, heads * width), BF16),
        in_specs=[whole()] * (1 + 2 * heads),
        out_specs=whole(),
        compiler_params=params(),
        cost_estimate=cost(10**6, 2**21),
        name="weights_last",
    )(blocks, *arrived)


def travel(blocks, head):
    count = lax.axis_size("pass")
    ways = [direction(head), -direction(head)]
    return [
        lax.ppermute(block, "pass", [(i, (i + way) % count) for i in range(count)])
        for block, way in zip(blocks, ways)
    ]


def direction(head):
    return 1 if head % 2 == 0 else -1


def finish_kernel(heads, x_ref, out_ref):
    owners, cores, _, _ = x_ref.shape
    for core in range(cores):
        total = x_ref[0, core].astype(F32)
        for owner in range(1, owners):
            total = total + x_ref[owner, core].astype(F32)
        for head in range(heads):
            lanes = slice((core * heads + head) * HD, (core * heads + head + 1) * HD)
            for part in range(2):
                first = (head * 2 + part) * HD
                out_ref[:, part, lanes] = total[:, first : first + HD]


def finish_weights(parts):
    owners, cores, rows, width = parts.shape
    return pl.pallas_call(
        functools.partial(finish_kernel, width // (2 * HD)),
        out_shape=jax.ShapeDtypeStruct((rows, 2, cores * width // 2), F32),
        in_specs=[whole()],
        out_specs=whole(),
        compiler_params=params(),
        cost_estimate=cost(10**6, 2**20),
        name="finish_weights",
    )(parts)


def local(
    question_q,
    question_grad,
    question_kv,
    passage_kv,
    question_hidden,
    passage_hidden,
    reuse,
    passage_blocks,
):
    me = lax.axis_index("dp")
    peers = lax.axis_size("dp")
    groups = lax.axis_size("pass")
    cores = lax.axis_size("tensor")
    slots, slot_len, _, channels = passage_kv.shape
    samples, rows, width = question_q.shape
    heads = channels // HD
    group = width // channels
    refs = reuse.reshape(reuse.shape[0], reuse.shape[2])
    model_width = passage_hidden.shape[2]

    def exchange(x):
        return lax.all_to_all(x, "dp", split_axis=0, concat_axis=0, tiled=True)

    def from_partner(x):
        return lax.ppermute(x, "tensor", [(i, cores - 1 - i) for i in range(cores)])

    packed = pack_queries(refs, question_q, question_grad, slots)
    got = exchange(packed)

    hit = quotient(refs, slots) == me
    slot_of = jnp.sum(jnp.where(hit, lax.rem(refs, jnp.int32(slots)), 0), axis=1)
    owners = quotient(lax.dynamic_index_in_dim(refs, me, 0, keepdims=False), slots)
    blocks = lax.dynamic_index_in_dim(passage_blocks, me, 0, keepdims=False).reshape(slots)
    table = jnp.concatenate([slot_of, blocks])
    kv = jnp.transpose(passage_kv, (2, 0, 1, 3))
    turned = jnp.transpose(passage_kv[:, :, 0], (0, 2, 1))
    own_keys, own_values = question_kv[:, :, 0], question_kv[:, :, 1]
    own = own_stats(question_q, question_grad, own_keys, own_values, group)
    hidden_t = transpose_hidden(
        lax.axis_index("tensor").reshape(1),
        passage_hidden.reshape(-1, model_width),
        from_partner(passage_hidden).reshape(-1, model_width),
        question_hidden.reshape(-1, model_width),
        from_partner(question_hidden).reshape(-1, model_width),
        slots,
        samples,
        peers,
        groups,
    )
    got, hidden_t, own, turned = lax.optimization_barrier((got, hidden_t, own, turned))

    stats = exchange(owner_stats(table, got, kv, group))
    back, merged = merge(refs, stats, own, slots)
    joint = exchange(back)
    grads_query, own_dq = own_grads(
        question_q, question_grad, own_keys, own_values, merged, group
    )
    joint, grads_query, own_dq = lax.optimization_barrier((joint, grads_query, own_dq))
    far = groups // 2
    depths, homes = [], {}

    def array_of(*blocks):
        for row, block in enumerate(blocks):
            homes[block] = (len(depths), row)
        depths.append(len(blocks))
        return len(depths) - 1

    firsts, pairs = [], {}
    for head in range(heads):
        way = direction(head)
        firsts.append((array_of((far, head)), array_of((way * (1 - far), head))))
    for distance in range(far - 1, 0, -1):
        for head in range(heads):
            way = direction(head)
            pair = [(way * distance, head), (way * (1 - distance), head)]
            pairs[distance, head] = array_of(*(pair if distance > 1 else pair[:1]))
    final = array_of(*[(0, head) for head in range(heads)])
    places = [
        (place, [(head, *home) for (one, head), home in homes.items() if one == place])
        for place in [far, *range(far - 1, -far, -1)]
    ]
    grads_pass, dq_parts, *blocks = owner_grads(
        places, depths, table, got, joint, kv, turned, hidden_t, grads_query
    )
    sums = [
        travel([blocks[ahead][0], blocks[behind][0]], head)
        for head, (ahead, behind) in enumerate(firsts)
    ]
    ends = [None] * heads
    after = grads_pass
    for distance in range(far - 1, 0, -1):
        for head in range(heads):
            arrived = sums[head]
            if distance == 1:
                ends[head] = arrived[1]
                arrived = arrived[:1]
            added = add_arrived(
                blocks[pairs[distance, head]], arrived, after, f"add_{head}_{distance}"
            )
            after = added[0]
            sums[head] = travel(added, head)
    returned = exchange(dq_parts)
    summed = last_sums(
        blocks[final], [one for head in range(heads) for one in (sums[head][0], ends[head])]
    )
    summed, returned = lax.optimization_barrier((summed, returned))
    question_dq = sum_dq(owners, [returned], own_dq)

    share = summed.shape[0] // (peers * cores)
    parts = lax.all_to_all(
        summed.reshape(peers * cores, share, -1),
        ("dp", "tensor"),
        split_axis=0,
        concat_axis=0,
        tiled=True,
    )
    weight_grad = finish_weights(parts.reshape(peers, cores, share, -1))
    question_dkv = jnp.swapaxes(grads_query.reshape(samples, rows, heads, 2, HD), 2, 3)
    question_dkv = question_dkv.reshape(samples, rows, 2, channels)
    passage_dkv = jnp.swapaxes(grads_pass.reshape(slots, slot_len, heads, 2, HD), 2, 3)
    passage_dkv = passage_dkv.reshape(slots, slot_len, 2, channels)
    return (question_dq, question_dkv, passage_dkv, weight_grad)


def solution(mesh):
    in_specs = (
        P(("dp", "pass"), None, "tensor"),
        P(("dp", "pass"), None, "tensor"),
        P(("dp", "pass"), None, None, "tensor"),
        P(("dp", "pass"), None, None, "tensor"),
        P(("dp", "pass"), "tensor", None),
        P(("dp", "pass"), "tensor", None),
        P(None, "pass", None),
        P(None, "pass", None),
    )
    out_specs = (
        P(("dp", "pass"), None, "tensor"),
        P(("dp", "pass"), None, None, "tensor"),
        P(("dp", "pass"), None, None, "tensor"),
        P(("dp", "pass", "tensor"), None, None),
    )
    return jax.shard_map(local, mesh=mesh, in_specs=in_specs, out_specs=out_specs, check_vma=False)
```

```python
import functools
import math

import jax
import jax.numpy as jnp
from jax import lax
from jax.experimental import pallas as pl
from jax.experimental.pallas import tpu as pltpu
from jax.sharding import PartitionSpec as P

HD = 128
BLOCK = 128
NEG_FILL = -1e30
SCALE = HD ** (-0.5)
SCALE_LOG2 = SCALE * math.log2(math.e)
VMEM_LIMIT = 24 * 1024 * 1024
VMEM_MOST = 60 * 1024 * 1024
NT = (((1,), (1,)), ((), ()))
TN = (((0,), (0,)), ((), ()))
F32 = jnp.float32
BF16 = jnp.bfloat16


def params(limit=VMEM_LIMIT):
    return pltpu.CompilerParams(vmem_limit_bytes=limit)


def whole():
    return pl.BlockSpec(memory_space=pltpu.VMEM)


def smem():
    return pl.BlockSpec(memory_space=pltpu.SMEM)


def in_hbm():
    return pl.BlockSpec(memory_space=pltpu.HBM)


def cost(flops, nbytes, trans=0):
    return pl.CostEstimate(flops=flops, bytes_accessed=nbytes, transcendentals=trans)


def quotient(value, divisor):
    return lax.div(value, jnp.int32(divisor))


def head_rows(block, head, group):
    first = head * group
    return jnp.concatenate(
        [block[:, (first + r) * HD : (first + r + 1) * HD] for r in range(group)], axis=0
    )


def pack_kernel(slots, refs, blocks, q_ref, g_ref, out_ref, table, held, load_sems, sems):
    peers = out_ref.shape[0]
    samples, rows, _ = q_ref.shape
    per = peers // samples
    me = lax.axis_index("dp")
    loads = []
    for sample in range(samples):
        pair = []
        for part, src in enumerate((q_ref, g_ref)):
            pair.append(
                pltpu.make_async_copy(
                    src.at[sample],
                    held.at[sample, pl.ds(part * rows, rows)],
                    load_sems.at[sample, part],
                )
            )
            pair[-1].start()
        loads.append(pair)
    copies = []
    for j in range(peers):
        sample = j // per
        if j % per == 0:
            for copy in loads[sample]:
                copy.wait()
        dest = quotient(refs[me, j], slots)
        table[peers + slots + j] = dest
        copy = pltpu.make_async_copy(held.at[sample], out_ref.at[dest], sems.at[j])
        copy.start()
        copies.append(copy)
    for slot in range(slots):
        table[peers + slot] = blocks[me, slot]

    @pl.loop(0, peers)
    def _(reader):
        slot = jnp.int32(0)
        for j in range(peers):
            entry = refs[reader, j]
            mine = quotient(entry, slots) == me
            slot = slot + jnp.where(mine, lax.rem(entry, jnp.int32(slots)), 0)
        table[reader] = slot

    for copy in copies:
        copy.wait()


def pack_queries(refs, blocks, question_q, question_grad):
    samples, rows, width = question_q.shape
    peers = refs.shape[0]
    slots = blocks.shape[1]
    return pl.pallas_call(
        functools.partial(pack_kernel, slots),
        out_shape=(
            jax.ShapeDtypeStruct((peers, 2 * rows, width), BF16),
            jax.ShapeDtypeStruct((2 * peers + slots,), jnp.int32),
        ),
        in_specs=[smem(), smem(), in_hbm(), in_hbm()],
        out_specs=(in_hbm(), smem()),
        scratch_shapes=[
            pltpu.VMEM((samples, 2 * rows, width), BF16),
            pltpu.SemaphoreType.DMA((samples, 2)),
            pltpu.SemaphoreType.DMA((peers,)),
        ],
        compiler_params=params(VMEM_MOST),
        cost_estimate=cost(0, 6 * 2**20),
        name="pack_queries",
    )(refs, blocks, question_q, question_grad)


def scores_t(keys, queries, valid):
    scores = lax.dot_general(keys, queries, NT, preferred_element_type=F32) * SCALE_LOG2
    return jnp.where(valid, scores, NEG_FILL)


def part_stats(scores, prob_grad):
    top = jnp.max(scores, axis=0, keepdims=True)
    shifted = jnp.exp2(scores - top)
    total = jnp.sum(shifted, axis=0, keepdims=True)
    weighted = jnp.sum(shifted * prob_grad, axis=0, keepdims=True)
    return top + jnp.log2(total), weighted / total


def passage_valid(blocks, slot_len, columns):
    shape = (slot_len, columns)
    return lax.broadcasted_iota(jnp.int32, shape, 0) < blocks * BLOCK


def load_groups(src, held, sems):
    count = sems.shape[0]
    per = src.shape[0] // count
    return [
        pltpu.make_async_copy(
            src.at[pl.ds(i * per, per)], held.at[pl.ds(i * per, per)], sems.at[i]
        )
        for i in range(count)
    ]


def wait_group(i, src, held, sems):
    per = src.shape[0] // sems.shape[0]
    rows = pl.ds(i * per, per)
    pltpu.make_async_copy(src.at[rows], held.at[rows], sems.at[i]).wait()


def owner_stats_kernel(group, table, got_hbm, kv_ref, out_ref, got_ref, sems):
    peers, both, _ = got_ref.shape
    steps = sems.shape[0]
    per = peers // steps
    rows = both // 2
    slot_len = kv_ref.shape[2]
    heads = kv_ref.shape[3] // HD
    columns = group * rows
    for load in load_groups(got_hbm, got_ref, sems):
        load.start()

    @pl.loop(0, steps)
    def _(step):
        wait_group(step, got_hbm, got_ref, sems)
        for one in range(per):
            reader = step * per + one
            slot = table[reader]
            valid = passage_valid(table[peers + slot], slot_len, columns)
            logs, deltas = [], []
            for head in range(heads):
                lanes = slice(head * HD, (head + 1) * HD)
                queries = head_rows(got_ref[reader, :rows], head, group)
                grads = head_rows(got_ref[reader, rows:], head, group)
                scores = scores_t(kv_ref[0, slot, :, lanes], queries, valid)
                prob_grad = lax.dot_general(
                    kv_ref[1, slot, :, lanes], grads, NT, preferred_element_type=F32
                )
                log, delta = part_stats(scores, prob_grad)
                logs.append(log)
                deltas.append(delta)
            out_ref[reader] = jnp.concatenate(logs + deltas, axis=0)


def owner_stats(table, got, kv, group):
    peers, both, width = got.shape
    heads = kv.shape[3] // HD
    columns = group * both // 2
    return pl.pallas_call(
        functools.partial(owner_stats_kernel, group),
        out_shape=jax.ShapeDtypeStruct((peers, 2 * heads, columns), F32),
        in_specs=[smem(), in_hbm(), whole()],
        out_specs=whole(),
        scratch_shapes=[pltpu.VMEM(got.shape, BF16), pltpu.SemaphoreType.DMA((4,))],
        compiler_params=params(VMEM_MOST),
        cost_estimate=cost(2 * 10**9, 6 * 2**20, 2 * 10**6),
        name="owner_stats",
    )(table, got, kv)


def own_valid(own_rows, rows, group):
    shape = (own_rows, group * rows)
    key_row = lax.broadcasted_iota(jnp.int32, shape, 0)
    query_row = lax.rem(lax.broadcasted_iota(jnp.int32, shape, 1), jnp.int32(rows))
    return key_row <= query_row


def own_stats_kernel(group, q_ref, g_ref, k_ref, v_ref, out_ref):
    samples, rows, _ = q_ref.shape
    heads = k_ref.shape[2] // HD
    valid = own_valid(rows, rows, group)
    for sample in range(samples):
        logs, deltas = [], []
        for head in range(heads):
            lanes = slice(head * HD, (head + 1) * HD)
            queries = head_rows(q_ref[sample], head, group)
            grads = head_rows(g_ref[sample], head, group)
            scores = scores_t(k_ref[sample, :, lanes], queries, valid)
            prob_grad = lax.dot_general(
                v_ref[sample, :, lanes], grads, NT, preferred_element_type=F32
            )
            log, delta = part_stats(scores, prob_grad)
            logs.append(log)
            deltas.append(delta)
        out_ref[sample] = jnp.concatenate(logs + deltas, axis=0)


def own_stats(question_q, question_grad, keys, values, group):
    samples, rows, _ = question_q.shape
    heads = keys.shape[2] // HD
    return pl.pallas_call(
        functools.partial(own_stats_kernel, group),
        out_shape=jax.ShapeDtypeStruct((samples, 2 * heads, group * rows), F32),
        in_specs=[whole()] * 4,
        out_specs=whole(),
        compiler_params=params(),
        cost_estimate=cost(10**8, 2**20, 10**5),
        name="own_stats",
    )(question_q, question_grad, keys, values)


def merge_kernel(slots, refs, st_ref, own_ref, back_ref, merged_ref):
    samples, stat_rows, _ = own_ref.shape
    heads = stat_rows // 2
    per = st_ref.shape[0] // samples
    me = lax.axis_index("dp")
    for sample in range(samples):
        owners = [quotient(refs[me, sample * per + k], slots) for k in range(per)]
        parts = [own_ref[sample]] + [st_ref[owner] for owner in owners]
        logs = [part[:heads] for part in parts]
        top = functools.reduce(jnp.maximum, logs)
        weights = [jnp.exp2(log - top) for log in logs]
        total = sum(weights)
        delta = sum(weight * part[heads:] for weight, part in zip(weights, parts)) / total
        joint = jnp.concatenate([top + jnp.log2(total), delta], axis=0)
        merged_ref[sample] = joint
        for owner in owners:
            back_ref[owner] = joint


def merge(refs, stats, own, slots):
    return pl.pallas_call(
        functools.partial(merge_kernel, slots),
        out_shape=(
            jax.ShapeDtypeStruct(stats.shape, F32),
            jax.ShapeDtypeStruct(own.shape, F32),
        ),
        in_specs=[smem(), whole(), whole()],
        out_specs=(whole(), whole()),
        compiler_params=params(),
        cost_estimate=cost(10**5, 2**17, 10**4),
        name="merge_stats",
    )(refs, stats, own)


def probs_and_dscore(scores, prob_grad, joint, delta):
    probs = jnp.exp2(scores - joint)
    dscore = (probs * (prob_grad - delta) * SCALE).astype(BF16)
    return probs.astype(BF16), dscore


def owner_grads_kernel(
    group,
    places,
    table,
    got_hbm,
    joint_ref,
    kv_ref,
    own_ref,
    lower_ref,
    upper_ref,
    grad_out,
    dq_out,
    *rest,
):
    outs = rest[:-12]
    acc_ref, got_ref, h_ref, grad_ref, dq_ref, block_ref, turned_ref = rest[-12:-5]
    got_sems, h_sem, grad_sem, dq_sems, sems = rest[-5:]
    peers, both, _ = got_ref.shape
    steps = got_sems.shape[0]
    per = peers // steps
    rows = both // 2
    slot_len = kv_ref.shape[2]
    heads = kv_ref.shape[3] // HD
    for load in load_groups(got_hbm, got_ref, got_sems):
        load.start()
    share = lower_ref.shape[1]
    hidden_loads = [
        pltpu.make_async_copy(src, h_ref.at[:, pl.ds(i * share, share)], h_sem.at[i])
        for i, src in enumerate((lower_ref, upper_ref))
    ]
    for load in hidden_loads:
        load.start()
    acc_ref[...] = jnp.zeros_like(acc_ref)
    for slot in range(turned_ref.shape[0]):
        turned_ref[slot] = kv_ref[0, slot].T

    @pl.loop(0, steps)
    def _(step):
        wait_group(step, got_hbm, got_ref, got_sems)
        for one in range(per):
            reader = step * per + one
            slot = table[reader]
            valid = passage_valid(table[peers + slot], slot_len, group * rows)
            for head in range(heads):
                lanes = slice(head * HD, (head + 1) * HD)
                key_lanes = slice(2 * head * HD, (2 * head + 1) * HD)
                value_lanes = slice((2 * head + 1) * HD, (2 * head + 2) * HD)
                queries = head_rows(got_ref[reader, :rows], head, group)
                grads = head_rows(got_ref[reader, rows:], head, group)
                scores = scores_t(kv_ref[0, slot, :, lanes], queries, valid)
                prob_grad = lax.dot_general(
                    kv_ref[1, slot, :, lanes], grads, NT, preferred_element_type=F32
                )
                joint = joint_ref[reader, head : head + 1]
                delta = joint_ref[reader, heads + head : heads + head + 1]
                probs, dscore = probs_and_dscore(scores, prob_grad, joint, delta)
                acc_ref[slot, :, key_lanes] += jnp.dot(
                    dscore, queries, preferred_element_type=F32
                )
                acc_ref[slot, :, value_lanes] += jnp.dot(
                    probs, grads, preferred_element_type=F32
                )
                dq = jnp.dot(turned_ref[slot, lanes], dscore, preferred_element_type=F32)
                dq = dq.astype(BF16).T
                for r in range(group):
                    column = (head * group + r) * HD
                    dq_ref[reader, :, column : column + HD] = dq[r * rows : (r + 1) * rows]
        part = pl.ds(step * per, per)
        pltpu.make_async_copy(dq_ref.at[part], dq_out.at[part], dq_sems.at[step]).start()

    for one in range(acc_ref.shape[0]):
        grad_ref[one * slot_len : (one + 1) * slot_len] = acc_ref[one].astype(BF16)
    copies = [pltpu.make_async_copy(grad_ref, grad_out, grad_sem)]
    copies[0].start()
    for load in hidden_loads:
        load.wait()
    count = h_ref.shape[0]
    tokens = grad_ref.shape[0]
    k = 0
    for place, uses in places:
        pass_group = lax.rem(lax.axis_index("pass") + (place + count), count)
        total = jnp.dot(h_ref[pass_group, :, :tokens], grad_ref[...], preferred_element_type=F32)
        total = total + jnp.dot(
            h_ref[pass_group, :, tokens:], own_ref[...], preferred_element_type=F32
        )
        for head, out, row in uses:
            lanes = slice(2 * head * HD, 2 * (head + 1) * HD)
            block_ref[k] = total[:, lanes].astype(BF16)
            copies.append(
                pltpu.make_async_copy(block_ref.at[k], outs[out].at[row], sems.at[k])
            )
            copies[-1].start()
            k += 1
    for copy in copies:
        copy.wait()
    for step in range(steps):
        wait_group(step, dq_ref, dq_out, dq_sems)


def owner_grads(places, depths, table, got, joint, kv, hidden_t, grads_query):
    peers, both, width = got.shape
    _, slots, slot_len, channels = kv.shape
    columns = joint.shape[2]
    groups, half, tokens = hidden_t[0].shape
    share = 2 * half
    count = sum(depths)
    grads = jax.ShapeDtypeStruct((slots * slot_len, 2 * channels), BF16)
    dq = jax.ShapeDtypeStruct((peers, both // 2, width), BF16)
    return pl.pallas_call(
        functools.partial(owner_grads_kernel, 2 * columns // both, places),
        out_shape=(
            grads,
            dq,
            *[jax.ShapeDtypeStruct((depth, share, 2 * HD), BF16) for depth in depths],
        ),
        in_specs=[smem(), in_hbm(), whole(), whole(), whole(), in_hbm(), in_hbm()],
        out_specs=tuple(in_hbm() for _ in range(2 + len(depths))),
        scratch_shapes=[
            pltpu.VMEM((slots, slot_len, 2 * channels), F32),
            pltpu.VMEM(got.shape, BF16),
            pltpu.VMEM((groups, share, tokens), BF16),
            pltpu.VMEM(grads.shape, BF16),
            pltpu.VMEM(dq.shape, BF16),
            pltpu.VMEM((count, share, 2 * HD), BF16),
            pltpu.VMEM((slots, channels, slot_len), BF16),
            pltpu.SemaphoreType.DMA((4,)),
            pltpu.SemaphoreType.DMA((2,)),
            pltpu.SemaphoreType.DMA,
            pltpu.SemaphoreType.DMA((4,)),
            pltpu.SemaphoreType.DMA((count,)),
        ],
        compiler_params=params(VMEM_MOST),
        cost_estimate=cost(16 * 10**9, 24 * 2**20, 2 * 10**6),
        name="owner_grads",
    )(table, got, joint, kv, grads_query, *hidden_t)


def own_grads_kernel(group, q_ref, g_ref, k_ref, v_ref, joint_ref, grad_ref, dq_ref):
    samples, rows, _ = q_ref.shape
    heads = k_ref.shape[2] // HD
    valid = own_valid(rows, rows, group)
    for sample in range(samples):
        token = slice(sample * rows, (sample + 1) * rows)
        for head in range(heads):
            lanes = slice(head * HD, (head + 1) * HD)
            joint = joint_ref[sample, head : head + 1]
            delta = joint_ref[sample, heads + head : heads + head + 1]
            queries = head_rows(q_ref[sample], head, group)
            grads = head_rows(g_ref[sample], head, group)
            keys = k_ref[sample, :, lanes]
            scores = scores_t(keys, queries, valid)
            prob_grad = lax.dot_general(
                v_ref[sample, :, lanes], grads, NT, preferred_element_type=F32
            )
            probs, dscore = probs_and_dscore(scores, prob_grad, joint, delta)
            key_grad = jnp.dot(dscore, queries, preferred_element_type=F32)
            value_grad = jnp.dot(probs, grads, preferred_element_type=F32)
            key_lanes = slice(2 * head * HD, (2 * head + 1) * HD)
            value_lanes = slice((2 * head + 1) * HD, (2 * head + 2) * HD)
            grad_ref[token, key_lanes] = key_grad.astype(BF16)
            grad_ref[token, value_lanes] = value_grad.astype(BF16)
            dq = lax.dot_general(dscore, keys, TN, preferred_element_type=F32).astype(BF16)
            for r in range(group):
                column = (head * group + r) * HD
                dq_ref[sample, :, column : column + HD] = dq[r * rows : (r + 1) * rows]


def own_grads(question_q, question_grad, keys, values, joint, group):
    samples, rows, width = question_q.shape
    heads = keys.shape[2] // HD
    return pl.pallas_call(
        functools.partial(own_grads_kernel, group),
        out_shape=(
            jax.ShapeDtypeStruct((samples * rows, 2 * heads * HD), BF16),
            jax.ShapeDtypeStruct((samples, rows, width), BF16),
        ),
        in_specs=[whole()] * 5,
        out_specs=(whole(), whole()),
        compiler_params=params(),
        cost_estimate=cost(3 * 10**8, 3 * 2**20, 10**5),
        name="own_grads",
    )(question_q, question_grad, keys, values, joint)


def sum_dq_kernel(heads, owners, *refs):
    out_ref = refs[-1]
    own_ref = refs[-2]
    per = (len(refs) - 2) // heads
    width = refs[0].shape[2]
    for head in range(heads):
        lanes = slice(head * width, (head + 1) * width)
        total = own_ref[0, :, lanes].astype(F32)
        for ref in refs[head * per : (head + 1) * per]:
            total = total + ref[0].astype(F32)
        out_ref[0, :, lanes] = total.astype(BF16)


def sum_dq(table, returned, own):
    samples, rows, width = own.shape
    peers = returned[0].shape[0]
    per = peers // samples
    heads = len(returned)
    first = table.shape[0] - peers

    def from_owner(k):
        return pl.BlockSpec((1, rows, width // heads), lambda s, o: (o[first + s * per + k], 0, 0))

    return pl.pallas_call(
        functools.partial(sum_dq_kernel, heads),
        out_shape=jax.ShapeDtypeStruct((samples, rows, width), BF16),
        grid_spec=pltpu.PrefetchScalarGridSpec(
            num_scalar_prefetch=1,
            grid=(samples,),
            in_specs=[from_owner(k) for k in range(per)] * heads
            + [pl.BlockSpec((1, rows, width), lambda s, o: (s, 0, 0))],
            out_specs=pl.BlockSpec((1, rows, width), lambda s, o: (s, 0, 0)),
        ),
        compiler_params=params(),
        cost_estimate=cost(2 * 10**6, 4 * 2**20),
        name="sum_dq",
    )(table, *[one for one in returned for _ in range(per)], own)


def transpose_kernel(slots, samples, owners, core, mine_p, other_p, mine_q, other_q, out_ref):
    groups, share, _ = out_ref.shape
    lower = core[0] == 0
    first_p = jnp.where(lower, mine_p[...], other_p[...])
    second_p = jnp.where(lower, other_p[...], mine_p[...])
    first_q = jnp.where(lower, mine_q[...], other_q[...])
    second_q = jnp.where(lower, other_q[...], mine_q[...])
    half = first_p.shape[0] // slots
    part = first_q.shape[0] // samples
    pieces = []
    for slot in range(slots):
        pieces.append(first_p[slot * half : (slot + 1) * half])
        pieces.append(second_p[slot * half : (slot + 1) * half])
    for sample in range(samples):
        pieces.append(first_q[sample * part : (sample + 1) * part])
        pieces.append(second_q[sample * part : (sample + 1) * part])
    turned = jnp.concatenate(pieces, axis=0).T
    rows = share // owners
    for owner in range(owners):
        for group in range(groups):
            first = (owner * groups + group) * rows
            out_ref[group, owner * rows : (owner + 1) * rows] = turned[first : first + rows]


def transpose_hidden(core, hidden, slots, samples, owners, groups, half):
    width = hidden[0].shape[1]
    tokens = sum(one.shape[0] for one in hidden)
    per = 2
    tile = per * width // owners
    steps = width // tile // 2
    return pl.pallas_call(
        functools.partial(transpose_kernel, slots, samples, per),
        out_shape=jax.ShapeDtypeStruct((groups, width // groups // 2, tokens), BF16),
        grid_spec=pltpu.PrefetchScalarGridSpec(
            num_scalar_prefetch=1,
            grid=(steps,),
            in_specs=[
                pl.BlockSpec((one.shape[0], tile), lambda i, c: (0, half * steps + i))
                for one in hidden
            ],
            out_specs=pl.BlockSpec((groups, tile // groups, tokens), lambda i, c: (0, i, 0)),
        ),
        compiler_params=params(VMEM_MOST),
        cost_estimate=cost(0, 12 * 2**20),
        name=f"transpose_hidden_{half}",
    )(core, *hidden)


def add_kernel(count, blocks_ref, *refs):
    outs = refs[len(refs) - count :]
    for k, (arrived, out_ref) in enumerate(zip(refs, outs)):
        out_ref[...] = (blocks_ref[k].astype(F32) + arrived[...].astype(F32)).astype(BF16)


def add_arrived(blocks, arrived, after, name):
    count = len(arrived)
    return pl.pallas_call(
        functools.partial(add_kernel, count),
        out_shape=tuple(jax.ShapeDtypeStruct(one.shape, BF16) for one in arrived),
        in_specs=[whole()] * (1 + count) + [pl.BlockSpec(memory_space=pl.ANY)],
        out_specs=(whole(),) * count,
        compiler_params=params(),
        cost_estimate=cost(8 * 10**9, 2**20),
        name=name,
    )(blocks, *arrived, after)


def last_kernel(heads, blocks_ref, *refs):
    out_ref = refs[-1]
    for head in range(heads):
        total = blocks_ref[head].astype(F32)
        for ref in refs[2 * head : 2 * head + 2]:
            total = total + ref[...].astype(F32)
        width = total.shape[1]
        out_ref[:, head * width : (head + 1) * width] = total.astype(BF16)


def last_sums(blocks, arrived):
    heads, share, width = blocks.shape
    return pl.pallas_call(
        functools.partial(last_kernel, heads),
        out_shape=jax.ShapeDtypeStruct((share, heads * width), BF16),
        in_specs=[whole()] * (1 + 2 * heads),
        out_specs=whole(),
        compiler_params=params(),
        cost_estimate=cost(10**6, 2**21),
        name="weights_last",
    )(blocks, *arrived)


def travel(blocks, head):
    count = lax.axis_size("pass")
    ways = [direction(head), -direction(head)]
    return [
        lax.ppermute(block, "pass", [(i, (i + way) % count) for i in range(count)])
        for block, way in zip(blocks, ways)
    ]


def direction(head):
    return 1 if head % 2 == 0 else -1


def finish_kernel(heads, x_ref, out_ref):
    owners, cores, _, _ = x_ref.shape
    for core in range(cores):
        total = x_ref[0, core].astype(F32)
        for owner in range(1, owners):
            total = total + x_ref[owner, core].astype(F32)
        for head in range(heads):
            lanes = slice((core * heads + head) * HD, (core * heads + head + 1) * HD)
            for part in range(2):
                first = (head * 2 + part) * HD
                out_ref[:, part, lanes] = total[:, first : first + HD]


def finish_weights(parts):
    owners, cores, rows, width = parts.shape
    return pl.pallas_call(
        functools.partial(finish_kernel, width // (2 * HD)),
        out_shape=jax.ShapeDtypeStruct((rows, 2, cores * width // 2), F32),
        in_specs=[whole()],
        out_specs=whole(),
        compiler_params=params(),
        cost_estimate=cost(10**6, 2**20),
        name="finish_weights",
    )(parts)


def local(
    question_q,
    question_grad,
    question_kv,
    passage_kv,
    question_hidden,
    passage_hidden,
    reuse,
    passage_blocks,
):
    peers = lax.axis_size("dp")
    groups = lax.axis_size("pass")
    cores = lax.axis_size("tensor")
    slots, slot_len, _, channels = passage_kv.shape
    samples, rows, width = question_q.shape
    heads = channels // HD
    group = width // channels
    refs = reuse.reshape(reuse.shape[0], reuse.shape[2])
    model_width = passage_hidden.shape[2]

    def exchange(x):
        return lax.all_to_all(x, "dp", split_axis=0, concat_axis=0, tiled=True)

    def from_partner(x):
        return lax.ppermute(x, "tensor", [(i, cores - 1 - i) for i in range(cores)])

    kv = jnp.transpose(passage_kv, (2, 0, 1, 3))
    blocks = passage_blocks.reshape(peers, slots)
    packed, table = pack_queries(refs, blocks, question_q, question_grad)
    packed, table, kv = lax.optimization_barrier((packed, table, kv))
    got = exchange(packed)
    got, passage_hidden, question_hidden, question_kv, question_q, question_grad = (
        lax.optimization_barrier(
            (got, passage_hidden, question_hidden, question_kv, question_q, question_grad)
        )
    )
    own_keys, own_values = question_kv[:, :, 0], question_kv[:, :, 1]

    parts = owner_stats(table, got, kv, group)
    parts, own_keys, own_values, passage_hidden, question_hidden = lax.optimization_barrier(
        (parts, own_keys, own_values, passage_hidden, question_hidden)
    )
    stats = exchange(parts)
    own = own_stats(question_q, question_grad, own_keys, own_values, group)
    hidden = [
        one.reshape(-1, model_width)
        for both in (passage_hidden, question_hidden)
        for one in (both, from_partner(both))
    ]

    def turned_half(half):
        core = lax.axis_index("tensor").reshape(1)
        return transpose_hidden(core, hidden, slots, samples, peers, groups, half)

    lower = turned_half(0)
    stats, lower = lax.optimization_barrier((stats, lower))
    back, merged = merge(refs, stats, own, slots)
    joint = exchange(back)
    grads_query, own_dq = own_grads(
        question_q, question_grad, own_keys, own_values, merged, group
    )
    upper = turned_half(1)
    joint, grads_query, own_dq, upper = lax.optimization_barrier(
        (joint, grads_query, own_dq, upper)
    )
    hidden_t = [lower, upper]
    far = groups // 2
    depths, homes = [], {}

    def array_of(*blocks):
        for row, block in enumerate(blocks):
            homes[block] = (len(depths), row)
        depths.append(len(blocks))
        return len(depths) - 1

    firsts, pairs = [], {}
    for head in range(heads):
        way = direction(head)
        firsts.append((array_of((far, head)), array_of((way * (1 - far), head))))
    for distance in range(far - 1, 0, -1):
        for head in range(heads):
            way = direction(head)
            pair = [(way * distance, head), (way * (1 - distance), head)]
            pairs[distance, head] = array_of(*(pair if distance > 1 else pair[:1]))
    final = array_of(*[(0, head) for head in range(heads)])
    places = [
        (place, [(head, *home) for (one, head), home in homes.items() if one == place])
        for place in [far, *range(far - 1, -far, -1)]
    ]
    grads_pass, dq_parts, *blocks = owner_grads(
        places, depths, table, got, joint, kv, hidden_t, grads_query
    )
    sums = [
        travel([blocks[ahead][0], blocks[behind][0]], head)
        for head, (ahead, behind) in enumerate(firsts)
    ]
    ends = [None] * heads
    after = grads_pass
    for distance in range(far - 1, 0, -1):
        for head in range(heads):
            arrived = sums[head]
            if distance == 1:
                ends[head] = arrived[1]
                arrived = arrived[:1]
            added = add_arrived(
                blocks[pairs[distance, head]], arrived, after, f"add_{head}_{distance}"
            )
            after = added[0]
            sums[head] = travel(added, head)
    returned = exchange(dq_parts)
    summed = last_sums(
        blocks[final], [one for head in range(heads) for one in (sums[head][0], ends[head])]
    )
    summed, returned = lax.optimization_barrier((summed, returned))
    question_dq = sum_dq(table, [returned], own_dq)

    share = summed.shape[0] // (peers * cores)
    parts = lax.all_to_all(
        summed.reshape(peers * cores, share, -1),
        ("dp", "tensor"),
        split_axis=0,
        concat_axis=0,
        tiled=True,
    )
    weight_grad = finish_weights(parts.reshape(peers, cores, share, -1))
    question_dkv = jnp.swapaxes(grads_query.reshape(samples, rows, heads, 2, HD), 2, 3)
    question_dkv = question_dkv.reshape(samples, rows, 2, channels)
    passage_dkv = jnp.swapaxes(grads_pass.reshape(slots, slot_len, heads, 2, HD), 2, 3)
    passage_dkv = passage_dkv.reshape(slots, slot_len, 2, channels)
    return (question_dq, question_dkv, passage_dkv, weight_grad)


def solution(mesh):
    in_specs = (
        P(("dp", "pass"), None, "tensor"),
        P(("dp", "pass"), None, "tensor"),
        P(("dp", "pass"), None, None, "tensor"),
        P(("dp", "pass"), None, None, "tensor"),
        P(("dp", "pass"), "tensor", None),
        P(("dp", "pass"), "tensor", None),
        P(None, "pass", None),
        P(None, "pass", None),
    )
    out_specs = (
        P(("dp", "pass"), None, "tensor"),
        P(("dp", "pass"), None, None, "tensor"),
        P(("dp", "pass"), None, None, "tensor"),
        P(("dp", "pass", "tensor"), None, None),
    )
    return jax.shard_map(local, mesh=mesh, in_specs=in_specs, out_specs=out_specs, check_vma=False)
```

```python
import functools
import math

import jax
import jax.numpy as jnp
from jax import lax
from jax.experimental import pallas as pl
from jax.experimental.pallas import tpu as pltpu
from jax.sharding import PartitionSpec as P

HD = 128
BLOCK = 128
NEG_FILL = -1e30
SCALE = HD ** (-0.5)
SCALE_LOG2 = SCALE * math.log2(math.e)
VMEM_LIMIT = 24 * 1024 * 1024
VMEM_MOST = 60 * 1024 * 1024
NT = (((1,), (1,)), ((), ()))
TN = (((0,), (0,)), ((), ()))
F32 = jnp.float32
BF16 = jnp.bfloat16


def params(limit=VMEM_LIMIT):
    return pltpu.CompilerParams(vmem_limit_bytes=limit)


def whole():
    return pl.BlockSpec(memory_space=pltpu.VMEM)


def smem():
    return pl.BlockSpec(memory_space=pltpu.SMEM)


def in_hbm():
    return pl.BlockSpec(memory_space=pltpu.HBM)


def cost(flops, nbytes, trans=0):
    return pl.CostEstimate(flops=flops, bytes_accessed=nbytes, transcendentals=trans)


def quotient(value, divisor):
    return lax.div(value, jnp.int32(divisor))


def head_rows(block, head, group):
    first = head * group
    return jnp.concatenate(
        [block[:, (first + r) * HD : (first + r + 1) * HD] for r in range(group)], axis=0
    )


def pack_kernel(slots, refs, blocks, q_ref, g_ref, out_ref, table, held, load_sems, sems):
    peers = out_ref.shape[0]
    samples, rows, _ = q_ref.shape
    per = peers // samples
    me = lax.axis_index("dp")
    loads = []
    for sample in range(samples):
        pair = []
        for part, src in enumerate((q_ref, g_ref)):
            pair.append(
                pltpu.make_async_copy(
                    src.at[sample],
                    held.at[sample, pl.ds(part * rows, rows)],
                    load_sems.at[sample, part],
                )
            )
            pair[-1].start()
        loads.append(pair)
    copies = []
    for j in range(peers):
        sample = j // per
        if j % per == 0:
            for copy in loads[sample]:
                copy.wait()
        dest = quotient(refs[me, j], slots)
        table[peers + slots + j] = dest
        copy = pltpu.make_async_copy(held.at[sample], out_ref.at[dest], sems.at[j])
        copy.start()
        copies.append(copy)
    for slot in range(slots):
        table[peers + slot] = blocks[me, slot]

    @pl.loop(0, peers)
    def _(reader):
        slot = jnp.int32(0)
        for j in range(peers):
            entry = refs[reader, j]
            mine = quotient(entry, slots) == me
            slot = slot + jnp.where(mine, lax.rem(entry, jnp.int32(slots)), 0)
        table[reader] = slot

    for copy in copies:
        copy.wait()


def pack_queries(refs, blocks, question_q, question_grad):
    samples, rows, width = question_q.shape
    peers = refs.shape[0]
    slots = blocks.shape[1]
    return pl.pallas_call(
        functools.partial(pack_kernel, slots),
        out_shape=(
            jax.ShapeDtypeStruct((peers, 2 * rows, width), BF16),
            jax.ShapeDtypeStruct((2 * peers + slots,), jnp.int32),
        ),
        in_specs=[smem(), smem(), in_hbm(), in_hbm()],
        out_specs=(in_hbm(), smem()),
        scratch_shapes=[
            pltpu.VMEM((samples, 2 * rows, width), BF16),
            pltpu.SemaphoreType.DMA((samples, 2)),
            pltpu.SemaphoreType.DMA((peers,)),
        ],
        compiler_params=params(VMEM_MOST),
        cost_estimate=cost(0, 6 * 2**20),
        name="pack_queries",
    )(refs, blocks, question_q, question_grad)


def scores_t(keys, queries, valid):
    scores = lax.dot_general(keys, queries, NT, preferred_element_type=F32) * SCALE_LOG2
    return jnp.where(valid, scores, NEG_FILL)


def part_stats(scores, prob_grad):
    top = jnp.max(scores, axis=0, keepdims=True)
    shifted = jnp.exp2(scores - top)
    total = jnp.sum(shifted, axis=0, keepdims=True)
    weighted = jnp.sum(shifted * prob_grad, axis=0, keepdims=True)
    return top + jnp.log2(total), weighted / total


def passage_valid(blocks, slot_len, columns):
    shape = (slot_len, columns)
    return lax.broadcasted_iota(jnp.int32, shape, 0) < blocks * BLOCK


def load_groups(src, held, sems):
    count = sems.shape[0]
    per = src.shape[0] // count
    return [
        pltpu.make_async_copy(
            src.at[pl.ds(i * per, per)], held.at[pl.ds(i * per, per)], sems.at[i]
        )
        for i in range(count)
    ]


def wait_group(i, src, held, sems):
    per = src.shape[0] // sems.shape[0]
    rows = pl.ds(i * per, per)
    pltpu.make_async_copy(src.at[rows], held.at[rows], sems.at[i]).wait()


def owner_stats_kernel(group, table, got_hbm, kv_ref, out_ref, got_ref, sems):
    peers, both, _ = got_ref.shape
    steps = sems.shape[0]
    per = peers // steps
    rows = both // 2
    slot_len = kv_ref.shape[2]
    heads = kv_ref.shape[3] // HD
    columns = group * rows
    for load in load_groups(got_hbm, got_ref, sems):
        load.start()

    @pl.loop(0, steps)
    def _(step):
        wait_group(step, got_hbm, got_ref, sems)
        for one in range(per):
            reader = step * per + one
            slot = table[reader]
            valid = passage_valid(table[peers + slot], slot_len, columns)
            logs, deltas = [], []
            for head in range(heads):
                lanes = slice(head * HD, (head + 1) * HD)
                queries = head_rows(got_ref[reader, :rows], head, group)
                grads = head_rows(got_ref[reader, rows:], head, group)
                scores = scores_t(kv_ref[0, slot, :, lanes], queries, valid)
                prob_grad = lax.dot_general(
                    kv_ref[1, slot, :, lanes], grads, NT, preferred_element_type=F32
                )
                log, delta = part_stats(scores, prob_grad)
                logs.append(log)
                deltas.append(delta)
            out_ref[reader] = jnp.concatenate(logs + deltas, axis=0)


def owner_stats(table, got, kv, group):
    peers, both, width = got.shape
    heads = kv.shape[3] // HD
    columns = group * both // 2
    return pl.pallas_call(
        functools.partial(owner_stats_kernel, group),
        out_shape=jax.ShapeDtypeStruct((peers, 2 * heads, columns), F32),
        in_specs=[smem(), in_hbm(), whole()],
        out_specs=whole(),
        scratch_shapes=[pltpu.VMEM(got.shape, BF16), pltpu.SemaphoreType.DMA((4,))],
        compiler_params=params(VMEM_MOST),
        cost_estimate=cost(2 * 10**9, 6 * 2**20, 2 * 10**6),
        name="owner_stats",
    )(table, got, kv)


def own_valid(own_rows, rows, group):
    shape = (own_rows, group * rows)
    key_row = lax.broadcasted_iota(jnp.int32, shape, 0)
    query_row = lax.rem(lax.broadcasted_iota(jnp.int32, shape, 1), jnp.int32(rows))
    return key_row <= query_row


def own_stats_kernel(group, q_ref, g_ref, k_ref, v_ref, out_ref):
    samples, rows, _ = q_ref.shape
    heads = k_ref.shape[2] // HD
    valid = own_valid(rows, rows, group)
    for sample in range(samples):
        logs, deltas = [], []
        for head in range(heads):
            lanes = slice(head * HD, (head + 1) * HD)
            queries = head_rows(q_ref[sample], head, group)
            grads = head_rows(g_ref[sample], head, group)
            scores = scores_t(k_ref[sample, :, lanes], queries, valid)
            prob_grad = lax.dot_general(
                v_ref[sample, :, lanes], grads, NT, preferred_element_type=F32
            )
            log, delta = part_stats(scores, prob_grad)
            logs.append(log)
            deltas.append(delta)
        out_ref[sample] = jnp.concatenate(logs + deltas, axis=0)


def own_stats(question_q, question_grad, keys, values, group):
    samples, rows, _ = question_q.shape
    heads = keys.shape[2] // HD
    return pl.pallas_call(
        functools.partial(own_stats_kernel, group),
        out_shape=jax.ShapeDtypeStruct((samples, 2 * heads, group * rows), F32),
        in_specs=[whole()] * 4,
        out_specs=whole(),
        compiler_params=params(),
        cost_estimate=cost(10**8, 2**20, 10**5),
        name="own_stats",
    )(question_q, question_grad, keys, values)


def merge_kernel(slots, refs, st_ref, own_ref, back_ref, merged_ref):
    samples, stat_rows, _ = own_ref.shape
    heads = stat_rows // 2
    per = st_ref.shape[0] // samples
    me = lax.axis_index("dp")
    for sample in range(samples):
        owners = [quotient(refs[me, sample * per + k], slots) for k in range(per)]
        parts = [own_ref[sample]] + [st_ref[owner] for owner in owners]
        logs = [part[:heads] for part in parts]
        top = functools.reduce(jnp.maximum, logs)
        weights = [jnp.exp2(log - top) for log in logs]
        total = sum(weights)
        delta = sum(weight * part[heads:] for weight, part in zip(weights, parts)) / total
        joint = jnp.concatenate([top + jnp.log2(total), delta], axis=0)
        merged_ref[sample] = joint
        for owner in owners:
            back_ref[owner] = joint


def merge(refs, stats, own, slots):
    return pl.pallas_call(
        functools.partial(merge_kernel, slots),
        out_shape=(
            jax.ShapeDtypeStruct(stats.shape, F32),
            jax.ShapeDtypeStruct(own.shape, F32),
        ),
        in_specs=[smem(), whole(), whole()],
        out_specs=(whole(), whole()),
        compiler_params=params(),
        cost_estimate=cost(10**5, 2**17, 10**4),
        name="merge_stats",
    )(refs, stats, own)


def probs_and_dscore(scores, prob_grad, joint, delta):
    probs = jnp.exp2(scores - joint)
    dscore = (probs * (prob_grad - delta) * SCALE).astype(BF16)
    return probs.astype(BF16), dscore


def owner_grads_kernel(
    group,
    places,
    table,
    got_hbm,
    joint_ref,
    kv_ref,
    own_ref,
    mine_pass,
    other_pass,
    mine_query,
    other_query,
    grad_out,
    dq_out,
    *rest,
):
    outs = rest[:-14]
    acc_ref, got_ref, h_ref, grad_ref, dq_ref, block_ref, turned_ref, mixed_ref = rest[-14:-6]
    plain_ref = rest[-6]
    got_sems, h_sem, grad_sem, dq_sems, sems = rest[-5:]
    peers, both, _ = got_ref.shape
    steps = got_sems.shape[0]
    per = peers // steps
    rows = both // 2
    slot_len = kv_ref.shape[2]
    heads = kv_ref.shape[3] // HD
    for load in load_groups(got_hbm, got_ref, got_sems):
        load.start()
    groups, share, _ = h_ref.shape
    tile = groups * share // peers
    part = share // peers

    def hidden_loads(step):
        lanes = pl.ds(pl.multiple_of(step * per * tile, per * tile), per * tile)
        loads, row = [], 0
        for k, src in enumerate((mine_pass, other_pass, mine_query, other_query)):
            rows_here = pl.ds(row, src.shape[0])
            loads.append(
                pltpu.make_async_copy(
                    src.at[:, lanes], plain_ref.at[rows_here, lanes], h_sem.at[step, k]
                )
            )
            row += src.shape[0]
        return loads

    for step in range(steps):
        for load in hidden_loads(step):
            load.start()
    acc_ref[...] = jnp.zeros_like(acc_ref)
    for slot in range(turned_ref.shape[0]):
        turned_ref[slot] = kv_ref[0, slot].T

    @pl.loop(0, steps)
    def _(step):
        wait_group(step, got_hbm, got_ref, got_sems)
        for load in hidden_loads(step):
            load.wait()
        for one in range(per):
            reader = step * per + one
            first = pl.multiple_of(reader * tile, tile)
            turned = plain_ref[:, pl.ds(first, tile)].T
            for k in range(groups):
                place = pl.ds(pl.multiple_of(reader * part, part), part)
                h_ref[k, place] = turned[k * part : (k + 1) * part]
            slot = table[reader]
            valid = passage_valid(table[peers + slot], slot_len, group * rows)
            for head in range(heads):
                lanes = slice(head * HD, (head + 1) * HD)
                key_lanes = slice(2 * head * HD, (2 * head + 1) * HD)
                value_lanes = slice((2 * head + 1) * HD, (2 * head + 2) * HD)
                queries = head_rows(got_ref[reader, :rows], head, group)
                grads = head_rows(got_ref[reader, rows:], head, group)
                scores = scores_t(kv_ref[0, slot, :, lanes], queries, valid)
                prob_grad = lax.dot_general(
                    kv_ref[1, slot, :, lanes], grads, NT, preferred_element_type=F32
                )
                joint = joint_ref[reader, head : head + 1]
                delta = joint_ref[reader, heads + head : heads + head + 1]
                probs, dscore = probs_and_dscore(scores, prob_grad, joint, delta)
                acc_ref[slot, :, key_lanes] += jnp.dot(
                    dscore, queries, preferred_element_type=F32
                )
                acc_ref[slot, :, value_lanes] += jnp.dot(
                    probs, grads, preferred_element_type=F32
                )
                dq = jnp.dot(turned_ref[slot, lanes], dscore, preferred_element_type=F32)
                dq = dq.astype(BF16).T
                for r in range(group):
                    column = (head * group + r) * HD
                    dq_ref[reader, :, column : column + HD] = dq[r * rows : (r + 1) * rows]
        done = pl.ds(step * per, per)
        pltpu.make_async_copy(dq_ref.at[done], dq_out.at[done], dq_sems.at[step]).start()

    for one in range(acc_ref.shape[0]):
        grad_ref[one * slot_len : (one + 1) * slot_len] = acc_ref[one].astype(BF16)
    copies = [pltpu.make_async_copy(grad_ref, grad_out, grad_sem)]
    copies[0].start()
    count = h_ref.shape[0]
    mix_tokens(grad_ref, mixed_ref, 0, acc_ref.shape[0])
    mix_tokens(own_ref, mixed_ref, grad_ref.shape[0], own_ref.shape[0] // rows)
    k = 0
    for place, uses in places:
        pass_group = lax.rem(lax.axis_index("pass") + (place + count), count)
        total = jnp.dot(h_ref[pass_group], mixed_ref[...], preferred_element_type=F32)
        for head, out, row in uses:
            lanes = slice(2 * head * HD, 2 * (head + 1) * HD)
            block_ref[k] = total[:, lanes].astype(BF16)
            copies.append(
                pltpu.make_async_copy(block_ref.at[k], outs[out].at[row], sems.at[k])
            )
            copies[-1].start()
            k += 1
    for copy in copies:
        copy.wait()
    for step in range(steps):
        wait_group(step, dq_ref, dq_out, dq_sems)


def mix_tokens(src, out_ref, start, pieces):
    half = src.shape[0] // pieces // 2
    core = lax.axis_index("tensor")
    for k, side in enumerate((core, 1 - core)):
        for piece in range(pieces):
            first = pl.multiple_of((2 * piece + side) * half, half)
            row = start + (k * pieces + piece) * half
            out_ref[row : row + half] = src[pl.ds(first, half)]


def owner_grads(places, depths, table, got, joint, kv, hidden, grads_query, groups):
    peers, both, width = got.shape
    _, slots, slot_len, channels = kv.shape
    columns = joint.shape[2]
    tokens = sum(one.shape[0] for one in hidden)
    model_width = hidden[0].shape[1]
    share = model_width // groups
    count = sum(depths)
    grads = jax.ShapeDtypeStruct((slots * slot_len, 2 * channels), BF16)
    dq = jax.ShapeDtypeStruct((peers, both // 2, width), BF16)
    return pl.pallas_call(
        functools.partial(owner_grads_kernel, 2 * columns // both, places),
        out_shape=(
            grads,
            dq,
            *[jax.ShapeDtypeStruct((depth, share, 2 * HD), BF16) for depth in depths],
        ),
        in_specs=[smem(), in_hbm(), whole(), whole(), whole()] + [in_hbm()] * 4,
        out_specs=tuple(in_hbm() for _ in range(2 + len(depths))),
        scratch_shapes=[
            pltpu.VMEM((slots, slot_len, 2 * channels), F32),
            pltpu.VMEM(got.shape, BF16),
            pltpu.VMEM((groups, share, tokens), BF16),
            pltpu.VMEM(grads.shape, BF16),
            pltpu.VMEM(dq.shape, BF16),
            pltpu.VMEM((count, share, 2 * HD), BF16),
            pltpu.VMEM((slots, channels, slot_len), BF16),
            pltpu.VMEM((tokens, 2 * channels), BF16),
            pltpu.VMEM((tokens, model_width), BF16),
            pltpu.SemaphoreType.DMA((4,)),
            pltpu.SemaphoreType.DMA((4, 4)),
            pltpu.SemaphoreType.DMA,
            pltpu.SemaphoreType.DMA((4,)),
            pltpu.SemaphoreType.DMA((count,)),
        ],
        compiler_params=params(VMEM_MOST),
        cost_estimate=cost(16 * 10**9, 24 * 2**20, 2 * 10**6),
        name="owner_grads",
    )(table, got, joint, kv, grads_query, *hidden)


def own_grads_kernel(group, q_ref, g_ref, k_ref, v_ref, joint_ref, grad_ref, dq_ref):
    samples, rows, _ = q_ref.shape
    heads = k_ref.shape[2] // HD
    valid = own_valid(rows, rows, group)
    for sample in range(samples):
        token = slice(sample * rows, (sample + 1) * rows)
        for head in range(heads):
            lanes = slice(head * HD, (head + 1) * HD)
            joint = joint_ref[sample, head : head + 1]
            delta = joint_ref[sample, heads + head : heads + head + 1]
            queries = head_rows(q_ref[sample], head, group)
            grads = head_rows(g_ref[sample], head, group)
            keys = k_ref[sample, :, lanes]
            scores = scores_t(keys, queries, valid)
            prob_grad = lax.dot_general(
                v_ref[sample, :, lanes], grads, NT, preferred_element_type=F32
            )
            probs, dscore = probs_and_dscore(scores, prob_grad, joint, delta)
            key_grad = jnp.dot(dscore, queries, preferred_element_type=F32)
            value_grad = jnp.dot(probs, grads, preferred_element_type=F32)
            key_lanes = slice(2 * head * HD, (2 * head + 1) * HD)
            value_lanes = slice((2 * head + 1) * HD, (2 * head + 2) * HD)
            grad_ref[token, key_lanes] = key_grad.astype(BF16)
            grad_ref[token, value_lanes] = value_grad.astype(BF16)
            dq = lax.dot_general(dscore, keys, TN, preferred_element_type=F32).astype(BF16)
            for r in range(group):
                column = (head * group + r) * HD
                dq_ref[sample, :, column : column + HD] = dq[r * rows : (r + 1) * rows]


def own_grads(question_q, question_grad, keys, values, joint, group):
    samples, rows, width = question_q.shape
    heads = keys.shape[2] // HD
    return pl.pallas_call(
        functools.partial(own_grads_kernel, group),
        out_shape=(
            jax.ShapeDtypeStruct((samples * rows, 2 * heads * HD), BF16),
            jax.ShapeDtypeStruct((samples, rows, width), BF16),
        ),
        in_specs=[whole()] * 5,
        out_specs=(whole(), whole()),
        compiler_params=params(),
        cost_estimate=cost(3 * 10**8, 3 * 2**20, 10**5),
        name="own_grads",
    )(question_q, question_grad, keys, values, joint)


def sum_dq_kernel(heads, owners, *refs):
    out_ref = refs[-1]
    own_ref = refs[-2]
    per = (len(refs) - 2) // heads
    width = refs[0].shape[2]
    for head in range(heads):
        lanes = slice(head * width, (head + 1) * width)
        total = own_ref[0, :, lanes].astype(F32)
        for ref in refs[head * per : (head + 1) * per]:
            total = total + ref[0].astype(F32)
        out_ref[0, :, lanes] = total.astype(BF16)


def sum_dq(table, returned, own):
    samples, rows, width = own.shape
    peers = returned[0].shape[0]
    per = peers // samples
    heads = len(returned)
    first = table.shape[0] - peers

    def from_owner(k):
        return pl.BlockSpec((1, rows, width // heads), lambda s, o: (o[first + s * per + k], 0, 0))

    return pl.pallas_call(
        functools.partial(sum_dq_kernel, heads),
        out_shape=jax.ShapeDtypeStruct((samples, rows, width), BF16),
        grid_spec=pltpu.PrefetchScalarGridSpec(
            num_scalar_prefetch=1,
            grid=(samples,),
            in_specs=[from_owner(k) for k in range(per)] * heads
            + [pl.BlockSpec((1, rows, width), lambda s, o: (s, 0, 0))],
            out_specs=pl.BlockSpec((1, rows, width), lambda s, o: (s, 0, 0)),
        ),
        compiler_params=params(),
        cost_estimate=cost(2 * 10**6, 4 * 2**20),
        name="sum_dq",
    )(table, *[one for one in returned for _ in range(per)], own)


def add_kernel(count, blocks_ref, *refs):
    outs = refs[len(refs) - count :]
    for k, (arrived, out_ref) in enumerate(zip(refs, outs)):
        out_ref[...] = (blocks_ref[k].astype(F32) + arrived[...].astype(F32)).astype(BF16)


def add_arrived(blocks, arrived, after, name):
    count = len(arrived)
    return pl.pallas_call(
        functools.partial(add_kernel, count),
        out_shape=tuple(jax.ShapeDtypeStruct(one.shape, BF16) for one in arrived),
        in_specs=[whole()] * (1 + count) + [pl.BlockSpec(memory_space=pl.ANY)],
        out_specs=(whole(),) * count,
        compiler_params=params(),
        cost_estimate=cost(8 * 10**9, 2**20),
        name=name,
    )(blocks, *arrived, after)


def last_kernel(heads, blocks_ref, *refs):
    out_ref = refs[-1]
    for head in range(heads):
        total = blocks_ref[head].astype(F32)
        for ref in refs[2 * head : 2 * head + 2]:
            total = total + ref[...].astype(F32)
        width = total.shape[1]
        out_ref[:, head * width : (head + 1) * width] = total.astype(BF16)


def last_sums(blocks, arrived):
    heads, share, width = blocks.shape
    return pl.pallas_call(
        functools.partial(last_kernel, heads),
        out_shape=jax.ShapeDtypeStruct((share, heads * width), BF16),
        in_specs=[whole()] * (1 + 2 * heads),
        out_specs=whole(),
        compiler_params=params(),
        cost_estimate=cost(10**6, 2**21),
        name="weights_last",
    )(blocks, *arrived)


def travel(blocks, head):
    count = lax.axis_size("pass")
    ways = [direction(head), -direction(head)]
    return [
        lax.ppermute(block, "pass", [(i, (i + way) % count) for i in range(count)])
        for block, way in zip(blocks, ways)
    ]


def direction(head):
    return 1 if head % 2 == 0 else -1


def finish_kernel(heads, x_ref, out_ref):
    owners, cores, _, _ = x_ref.shape
    for core in range(cores):
        total = x_ref[0, core].astype(F32)
        for owner in range(1, owners):
            total = total + x_ref[owner, core].astype(F32)
        for head in range(heads):
            lanes = slice((core * heads + head) * HD, (core * heads + head + 1) * HD)
            for part in range(2):
                first = (head * 2 + part) * HD
                out_ref[:, part, lanes] = total[:, first : first + HD]


def finish_weights(parts):
    owners, cores, rows, width = parts.shape
    return pl.pallas_call(
        functools.partial(finish_kernel, width // (2 * HD)),
        out_shape=jax.ShapeDtypeStruct((rows, 2, cores * width // 2), F32),
        in_specs=[whole()],
        out_specs=whole(),
        compiler_params=params(),
        cost_estimate=cost(10**6, 2**20),
        name="finish_weights",
    )(parts)


def local(
    question_q,
    question_grad,
    question_kv,
    passage_kv,
    question_hidden,
    passage_hidden,
    reuse,
    passage_blocks,
):
    peers = lax.axis_size("dp")
    groups = lax.axis_size("pass")
    cores = lax.axis_size("tensor")
    slots, slot_len, _, channels = passage_kv.shape
    samples, rows, width = question_q.shape
    heads = channels // HD
    group = width // channels
    refs = reuse.reshape(reuse.shape[0], reuse.shape[2])
    model_width = passage_hidden.shape[2]

    def exchange(x):
        return lax.all_to_all(x, "dp", split_axis=0, concat_axis=0, tiled=True)

    def from_partner(x):
        return lax.ppermute(x, "tensor", [(i, cores - 1 - i) for i in range(cores)])

    kv = jnp.transpose(passage_kv, (2, 0, 1, 3))
    blocks = passage_blocks.reshape(peers, slots)
    packed, table = pack_queries(refs, blocks, question_q, question_grad)
    packed, table, kv = lax.optimization_barrier((packed, table, kv))
    got = exchange(packed)
    got, passage_hidden, question_hidden, question_kv, question_q, question_grad = (
        lax.optimization_barrier(
            (got, passage_hidden, question_hidden, question_kv, question_q, question_grad)
        )
    )
    own_keys, own_values = question_kv[:, :, 0], question_kv[:, :, 1]

    parts = owner_stats(table, got, kv, group)
    parts, own_keys, own_values, passage_hidden, question_hidden = lax.optimization_barrier(
        (parts, own_keys, own_values, passage_hidden, question_hidden)
    )
    stats = exchange(parts)
    own = own_stats(question_q, question_grad, own_keys, own_values, group)
    hidden = [
        one.reshape(-1, model_width)
        for both in (passage_hidden, question_hidden)
        for one in (both, from_partner(both))
    ]

    stats, *hidden = lax.optimization_barrier((stats, *hidden))
    back, merged = merge(refs, stats, own, slots)
    joint = exchange(back)
    grads_query, own_dq = own_grads(
        question_q, question_grad, own_keys, own_values, merged, group
    )
    joint, grads_query, own_dq = lax.optimization_barrier((joint, grads_query, own_dq))
    far = groups // 2
    depths, homes = [], {}

    def array_of(*blocks):
        for row, block in enumerate(blocks):
            homes[block] = (len(depths), row)
        depths.append(len(blocks))
        return len(depths) - 1

    firsts, pairs = [], {}
    for head in range(heads):
        way = direction(head)
        firsts.append((array_of((far, head)), array_of((way * (1 - far), head))))
    for distance in range(far - 1, 0, -1):
        for head in range(heads):
            way = direction(head)
            pair = [(way * distance, head), (way * (1 - distance), head)]
            pairs[distance, head] = array_of(*(pair if distance > 1 else pair[:1]))
    final = array_of(*[(0, head) for head in range(heads)])
    places = [
        (place, [(head, *home) for (one, head), home in homes.items() if one == place])
        for place in [far, *range(far - 1, -far, -1)]
    ]
    grads_pass, dq_parts, *blocks = owner_grads(
        places, depths, table, got, joint, kv, hidden, grads_query, groups
    )
    sums = [
        travel([blocks[ahead][0], blocks[behind][0]], head)
        for head, (ahead, behind) in enumerate(firsts)
    ]
    ends = [None] * heads
    after = grads_pass
    for distance in range(far - 1, 0, -1):
        for head in range(heads):
            arrived = sums[head]
            if distance == 1:
                ends[head] = arrived[1]
                arrived = arrived[:1]
            added = add_arrived(
                blocks[pairs[distance, head]], arrived, after, f"add_{head}_{distance}"
            )
            after = added[0]
            sums[head] = travel(added, head)
    returned = exchange(dq_parts)
    summed = last_sums(
        blocks[final], [one for head in range(heads) for one in (sums[head][0], ends[head])]
    )
    summed, returned = lax.optimization_barrier((summed, returned))
    question_dq = sum_dq(table, [returned], own_dq)

    share = summed.shape[0] // (peers * cores)
    parts = lax.all_to_all(
        summed.reshape(peers * cores, share, -1),
        ("dp", "tensor"),
        split_axis=0,
        concat_axis=0,
        tiled=True,
    )
    weight_grad = finish_weights(parts.reshape(peers, cores, share, -1))
    question_dkv = jnp.swapaxes(grads_query.reshape(samples, rows, heads, 2, HD), 2, 3)
    question_dkv = question_dkv.reshape(samples, rows, 2, channels)
    passage_dkv = jnp.swapaxes(grads_pass.reshape(slots, slot_len, heads, 2, HD), 2, 3)
    passage_dkv = passage_dkv.reshape(slots, slot_len, 2, channels)
    return (question_dq, question_dkv, passage_dkv, weight_grad)


def solution(mesh):
    in_specs = (
        P(("dp", "pass"), None, "tensor"),
        P(("dp", "pass"), None, "tensor"),
        P(("dp", "pass"), None, None, "tensor"),
        P(("dp", "pass"), None, None, "tensor"),
        P(("dp", "pass"), "tensor", None),
        P(("dp", "pass"), "tensor", None),
        P(None, "pass", None),
        P(None, "pass", None),
    )
    out_specs = (
        P(("dp", "pass"), None, "tensor"),
        P(("dp", "pass"), None, None, "tensor"),
        P(("dp", "pass"), None, None, "tensor"),
        P(("dp", "pass", "tensor"), None, None),
    )
    return jax.shard_map(local, mesh=mesh, in_specs=in_specs, out_specs=out_specs, check_vma=False)
```

```python
import functools
import math

import jax
import jax.numpy as jnp
from jax import lax
from jax.experimental import pallas as pl
from jax.experimental.pallas import tpu as pltpu
from jax.sharding import PartitionSpec as P

HD = 128
BLOCK = 128
NEG_FILL = -1e30
SCALE = HD ** (-0.5)
SCALE_LOG2 = SCALE * math.log2(math.e)
VMEM_LIMIT = 24 * 1024 * 1024
VMEM_MOST = 60 * 1024 * 1024
NT = (((1,), (1,)), ((), ()))
TN = (((0,), (0,)), ((), ()))
F32 = jnp.float32
BF16 = jnp.bfloat16


def params(limit=VMEM_LIMIT):
    return pltpu.CompilerParams(vmem_limit_bytes=limit)


def whole():
    return pl.BlockSpec(memory_space=pltpu.VMEM)


def smem():
    return pl.BlockSpec(memory_space=pltpu.SMEM)


def in_hbm():
    return pl.BlockSpec(memory_space=pltpu.HBM)


def cost(flops, nbytes, trans=0):
    return pl.CostEstimate(flops=flops, bytes_accessed=nbytes, transcendentals=trans)


def quotient(value, divisor):
    return lax.div(value, jnp.int32(divisor))


def head_rows(block, head, group):
    first = head * group
    return jnp.concatenate(
        [block[:, (first + r) * HD : (first + r + 1) * HD] for r in range(group)], axis=0
    )


def pack_kernel(slots, refs, blocks, q_ref, g_ref, raw_ref, out_ref, table, kv_ref, *scratch):
    held, raw_held, raw_sem, load_sems, sems = scratch
    peers = out_ref.shape[0]
    samples, rows, _ = q_ref.shape
    per = peers // samples
    me = lax.axis_index("dp")
    raw_load = pltpu.make_async_copy(raw_ref, raw_held, raw_sem)
    loads = []
    for sample in range(samples):
        pair = []
        for part, src in enumerate((q_ref, g_ref)):
            pair.append(
                pltpu.make_async_copy(
                    src.at[sample],
                    held.at[sample, pl.ds(part * rows, rows)],
                    load_sems.at[sample, part],
                )
            )
            pair[-1].start()
        loads.append(pair)
    raw_load.start()
    copies = []
    for j in range(peers):
        sample = j // per
        if j % per == 0:
            for copy in loads[sample]:
                copy.wait()
        dest = quotient(refs[me, j], slots)
        table[peers + slots + j] = dest
        copy = pltpu.make_async_copy(held.at[sample], out_ref.at[dest], sems.at[j])
        copy.start()
        copies.append(copy)
    raw_load.wait()
    for slot in range(slots):
        table[peers + slot] = blocks[slot]
        for part in range(2):
            kv_ref[part, slot] = raw_held[slot, :, part, :]

    @pl.loop(0, peers)
    def _(reader):
        slot = jnp.int32(0)
        for j in range(peers):
            entry = refs[reader, j]
            mine = quotient(entry, slots) == me
            slot = slot + jnp.where(mine, lax.rem(entry, jnp.int32(slots)), 0)
        table[reader] = slot

    for copy in copies:
        copy.wait()


def pack_queries(refs, blocks, question_q, question_grad, passage_kv):
    samples, rows, width = question_q.shape
    peers = refs.shape[0]
    slots, slot_len, _, channels = passage_kv.shape
    return pl.pallas_call(
        functools.partial(pack_kernel, slots),
        out_shape=(
            jax.ShapeDtypeStruct((peers, 2 * rows, width), BF16),
            jax.ShapeDtypeStruct((2 * peers + slots,), jnp.int32),
            jax.ShapeDtypeStruct((2, slots, slot_len, channels), BF16),
        ),
        in_specs=[smem(), smem(), in_hbm(), in_hbm(), in_hbm()],
        out_specs=(in_hbm(), smem(), whole()),
        scratch_shapes=[
            pltpu.VMEM((samples, 2 * rows, width), BF16),
            pltpu.VMEM(passage_kv.shape, BF16),
            pltpu.SemaphoreType.DMA,
            pltpu.SemaphoreType.DMA((samples, 2)),
            pltpu.SemaphoreType.DMA((peers,)),
        ],
        compiler_params=params(VMEM_MOST),
        cost_estimate=cost(0, 6 * 2**20),
        name="pack_queries",
    )(refs, blocks, question_q, question_grad, passage_kv)


def scores_t(keys, queries, valid):
    scores = lax.dot_general(keys, queries, NT, preferred_element_type=F32) * SCALE_LOG2
    return jnp.where(valid, scores, NEG_FILL)


def part_stats(scores, prob_grad):
    top = jnp.max(scores, axis=0, keepdims=True)
    shifted = jnp.exp2(scores - top)
    total = jnp.sum(shifted, axis=0, keepdims=True)
    weighted = jnp.sum(shifted * prob_grad, axis=0, keepdims=True)
    return top + jnp.log2(total), weighted / total


def passage_valid(blocks, slot_len, columns):
    shape = (slot_len, columns)
    return lax.broadcasted_iota(jnp.int32, shape, 0) < blocks * BLOCK


def load_groups(src, held, sems):
    count = sems.shape[0]
    per = src.shape[0] // count
    return [
        pltpu.make_async_copy(
            src.at[pl.ds(i * per, per)], held.at[pl.ds(i * per, per)], sems.at[i]
        )
        for i in range(count)
    ]


def wait_group(i, src, held, sems):
    per = src.shape[0] // sems.shape[0]
    rows = pl.ds(i * per, per)
    pltpu.make_async_copy(src.at[rows], held.at[rows], sems.at[i]).wait()


def owner_stats_kernel(group, table, got_hbm, kv_ref, out_ref, got_ref, sems):
    peers, both, _ = got_ref.shape
    steps = sems.shape[0]
    per = peers // steps
    rows = both // 2
    slot_len = kv_ref.shape[2]
    heads = kv_ref.shape[3] // HD
    columns = group * rows
    for load in load_groups(got_hbm, got_ref, sems):
        load.start()

    @pl.loop(0, steps)
    def _(step):
        wait_group(step, got_hbm, got_ref, sems)
        for one in range(per):
            reader = step * per + one
            slot = table[reader]
            valid = passage_valid(table[peers + slot], slot_len, columns)
            logs, deltas = [], []
            for head in range(heads):
                lanes = slice(head * HD, (head + 1) * HD)
                queries = head_rows(got_ref[reader, :rows], head, group)
                grads = head_rows(got_ref[reader, rows:], head, group)
                scores = scores_t(kv_ref[0, slot, :, lanes], queries, valid)
                prob_grad = lax.dot_general(
                    kv_ref[1, slot, :, lanes], grads, NT, preferred_element_type=F32
                )
                log, delta = part_stats(scores, prob_grad)
                logs.append(log)
                deltas.append(delta)
            out_ref[reader] = jnp.concatenate(logs + deltas, axis=0)


def owner_stats(table, got, kv, group):
    peers, both, width = got.shape
    heads = kv.shape[3] // HD
    columns = group * both // 2
    return pl.pallas_call(
        functools.partial(owner_stats_kernel, group),
        out_shape=jax.ShapeDtypeStruct((peers, 2 * heads, columns), F32),
        in_specs=[smem(), in_hbm(), whole()],
        out_specs=whole(),
        scratch_shapes=[pltpu.VMEM(got.shape, BF16), pltpu.SemaphoreType.DMA((4,))],
        compiler_params=params(VMEM_MOST),
        cost_estimate=cost(2 * 10**9, 6 * 2**20, 2 * 10**6),
        name="owner_stats",
    )(table, got, kv)


def own_valid(own_rows, rows, group):
    shape = (own_rows, group * rows)
    key_row = lax.broadcasted_iota(jnp.int32, shape, 0)
    query_row = lax.rem(lax.broadcasted_iota(jnp.int32, shape, 1), jnp.int32(rows))
    return key_row <= query_row


def own_stats_kernel(group, q_ref, g_ref, k_ref, v_ref, out_ref):
    samples, rows, _ = q_ref.shape
    heads = k_ref.shape[2] // HD
    valid = own_valid(rows, rows, group)
    for sample in range(samples):
        logs, deltas = [], []
        for head in range(heads):
            lanes = slice(head * HD, (head + 1) * HD)
            queries = head_rows(q_ref[sample], head, group)
            grads = head_rows(g_ref[sample], head, group)
            scores = scores_t(k_ref[sample, :, lanes], queries, valid)
            prob_grad = lax.dot_general(
                v_ref[sample, :, lanes], grads, NT, preferred_element_type=F32
            )
            log, delta = part_stats(scores, prob_grad)
            logs.append(log)
            deltas.append(delta)
        out_ref[sample] = jnp.concatenate(logs + deltas, axis=0)


def own_stats(question_q, question_grad, keys, values, group):
    samples, rows, _ = question_q.shape
    heads = keys.shape[2] // HD
    return pl.pallas_call(
        functools.partial(own_stats_kernel, group),
        out_shape=jax.ShapeDtypeStruct((samples, 2 * heads, group * rows), F32),
        in_specs=[whole()] * 4,
        out_specs=whole(),
        compiler_params=params(),
        cost_estimate=cost(10**8, 2**20, 10**5),
        name="own_stats",
    )(question_q, question_grad, keys, values)


def merge_kernel(slots, refs, st_ref, own_ref, back_ref, merged_ref):
    samples, stat_rows, _ = own_ref.shape
    heads = stat_rows // 2
    per = st_ref.shape[0] // samples
    me = lax.axis_index("dp")
    for sample in range(samples):
        owners = [quotient(refs[me, sample * per + k], slots) for k in range(per)]
        parts = [own_ref[sample]] + [st_ref[owner] for owner in owners]
        logs = [part[:heads] for part in parts]
        top = functools.reduce(jnp.maximum, logs)
        weights = [jnp.exp2(log - top) for log in logs]
        total = sum(weights)
        delta = sum(weight * part[heads:] for weight, part in zip(weights, parts)) / total
        joint = jnp.concatenate([top + jnp.log2(total), delta], axis=0)
        merged_ref[sample] = joint
        for owner in owners:
            back_ref[owner] = joint


def merge(refs, stats, own, slots):
    return pl.pallas_call(
        functools.partial(merge_kernel, slots),
        out_shape=(
            jax.ShapeDtypeStruct(stats.shape, F32),
            jax.ShapeDtypeStruct(own.shape, F32),
        ),
        in_specs=[smem(), whole(), whole()],
        out_specs=(whole(), whole()),
        compiler_params=params(),
        cost_estimate=cost(10**5, 2**17, 10**4),
        name="merge_stats",
    )(refs, stats, own)


def probs_and_dscore(scores, prob_grad, joint, delta):
    probs = jnp.exp2(scores - joint)
    dscore = (probs * (prob_grad - delta) * SCALE).astype(BF16)
    return probs.astype(BF16), dscore


def owner_grads_kernel(
    group,
    places,
    table,
    got_hbm,
    joint_ref,
    kv_ref,
    own_ref,
    mine_pass,
    other_pass,
    mine_query,
    other_query,
    grad_out,
    dq_out,
    *rest,
):
    outs = rest[:-14]
    acc_ref, got_ref, h_ref, grad_ref, dq_ref, block_ref, turned_ref, mixed_ref = rest[-14:-6]
    plain_ref = rest[-6]
    got_sems, h_sem, grad_sem, dq_sems, sems = rest[-5:]
    peers, both, _ = got_ref.shape
    steps = got_sems.shape[0]
    per = peers // steps
    rows = both // 2
    slot_len = kv_ref.shape[2]
    heads = kv_ref.shape[3] // HD
    for load in load_groups(got_hbm, got_ref, got_sems):
        load.start()
    groups, share, _ = h_ref.shape
    tile = groups * share // peers
    part = share // peers

    def hidden_loads(step):
        lanes = pl.ds(pl.multiple_of(step * per * tile, per * tile), per * tile)
        loads, row = [], 0
        for k, src in enumerate((mine_pass, other_pass, mine_query, other_query)):
            rows_here = pl.ds(row, src.shape[0])
            loads.append(
                pltpu.make_async_copy(
                    src.at[:, lanes], plain_ref.at[rows_here, lanes], h_sem.at[step, k]
                )
            )
            row += src.shape[0]
        return loads

    for step in range(steps):
        for load in hidden_loads(step):
            load.start()
    acc_ref[...] = jnp.zeros_like(acc_ref)
    for slot in range(turned_ref.shape[0]):
        turned_ref[slot] = kv_ref[0, slot].T

    @pl.loop(0, steps)
    def _(step):
        wait_group(step, got_hbm, got_ref, got_sems)
        for load in hidden_loads(step):
            load.wait()
        for one in range(per):
            reader = step * per + one
            first = pl.multiple_of(reader * tile, tile)
            turned = plain_ref[:, pl.ds(first, tile)].T
            for k in range(groups):
                place = pl.ds(pl.multiple_of(reader * part, part), part)
                h_ref[k, place] = turned[k * part : (k + 1) * part]
            slot = table[reader]
            valid = passage_valid(table[peers + slot], slot_len, group * rows)
            for head in range(heads):
                lanes = slice(head * HD, (head + 1) * HD)
                key_lanes = slice(2 * head * HD, (2 * head + 1) * HD)
                value_lanes = slice((2 * head + 1) * HD, (2 * head + 2) * HD)
                queries = head_rows(got_ref[reader, :rows], head, group)
                grads = head_rows(got_ref[reader, rows:], head, group)
                scores = scores_t(kv_ref[0, slot, :, lanes], queries, valid)
                prob_grad = lax.dot_general(
                    kv_ref[1, slot, :, lanes], grads, NT, preferred_element_type=F32
                )
                joint = joint_ref[reader, head : head + 1]
                delta = joint_ref[reader, heads + head : heads + head + 1]
                probs, dscore = probs_and_dscore(scores, prob_grad, joint, delta)
                acc_ref[slot, :, key_lanes] += jnp.dot(
                    dscore, queries, preferred_element_type=F32
                )
                acc_ref[slot, :, value_lanes] += jnp.dot(
                    probs, grads, preferred_element_type=F32
                )
                dq = jnp.dot(turned_ref[slot, lanes], dscore, preferred_element_type=F32)
                dq = dq.astype(BF16).T
                for r in range(group):
                    column = (head * group + r) * HD
                    dq_ref[reader, :, column : column + HD] = dq[r * rows : (r + 1) * rows]
        done = pl.ds(step * per, per)
        pltpu.make_async_copy(dq_ref.at[done], dq_out.at[done], dq_sems.at[step]).start()

    for one in range(acc_ref.shape[0]):
        grad_ref[one * slot_len : (one + 1) * slot_len] = acc_ref[one].astype(BF16)
    copies = [pltpu.make_async_copy(grad_ref, grad_out, grad_sem)]
    copies[0].start()
    count = h_ref.shape[0]
    mix_tokens(grad_ref, mixed_ref, 0, acc_ref.shape[0])
    mix_tokens(own_ref, mixed_ref, grad_ref.shape[0], own_ref.shape[0] // rows)
    k = 0
    for place, uses in places:
        pass_group = lax.rem(lax.axis_index("pass") + (place + count), count)
        total = jnp.dot(h_ref[pass_group], mixed_ref[...], preferred_element_type=F32)
        for head, out, row in uses:
            lanes = slice(2 * head * HD, 2 * (head + 1) * HD)
            block_ref[k] = total[:, lanes].astype(BF16)
            copies.append(
                pltpu.make_async_copy(block_ref.at[k], outs[out].at[row], sems.at[k])
            )
            copies[-1].start()
            k += 1
    for copy in copies:
        copy.wait()
    for step in range(steps):
        wait_group(step, dq_ref, dq_out, dq_sems)


def mix_tokens(src, out_ref, start, pieces):
    half = src.shape[0] // pieces // 2
    core = lax.axis_index("tensor")
    for k, side in enumerate((core, 1 - core)):
        for piece in range(pieces):
            first = pl.multiple_of((2 * piece + side) * half, half)
            row = start + (k * pieces + piece) * half
            out_ref[row : row + half] = src[pl.ds(first, half)]


def owner_grads(places, depths, table, got, joint, kv, hidden, grads_query, groups):
    peers, both, width = got.shape
    _, slots, slot_len, channels = kv.shape
    columns = joint.shape[2]
    tokens = sum(one.shape[0] for one in hidden)
    model_width = hidden[0].shape[1]
    share = model_width // groups
    count = sum(depths)
    grads = jax.ShapeDtypeStruct((slots * slot_len, 2 * channels), BF16)
    dq = jax.ShapeDtypeStruct((peers, both // 2, width), BF16)
    return pl.pallas_call(
        functools.partial(owner_grads_kernel, 2 * columns // both, places),
        out_shape=(
            grads,
            dq,
            *[jax.ShapeDtypeStruct((depth, share, 2 * HD), BF16) for depth in depths],
        ),
        in_specs=[smem(), in_hbm(), whole(), whole(), whole()] + [in_hbm()] * 4,
        out_specs=tuple(in_hbm() for _ in range(2 + len(depths))),
        scratch_shapes=[
            pltpu.VMEM((slots, slot_len, 2 * channels), F32),
            pltpu.VMEM(got.shape, BF16),
            pltpu.VMEM((groups, share, tokens), BF16),
            pltpu.VMEM(grads.shape, BF16),
            pltpu.VMEM(dq.shape, BF16),
            pltpu.VMEM((count, share, 2 * HD), BF16),
            pltpu.VMEM((slots, channels, slot_len), BF16),
            pltpu.VMEM((tokens, 2 * channels), BF16),
            pltpu.VMEM((tokens, model_width), BF16),
            pltpu.SemaphoreType.DMA((4,)),
            pltpu.SemaphoreType.DMA((4, 4)),
            pltpu.SemaphoreType.DMA,
            pltpu.SemaphoreType.DMA((4,)),
            pltpu.SemaphoreType.DMA((count,)),
        ],
        compiler_params=params(VMEM_MOST),
        cost_estimate=cost(16 * 10**9, 24 * 2**20, 2 * 10**6),
        name="owner_grads",
    )(table, got, joint, kv, grads_query, *hidden)


def own_grads_kernel(group, q_ref, g_ref, k_ref, v_ref, joint_ref, grad_ref, dq_ref):
    samples, rows, _ = q_ref.shape
    heads = k_ref.shape[2] // HD
    valid = own_valid(rows, rows, group)
    for sample in range(samples):
        token = slice(sample * rows, (sample + 1) * rows)
        for head in range(heads):
            lanes = slice(head * HD, (head + 1) * HD)
            joint = joint_ref[sample, head : head + 1]
            delta = joint_ref[sample, heads + head : heads + head + 1]
            queries = head_rows(q_ref[sample], head, group)
            grads = head_rows(g_ref[sample], head, group)
            keys = k_ref[sample, :, lanes]
            scores = scores_t(keys, queries, valid)
            prob_grad = lax.dot_general(
                v_ref[sample, :, lanes], grads, NT, preferred_element_type=F32
            )
            probs, dscore = probs_and_dscore(scores, prob_grad, joint, delta)
            key_grad = jnp.dot(dscore, queries, preferred_element_type=F32)
            value_grad = jnp.dot(probs, grads, preferred_element_type=F32)
            key_lanes = slice(2 * head * HD, (2 * head + 1) * HD)
            value_lanes = slice((2 * head + 1) * HD, (2 * head + 2) * HD)
            grad_ref[token, key_lanes] = key_grad.astype(BF16)
            grad_ref[token, value_lanes] = value_grad.astype(BF16)
            dq = lax.dot_general(dscore, keys, TN, preferred_element_type=F32).astype(BF16)
            for r in range(group):
                column = (head * group + r) * HD
                dq_ref[sample, :, column : column + HD] = dq[r * rows : (r + 1) * rows]


def own_grads(question_q, question_grad, keys, values, joint, group):
    samples, rows, width = question_q.shape
    heads = keys.shape[2] // HD
    return pl.pallas_call(
        functools.partial(own_grads_kernel, group),
        out_shape=(
            jax.ShapeDtypeStruct((samples * rows, 2 * heads * HD), BF16),
            jax.ShapeDtypeStruct((samples, rows, width), BF16),
        ),
        in_specs=[whole()] * 5,
        out_specs=(whole(), whole()),
        compiler_params=params(),
        cost_estimate=cost(3 * 10**8, 3 * 2**20, 10**5),
        name="own_grads",
    )(question_q, question_grad, keys, values, joint)


def sum_dq_kernel(heads, owners, *refs):
    out_ref = refs[-1]
    own_ref = refs[-2]
    per = (len(refs) - 2) // heads
    width = refs[0].shape[2]
    for head in range(heads):
        lanes = slice(head * width, (head + 1) * width)
        total = own_ref[0, :, lanes].astype(F32)
        for ref in refs[head * per : (head + 1) * per]:
            total = total + ref[0].astype(F32)
        out_ref[0, :, lanes] = total.astype(BF16)


def sum_dq(table, returned, own):
    samples, rows, width = own.shape
    peers = returned[0].shape[0]
    per = peers // samples
    heads = len(returned)
    first = table.shape[0] - peers

    def from_owner(k):
        return pl.BlockSpec((1, rows, width // heads), lambda s, o: (o[first + s * per + k], 0, 0))

    return pl.pallas_call(
        functools.partial(sum_dq_kernel, heads),
        out_shape=jax.ShapeDtypeStruct((samples, rows, width), BF16),
        grid_spec=pltpu.PrefetchScalarGridSpec(
            num_scalar_prefetch=1,
            grid=(samples,),
            in_specs=[from_owner(k) for k in range(per)] * heads
            + [pl.BlockSpec((1, rows, width), lambda s, o: (s, 0, 0))],
            out_specs=pl.BlockSpec((1, rows, width), lambda s, o: (s, 0, 0)),
        ),
        compiler_params=params(),
        cost_estimate=cost(2 * 10**6, 4 * 2**20),
        name="sum_dq",
    )(table, *[one for one in returned for _ in range(per)], own)


def add_kernel(count, blocks_ref, *refs):
    outs = refs[len(refs) - count :]
    for k, (arrived, out_ref) in enumerate(zip(refs, outs)):
        out_ref[...] = (blocks_ref[k].astype(F32) + arrived[...].astype(F32)).astype(BF16)


def add_arrived(blocks, arrived, after, name):
    count = len(arrived)
    return pl.pallas_call(
        functools.partial(add_kernel, count),
        out_shape=tuple(jax.ShapeDtypeStruct(one.shape, BF16) for one in arrived),
        in_specs=[whole()] * (1 + count) + [pl.BlockSpec(memory_space=pl.ANY)],
        out_specs=(whole(),) * count,
        compiler_params=params(),
        cost_estimate=cost(8 * 10**9, 2**20),
        name=name,
    )(blocks, *arrived, after)


def last_kernel(heads, blocks_ref, *refs):
    out_ref = refs[-1]
    for head in range(heads):
        total = blocks_ref[head].astype(F32)
        for ref in refs[2 * head : 2 * head + 2]:
            total = total + ref[...].astype(F32)
        width = total.shape[1]
        out_ref[:, head * width : (head + 1) * width] = total.astype(BF16)


def last_sums(blocks, arrived):
    heads, share, width = blocks.shape
    return pl.pallas_call(
        functools.partial(last_kernel, heads),
        out_shape=jax.ShapeDtypeStruct((share, heads * width), BF16),
        in_specs=[whole()] * (1 + 2 * heads),
        out_specs=whole(),
        compiler_params=params(),
        cost_estimate=cost(10**6, 2**21),
        name="weights_last",
    )(blocks, *arrived)


def travel(blocks, head):
    count = lax.axis_size("pass")
    ways = [direction(head), -direction(head)]
    return [
        lax.ppermute(block, "pass", [(i, (i + way) % count) for i in range(count)])
        for block, way in zip(blocks, ways)
    ]


def direction(head):
    return 1 if head % 2 == 0 else -1


def finish_kernel(heads, x_ref, out_ref):
    owners, cores, _, _ = x_ref.shape
    for core in range(cores):
        total = x_ref[0, core].astype(F32)
        for owner in range(1, owners):
            total = total + x_ref[owner, core].astype(F32)
        for head in range(heads):
            lanes = slice((core * heads + head) * HD, (core * heads + head + 1) * HD)
            for part in range(2):
                first = (head * 2 + part) * HD
                out_ref[:, part, lanes] = total[:, first : first + HD]


def finish_weights(parts):
    owners, cores, rows, width = parts.shape
    return pl.pallas_call(
        functools.partial(finish_kernel, width // (2 * HD)),
        out_shape=jax.ShapeDtypeStruct((rows, 2, cores * width // 2), F32),
        in_specs=[whole()],
        out_specs=whole(),
        compiler_params=params(),
        cost_estimate=cost(10**6, 2**20),
        name="finish_weights",
    )(parts)


def local(
    question_q,
    question_grad,
    question_kv,
    passage_kv,
    question_hidden,
    passage_hidden,
    reuse,
    passage_blocks,
):
    peers = lax.axis_size("dp")
    groups = lax.axis_size("pass")
    cores = lax.axis_size("tensor")
    slots, slot_len, _, channels = passage_kv.shape
    samples, rows, width = question_q.shape
    heads = channels // HD
    group = width // channels
    refs = reuse.reshape(reuse.shape[0], reuse.shape[2])
    model_width = passage_hidden.shape[2]

    def exchange(x):
        return lax.all_to_all(x, "dp", split_axis=0, concat_axis=0, tiled=True)

    def from_partner(x):
        return lax.ppermute(x, "tensor", [(i, cores - 1 - i) for i in range(cores)])

    me = lax.axis_index("dp")
    blocks = lax.dynamic_index_in_dim(passage_blocks, me, 0, keepdims=False).reshape(slots)
    packed, table, kv = pack_queries(refs, blocks, question_q, question_grad, passage_kv)
    packed, table, kv = lax.optimization_barrier((packed, table, kv))
    got = exchange(packed)
    got, passage_hidden, question_hidden, question_kv, question_q, question_grad = (
        lax.optimization_barrier(
            (got, passage_hidden, question_hidden, question_kv, question_q, question_grad)
        )
    )
    own_keys, own_values = question_kv[:, :, 0], question_kv[:, :, 1]

    parts = owner_stats(table, got, kv, group)
    parts, own_keys, own_values, passage_hidden, question_hidden = lax.optimization_barrier(
        (parts, own_keys, own_values, passage_hidden, question_hidden)
    )
    stats = exchange(parts)
    own = own_stats(question_q, question_grad, own_keys, own_values, group)
    hidden = [
        one.reshape(-1, model_width)
        for both in (passage_hidden, question_hidden)
        for one in (both, from_partner(both))
    ]

    stats, *hidden = lax.optimization_barrier((stats, *hidden))
    back, merged = merge(refs, stats, own, slots)
    joint = exchange(back)
    grads_query, own_dq = own_grads(
        question_q, question_grad, own_keys, own_values, merged, group
    )
    joint, grads_query, own_dq = lax.optimization_barrier((joint, grads_query, own_dq))
    far = groups // 2
    depths, homes = [], {}

    def array_of(*blocks):
        for row, block in enumerate(blocks):
            homes[block] = (len(depths), row)
        depths.append(len(blocks))
        return len(depths) - 1

    firsts, pairs = [], {}
    for head in range(heads):
        way = direction(head)
        firsts.append((array_of((far, head)), array_of((way * (1 - far), head))))
    for distance in range(far - 1, 0, -1):
        for head in range(heads):
            way = direction(head)
            pair = [(way * distance, head), (way * (1 - distance), head)]
            pairs[distance, head] = array_of(*(pair if distance > 1 else pair[:1]))
    final = array_of(*[(0, head) for head in range(heads)])
    places = [
        (place, [(head, *home) for (one, head), home in homes.items() if one == place])
        for place in [far, *range(far - 1, -far, -1)]
    ]
    grads_pass, dq_parts, *blocks = owner_grads(
        places, depths, table, got, joint, kv, hidden, grads_query, groups
    )
    sums = [
        travel([blocks[ahead][0], blocks[behind][0]], head)
        for head, (ahead, behind) in enumerate(firsts)
    ]
    ends = [None] * heads
    after = grads_pass
    for distance in range(far - 1, 0, -1):
        for head in range(heads):
            arrived = sums[head]
            if distance == 1:
                ends[head] = arrived[1]
                arrived = arrived[:1]
            added = add_arrived(
                blocks[pairs[distance, head]], arrived, after, f"add_{head}_{distance}"
            )
            after = added[0]
            sums[head] = travel(added, head)
    returned = exchange(dq_parts)
    summed = last_sums(
        blocks[final], [one for head in range(heads) for one in (sums[head][0], ends[head])]
    )
    summed, returned = lax.optimization_barrier((summed, returned))
    question_dq = sum_dq(table, [returned], own_dq)

    share = summed.shape[0] // (peers * cores)
    parts = lax.all_to_all(
        summed.reshape(peers * cores, share, -1),
        ("dp", "tensor"),
        split_axis=0,
        concat_axis=0,
        tiled=True,
    )
    weight_grad = finish_weights(parts.reshape(peers, cores, share, -1))
    question_dkv = jnp.swapaxes(grads_query.reshape(samples, rows, heads, 2, HD), 2, 3)
    question_dkv = question_dkv.reshape(samples, rows, 2, channels)
    passage_dkv = jnp.swapaxes(grads_pass.reshape(slots, slot_len, heads, 2, HD), 2, 3)
    passage_dkv = passage_dkv.reshape(slots, slot_len, 2, channels)
    return (question_dq, question_dkv, passage_dkv, weight_grad)


def solution(mesh):
    in_specs = (
        P(("dp", "pass"), None, "tensor"),
        P(("dp", "pass"), None, "tensor"),
        P(("dp", "pass"), None, None, "tensor"),
        P(("dp", "pass"), None, None, "tensor"),
        P(("dp", "pass"), "tensor", None),
        P(("dp", "pass"), "tensor", None),
        P(None, "pass", None),
        P(None, "pass", None),
    )
    out_specs = (
        P(("dp", "pass"), None, "tensor"),
        P(("dp", "pass"), None, None, "tensor"),
        P(("dp", "pass"), None, None, "tensor"),
        P(("dp", "pass", "tensor"), None, None),
    )
    return jax.shard_map(local, mesh=mesh, in_specs=in_specs, out_specs=out_specs, check_vma=False)
```

```python
import functools
import math

import jax
import jax.numpy as jnp
from jax import lax
from jax.experimental import pallas as pl
from jax.experimental.pallas import tpu as pltpu
from jax.sharding import PartitionSpec as P

HD = 128
BLOCK = 128
NEG_FILL = -1e30
SCALE = HD ** (-0.5)
SCALE_LOG2 = SCALE * math.log2(math.e)
VMEM_LIMIT = 24 * 1024 * 1024
VMEM_MOST = 60 * 1024 * 1024
NT = (((1,), (1,)), ((), ()))
TN = (((0,), (0,)), ((), ()))
F32 = jnp.float32
BF16 = jnp.bfloat16


def params(limit=VMEM_LIMIT):
    return pltpu.CompilerParams(vmem_limit_bytes=limit)


def whole():
    return pl.BlockSpec(memory_space=pltpu.VMEM)


def smem():
    return pl.BlockSpec(memory_space=pltpu.SMEM)


def in_hbm():
    return pl.BlockSpec(memory_space=pltpu.HBM)


def cost(flops, nbytes, trans=0):
    return pl.CostEstimate(flops=flops, bytes_accessed=nbytes, transcendentals=trans)


def quotient(value, divisor):
    return lax.div(value, jnp.int32(divisor))


def head_rows(block, head, group):
    first = head * group
    return jnp.concatenate(
        [block[:, (first + r) * HD : (first + r + 1) * HD] for r in range(group)], axis=0
    )


def pack_kernel(slots, refs, blocks, q_ref, g_ref, raw_ref, out_ref, table, kv_ref, *scratch):
    held, raw_held, raw_sem, load_sems, sems = scratch
    peers = out_ref.shape[0]
    samples, rows, _ = q_ref.shape
    per = peers // samples
    me = lax.axis_index("dp")
    raw_load = pltpu.make_async_copy(raw_ref, raw_held, raw_sem)
    loads = []
    for sample in range(samples):
        pair = []
        for part, src in enumerate((q_ref, g_ref)):
            pair.append(
                pltpu.make_async_copy(
                    src.at[sample],
                    held.at[sample, pl.ds(part * rows, rows)],
                    load_sems.at[sample, part],
                )
            )
            pair[-1].start()
        loads.append(pair)
    raw_load.start()
    copies = []
    for j in range(peers):
        sample = j // per
        if j % per == 0:
            for copy in loads[sample]:
                copy.wait()
        dest = quotient(refs[me, j], slots)
        table[peers + slots + j] = dest
        copy = pltpu.make_async_copy(held.at[sample], out_ref.at[dest], sems.at[j])
        copy.start()
        copies.append(copy)
    raw_load.wait()
    for slot in range(slots):
        table[peers + slot] = blocks[slot]
        for part in range(2):
            kv_ref[part, slot] = raw_held[slot, :, part, :]

    @pl.loop(0, peers)
    def _(reader):
        slot = jnp.int32(0)
        for j in range(peers):
            entry = refs[reader, j]
            mine = quotient(entry, slots) == me
            slot = slot + jnp.where(mine, lax.rem(entry, jnp.int32(slots)), 0)
        table[reader] = slot

    for copy in copies:
        copy.wait()


def pack_queries(refs, blocks, question_q, question_grad, passage_kv):
    samples, rows, width = question_q.shape
    peers = refs.shape[0]
    slots, slot_len, _, channels = passage_kv.shape
    return pl.pallas_call(
        functools.partial(pack_kernel, slots),
        out_shape=(
            jax.ShapeDtypeStruct((peers, 2 * rows, width), BF16),
            jax.ShapeDtypeStruct((2 * peers + slots,), jnp.int32),
            jax.ShapeDtypeStruct((2, slots, slot_len, channels), BF16),
        ),
        in_specs=[smem(), smem(), in_hbm(), in_hbm(), in_hbm()],
        out_specs=(in_hbm(), smem(), whole()),
        scratch_shapes=[
            pltpu.VMEM((samples, 2 * rows, width), BF16),
            pltpu.VMEM(passage_kv.shape, BF16),
            pltpu.SemaphoreType.DMA,
            pltpu.SemaphoreType.DMA((samples, 2)),
            pltpu.SemaphoreType.DMA((peers,)),
        ],
        compiler_params=params(VMEM_MOST),
        cost_estimate=cost(0, 6 * 2**20),
        name="pack_queries",
    )(refs, blocks, question_q, question_grad, passage_kv)


def scores_t(keys, queries, valid):
    scores = lax.dot_general(keys, queries, NT, preferred_element_type=F32) * SCALE_LOG2
    return jnp.where(valid, scores, NEG_FILL)


def part_stats(scores, prob_grad):
    top = jnp.max(scores, axis=0, keepdims=True)
    shifted = jnp.exp2(scores - top)
    total = jnp.sum(shifted, axis=0, keepdims=True)
    weighted = jnp.sum(shifted * prob_grad, axis=0, keepdims=True)
    return top + jnp.log2(total), weighted / total


def passage_valid(blocks, slot_len, columns):
    shape = (slot_len, columns)
    return lax.broadcasted_iota(jnp.int32, shape, 0) < blocks * BLOCK


def load_groups(src, held, sems):
    count = sems.shape[0]
    per = src.shape[0] // count
    return [
        pltpu.make_async_copy(
            src.at[pl.ds(i * per, per)], held.at[pl.ds(i * per, per)], sems.at[i]
        )
        for i in range(count)
    ]


def wait_group(i, src, held, sems):
    per = src.shape[0] // sems.shape[0]
    rows = pl.ds(i * per, per)
    pltpu.make_async_copy(src.at[rows], held.at[rows], sems.at[i]).wait()


def owner_stats_kernel(group, table, got_hbm, kv_ref, out_ref, got_ref, sems):
    peers, both, _ = got_ref.shape
    steps = sems.shape[0]
    per = peers // steps
    rows = both // 2
    slot_len = kv_ref.shape[2]
    heads = kv_ref.shape[3] // HD
    columns = group * rows
    for load in load_groups(got_hbm, got_ref, sems):
        load.start()

    @pl.loop(0, steps)
    def _(step):
        wait_group(step, got_hbm, got_ref, sems)
        for one in range(per):
            reader = step * per + one
            slot = table[reader]
            valid = passage_valid(table[peers + slot], slot_len, columns)
            logs, deltas = [], []
            for head in range(heads):
                lanes = slice(head * HD, (head + 1) * HD)
                queries = head_rows(got_ref[reader, :rows], head, group)
                grads = head_rows(got_ref[reader, rows:], head, group)
                scores = scores_t(kv_ref[0, slot, :, lanes], queries, valid)
                prob_grad = lax.dot_general(
                    kv_ref[1, slot, :, lanes], grads, NT, preferred_element_type=F32
                )
                log, delta = part_stats(scores, prob_grad)
                logs.append(log)
                deltas.append(delta)
            out_ref[reader] = jnp.concatenate(logs + deltas, axis=0)


def owner_stats(table, got, kv, group):
    peers, both, width = got.shape
    heads = kv.shape[3] // HD
    columns = group * both // 2
    return pl.pallas_call(
        functools.partial(owner_stats_kernel, group),
        out_shape=jax.ShapeDtypeStruct((peers, 2 * heads, columns), F32),
        in_specs=[smem(), in_hbm(), whole()],
        out_specs=whole(),
        scratch_shapes=[pltpu.VMEM(got.shape, BF16), pltpu.SemaphoreType.DMA((8,))],
        compiler_params=params(VMEM_MOST),
        cost_estimate=cost(2 * 10**9, 6 * 2**20, 2 * 10**6),
        name="owner_stats",
    )(table, got, kv)


def own_valid(own_rows, rows, group):
    shape = (own_rows, group * rows)
    key_row = lax.broadcasted_iota(jnp.int32, shape, 0)
    query_row = lax.rem(lax.broadcasted_iota(jnp.int32, shape, 1), jnp.int32(rows))
    return key_row <= query_row


def own_stats_kernel(group, q_ref, g_ref, k_ref, v_ref, out_ref):
    samples, rows, _ = q_ref.shape
    heads = k_ref.shape[2] // HD
    valid = own_valid(rows, rows, group)
    for sample in range(samples):
        logs, deltas = [], []
        for head in range(heads):
            lanes = slice(head * HD, (head + 1) * HD)
            queries = head_rows(q_ref[sample], head, group)
            grads = head_rows(g_ref[sample], head, group)
            scores = scores_t(k_ref[sample, :, lanes], queries, valid)
            prob_grad = lax.dot_general(
                v_ref[sample, :, lanes], grads, NT, preferred_element_type=F32
            )
            log, delta = part_stats(scores, prob_grad)
            logs.append(log)
            deltas.append(delta)
        out_ref[sample] = jnp.concatenate(logs + deltas, axis=0)


def own_stats(question_q, question_grad, keys, values, group):
    samples, rows, _ = question_q.shape
    heads = keys.shape[2] // HD
    return pl.pallas_call(
        functools.partial(own_stats_kernel, group),
        out_shape=jax.ShapeDtypeStruct((samples, 2 * heads, group * rows), F32),
        in_specs=[whole()] * 4,
        out_specs=whole(),
        compiler_params=params(),
        cost_estimate=cost(10**8, 2**20, 10**5),
        name="own_stats",
    )(question_q, question_grad, keys, values)


def merge_kernel(slots, refs, st_ref, own_ref, back_ref, merged_ref):
    samples, stat_rows, _ = own_ref.shape
    heads = stat_rows // 2
    per = st_ref.shape[0] // samples
    me = lax.axis_index("dp")
    for sample in range(samples):
        owners = [quotient(refs[me, sample * per + k], slots) for k in range(per)]
        parts = [own_ref[sample]] + [st_ref[owner] for owner in owners]
        logs = [part[:heads] for part in parts]
        top = functools.reduce(jnp.maximum, logs)
        weights = [jnp.exp2(log - top) for log in logs]
        total = sum(weights)
        delta = sum(weight * part[heads:] for weight, part in zip(weights, parts)) / total
        joint = jnp.concatenate([top + jnp.log2(total), delta], axis=0)
        merged_ref[sample] = joint
        for owner in owners:
            back_ref[owner] = joint


def merge(refs, stats, own, slots):
    return pl.pallas_call(
        functools.partial(merge_kernel, slots),
        out_shape=(
            jax.ShapeDtypeStruct(stats.shape, F32),
            jax.ShapeDtypeStruct(own.shape, F32),
        ),
        in_specs=[smem(), whole(), whole()],
        out_specs=(whole(), whole()),
        compiler_params=params(),
        cost_estimate=cost(10**5, 2**17, 10**4),
        name="merge_stats",
    )(refs, stats, own)


def probs_and_dscore(scores, prob_grad, joint, delta):
    probs = jnp.exp2(scores - joint)
    dscore = (probs * (prob_grad - delta) * SCALE).astype(BF16)
    return probs.astype(BF16), dscore


def owner_grads_kernel(
    group,
    places,
    table,
    got_hbm,
    joint_ref,
    kv_ref,
    own_ref,
    mine_pass,
    other_pass,
    mine_query,
    other_query,
    grad_out,
    dq_out,
    *rest,
):
    outs = rest[:-14]
    acc_ref, got_ref, h_ref, grad_ref, dq_ref, block_ref, turned_ref, mixed_ref = rest[-14:-6]
    plain_ref = rest[-6]
    got_sems, h_sem, grad_sem, dq_sems, sems = rest[-5:]
    peers, both, _ = got_ref.shape
    steps = got_sems.shape[0]
    per = peers // steps
    rows = both // 2
    slot_len = kv_ref.shape[2]
    heads = kv_ref.shape[3] // HD
    for load in load_groups(got_hbm, got_ref, got_sems):
        load.start()
    groups, share, _ = h_ref.shape
    tile = groups * share // peers
    part = share // peers

    def hidden_loads(step):
        lanes = pl.ds(pl.multiple_of(step * per * tile, per * tile), per * tile)
        loads, row = [], 0
        for k, src in enumerate((mine_pass, other_pass, mine_query, other_query)):
            rows_here = pl.ds(row, src.shape[0])
            loads.append(
                pltpu.make_async_copy(
                    src.at[:, lanes], plain_ref.at[rows_here, lanes], h_sem.at[step, k]
                )
            )
            row += src.shape[0]
        return loads

    for step in range(steps):
        for load in hidden_loads(step):
            load.start()
    acc_ref[...] = jnp.zeros_like(acc_ref)
    for slot in range(turned_ref.shape[0]):
        turned_ref[slot] = kv_ref[0, slot].T

    @pl.loop(0, steps)
    def _(step):
        wait_group(step, got_hbm, got_ref, got_sems)
        for load in hidden_loads(step):
            load.wait()
        for one in range(per):
            reader = step * per + one
            first = pl.multiple_of(reader * tile, tile)
            turned = plain_ref[:, pl.ds(first, tile)].T
            for k in range(groups):
                place = pl.ds(pl.multiple_of(reader * part, part), part)
                h_ref[k, place] = turned[k * part : (k + 1) * part]
            slot = table[reader]
            valid = passage_valid(table[peers + slot], slot_len, group * rows)
            for head in range(heads):
                lanes = slice(head * HD, (head + 1) * HD)
                key_lanes = slice(2 * head * HD, (2 * head + 1) * HD)
                value_lanes = slice((2 * head + 1) * HD, (2 * head + 2) * HD)
                queries = head_rows(got_ref[reader, :rows], head, group)
                grads = head_rows(got_ref[reader, rows:], head, group)
                scores = scores_t(kv_ref[0, slot, :, lanes], queries, valid)
                prob_grad = lax.dot_general(
                    kv_ref[1, slot, :, lanes], grads, NT, preferred_element_type=F32
                )
                joint = joint_ref[reader, head : head + 1]
                delta = joint_ref[reader, heads + head : heads + head + 1]
                probs, dscore = probs_and_dscore(scores, prob_grad, joint, delta)
                acc_ref[slot, :, key_lanes] += jnp.dot(
                    dscore, queries, preferred_element_type=F32
                )
                acc_ref[slot, :, value_lanes] += jnp.dot(
                    probs, grads, preferred_element_type=F32
                )
                dq = jnp.dot(turned_ref[slot, lanes], dscore, preferred_element_type=F32)
                dq = dq.astype(BF16).T
                for r in range(group):
                    column = (head * group + r) * HD
                    dq_ref[reader, :, column : column + HD] = dq[r * rows : (r + 1) * rows]
        done = pl.ds(step * per, per)
        pltpu.make_async_copy(dq_ref.at[done], dq_out.at[done], dq_sems.at[step]).start()

    for one in range(acc_ref.shape[0]):
        grad_ref[one * slot_len : (one + 1) * slot_len] = acc_ref[one].astype(BF16)
    copies = [pltpu.make_async_copy(grad_ref, grad_out, grad_sem)]
    copies[0].start()
    count = h_ref.shape[0]
    mix_tokens(grad_ref, mixed_ref, 0, acc_ref.shape[0])
    mix_tokens(own_ref, mixed_ref, grad_ref.shape[0], own_ref.shape[0] // rows)
    k = 0
    for place, uses in places:
        pass_group = lax.rem(lax.axis_index("pass") + (place + count), count)
        total = jnp.dot(h_ref[pass_group], mixed_ref[...], preferred_element_type=F32)
        for head, out, row in uses:
            lanes = slice(2 * head * HD, 2 * (head + 1) * HD)
            block_ref[k] = total[:, lanes].astype(BF16)
            copies.append(
                pltpu.make_async_copy(block_ref.at[k], outs[out].at[row], sems.at[k])
            )
            copies[-1].start()
            k += 1
    for copy in copies:
        copy.wait()
    for step in range(steps):
        wait_group(step, dq_ref, dq_out, dq_sems)


def mix_tokens(src, out_ref, start, pieces):
    half = src.shape[0] // pieces // 2
    core = lax.axis_index("tensor")
    for k, side in enumerate((core, 1 - core)):
        for piece in range(pieces):
            first = pl.multiple_of((2 * piece + side) * half, half)
            row = start + (k * pieces + piece) * half
            out_ref[row : row + half] = src[pl.ds(first, half)]


def owner_grads(places, depths, table, got, joint, kv, hidden, grads_query, groups):
    peers, both, width = got.shape
    _, slots, slot_len, channels = kv.shape
    columns = joint.shape[2]
    tokens = sum(one.shape[0] for one in hidden)
    model_width = hidden[0].shape[1]
    share = model_width // groups
    count = sum(depths)
    grads = jax.ShapeDtypeStruct((slots * slot_len, 2 * channels), BF16)
    dq = jax.ShapeDtypeStruct((peers, both // 2, width), BF16)
    return pl.pallas_call(
        functools.partial(owner_grads_kernel, 2 * columns // both, places),
        out_shape=(
            grads,
            dq,
            *[jax.ShapeDtypeStruct((depth, share, 2 * HD), BF16) for depth in depths],
        ),
        in_specs=[smem(), in_hbm(), whole(), whole(), whole()] + [in_hbm()] * 4,
        out_specs=tuple(in_hbm() for _ in range(2 + len(depths))),
        scratch_shapes=[
            pltpu.VMEM((slots, slot_len, 2 * channels), F32),
            pltpu.VMEM(got.shape, BF16),
            pltpu.VMEM((groups, share, tokens), BF16),
            pltpu.VMEM(grads.shape, BF16),
            pltpu.VMEM(dq.shape, BF16),
            pltpu.VMEM((count, share, 2 * HD), BF16),
            pltpu.VMEM((slots, channels, slot_len), BF16),
            pltpu.VMEM((tokens, 2 * channels), BF16),
            pltpu.VMEM((tokens, model_width), BF16),
            pltpu.SemaphoreType.DMA((4,)),
            pltpu.SemaphoreType.DMA((4, 4)),
            pltpu.SemaphoreType.DMA,
            pltpu.SemaphoreType.DMA((4,)),
            pltpu.SemaphoreType.DMA((count,)),
        ],
        compiler_params=params(VMEM_MOST),
        cost_estimate=cost(16 * 10**9, 24 * 2**20, 2 * 10**6),
        name="owner_grads",
    )(table, got, joint, kv, grads_query, *hidden)


def own_grads_kernel(group, q_ref, g_ref, k_ref, v_ref, joint_ref, grad_ref, dq_ref):
    samples, rows, _ = q_ref.shape
    heads = k_ref.shape[2] // HD
    valid = own_valid(rows, rows, group)
    for sample in range(samples):
        token = slice(sample * rows, (sample + 1) * rows)
        for head in range(heads):
            lanes = slice(head * HD, (head + 1) * HD)
            joint = joint_ref[sample, head : head + 1]
            delta = joint_ref[sample, heads + head : heads + head + 1]
            queries = head_rows(q_ref[sample], head, group)
            grads = head_rows(g_ref[sample], head, group)
            keys = k_ref[sample, :, lanes]
            scores = scores_t(keys, queries, valid)
            prob_grad = lax.dot_general(
                v_ref[sample, :, lanes], grads, NT, preferred_element_type=F32
            )
            probs, dscore = probs_and_dscore(scores, prob_grad, joint, delta)
            key_grad = jnp.dot(dscore, queries, preferred_element_type=F32)
            value_grad = jnp.dot(probs, grads, preferred_element_type=F32)
            key_lanes = slice(2 * head * HD, (2 * head + 1) * HD)
            value_lanes = slice((2 * head + 1) * HD, (2 * head + 2) * HD)
            grad_ref[token, key_lanes] = key_grad.astype(BF16)
            grad_ref[token, value_lanes] = value_grad.astype(BF16)
            dq = lax.dot_general(dscore, keys, TN, preferred_element_type=F32).astype(BF16)
            for r in range(group):
                column = (head * group + r) * HD
                dq_ref[sample, :, column : column + HD] = dq[r * rows : (r + 1) * rows]


def own_grads(question_q, question_grad, keys, values, joint, group):
    samples, rows, width = question_q.shape
    heads = keys.shape[2] // HD
    return pl.pallas_call(
        functools.partial(own_grads_kernel, group),
        out_shape=(
            jax.ShapeDtypeStruct((samples * rows, 2 * heads * HD), BF16),
            jax.ShapeDtypeStruct((samples, rows, width), BF16),
        ),
        in_specs=[whole()] * 5,
        out_specs=(whole(), whole()),
        compiler_params=params(),
        cost_estimate=cost(3 * 10**8, 3 * 2**20, 10**5),
        name="own_grads",
    )(question_q, question_grad, keys, values, joint)


def sum_dq_kernel(heads, owners, *refs):
    out_ref = refs[-1]
    own_ref = refs[-2]
    per = (len(refs) - 2) // heads
    width = refs[0].shape[2]
    for head in range(heads):
        lanes = slice(head * width, (head + 1) * width)
        total = own_ref[0, :, lanes].astype(F32)
        for ref in refs[head * per : (head + 1) * per]:
            total = total + ref[0].astype(F32)
        out_ref[0, :, lanes] = total.astype(BF16)


def sum_dq(table, returned, own):
    samples, rows, width = own.shape
    peers = returned[0].shape[0]
    per = peers // samples
    heads = len(returned)
    first = table.shape[0] - peers

    def from_owner(k):
        return pl.BlockSpec((1, rows, width // heads), lambda s, o: (o[first + s * per + k], 0, 0))

    return pl.pallas_call(
        functools.partial(sum_dq_kernel, heads),
        out_shape=jax.ShapeDtypeStruct((samples, rows, width), BF16),
        grid_spec=pltpu.PrefetchScalarGridSpec(
            num_scalar_prefetch=1,
            grid=(samples,),
            in_specs=[from_owner(k) for k in range(per)] * heads
            + [pl.BlockSpec((1, rows, width), lambda s, o: (s, 0, 0))],
            out_specs=pl.BlockSpec((1, rows, width), lambda s, o: (s, 0, 0)),
        ),
        compiler_params=params(),
        cost_estimate=cost(2 * 10**6, 4 * 2**20),
        name="sum_dq",
    )(table, *[one for one in returned for _ in range(per)], own)


def add_kernel(count, blocks_ref, *refs):
    outs = refs[len(refs) - count :]
    for k, (arrived, out_ref) in enumerate(zip(refs, outs)):
        out_ref[...] = (blocks_ref[k].astype(F32) + arrived[...].astype(F32)).astype(BF16)


def add_arrived(blocks, arrived, after, name):
    count = len(arrived)
    return pl.pallas_call(
        functools.partial(add_kernel, count),
        out_shape=tuple(jax.ShapeDtypeStruct(one.shape, BF16) for one in arrived),
        in_specs=[whole()] * (1 + count) + [pl.BlockSpec(memory_space=pl.ANY)],
        out_specs=(whole(),) * count,
        compiler_params=params(),
        cost_estimate=cost(8 * 10**9, 2**20),
        name=name,
    )(blocks, *arrived, after)


def last_kernel(heads, blocks_ref, *refs):
    out_ref = refs[-1]
    for head in range(heads):
        total = blocks_ref[head].astype(F32)
        for ref in refs[2 * head : 2 * head + 2]:
            total = total + ref[...].astype(F32)
        width = total.shape[1]
        out_ref[:, head * width : (head + 1) * width] = total.astype(BF16)


def last_sums(blocks, arrived):
    heads, share, width = blocks.shape
    return pl.pallas_call(
        functools.partial(last_kernel, heads),
        out_shape=jax.ShapeDtypeStruct((share, heads * width), BF16),
        in_specs=[whole()] * (1 + 2 * heads),
        out_specs=whole(),
        compiler_params=params(),
        cost_estimate=cost(10**6, 2**21),
        name="weights_last",
    )(blocks, *arrived)


def travel(blocks, head):
    count = lax.axis_size("pass")
    ways = [direction(head), -direction(head)]
    return [
        lax.ppermute(block, "pass", [(i, (i + way) % count) for i in range(count)])
        for block, way in zip(blocks, ways)
    ]


def direction(head):
    return 1 if head % 2 == 0 else -1


def finish_kernel(heads, x_ref, out_ref):
    owners, cores, _, _ = x_ref.shape
    for core in range(cores):
        total = x_ref[0, core].astype(F32)
        for owner in range(1, owners):
            total = total + x_ref[owner, core].astype(F32)
        for head in range(heads):
            lanes = slice((core * heads + head) * HD, (core * heads + head + 1) * HD)
            for part in range(2):
                first = (head * 2 + part) * HD
                out_ref[:, part, lanes] = total[:, first : first + HD]


def finish_weights(parts):
    owners, cores, rows, width = parts.shape
    return pl.pallas_call(
        functools.partial(finish_kernel, width // (2 * HD)),
        out_shape=jax.ShapeDtypeStruct((rows, 2, cores * width // 2), F32),
        in_specs=[whole()],
        out_specs=whole(),
        compiler_params=params(),
        cost_estimate=cost(10**6, 2**20),
        name="finish_weights",
    )(parts)


def local(
    question_q,
    question_grad,
    question_kv,
    passage_kv,
    question_hidden,
    passage_hidden,
    reuse,
    passage_blocks,
):
    peers = lax.axis_size("dp")
    groups = lax.axis_size("pass")
    cores = lax.axis_size("tensor")
    slots, slot_len, _, channels = passage_kv.shape
    samples, rows, width = question_q.shape
    heads = channels // HD
    group = width // channels
    refs = reuse.reshape(reuse.shape[0], reuse.shape[2])
    model_width = passage_hidden.shape[2]

    def exchange(x):
        return lax.all_to_all(x, "dp", split_axis=0, concat_axis=0, tiled=True)

    def from_partner(x):
        return lax.ppermute(x, "tensor", [(i, cores - 1 - i) for i in range(cores)])

    me = lax.axis_index("dp")
    blocks = lax.dynamic_index_in_dim(passage_blocks, me, 0, keepdims=False).reshape(slots)
    packed, table, kv = pack_queries(refs, blocks, question_q, question_grad, passage_kv)
    packed, table, kv = lax.optimization_barrier((packed, table, kv))
    got = exchange(packed)
    got, passage_hidden, question_hidden, question_kv, question_q, question_grad = (
        lax.optimization_barrier(
            (got, passage_hidden, question_hidden, question_kv, question_q, question_grad)
        )
    )
    own_keys, own_values = question_kv[:, :, 0], question_kv[:, :, 1]

    parts = owner_stats(table, got, kv, group)
    parts, own_keys, own_values, passage_hidden, question_hidden = lax.optimization_barrier(
        (parts, own_keys, own_values, passage_hidden, question_hidden)
    )
    stats = exchange(parts)
    own = own_stats(question_q, question_grad, own_keys, own_values, group)
    hidden = [
        one.reshape(-1, model_width)
        for both in (passage_hidden, question_hidden)
        for one in (both, from_partner(both))
    ]

    stats, *hidden = lax.optimization_barrier((stats, *hidden))
    back, merged = merge(refs, stats, own, slots)
    joint = exchange(back)
    grads_query, own_dq = own_grads(
        question_q, question_grad, own_keys, own_values, merged, group
    )
    joint, grads_query, own_dq = lax.optimization_barrier((joint, grads_query, own_dq))
    far = groups // 2
    depths, homes = [], {}

    def array_of(*blocks):
        for row, block in enumerate(blocks):
            homes[block] = (len(depths), row)
        depths.append(len(blocks))
        return len(depths) - 1

    firsts, pairs = [], {}
    for head in range(heads):
        way = direction(head)
        firsts.append((array_of((far, head)), array_of((way * (1 - far), head))))
    for distance in range(far - 1, 0, -1):
        for head in range(heads):
            way = direction(head)
            pair = [(way * distance, head), (way * (1 - distance), head)]
            pairs[distance, head] = array_of(*(pair if distance > 1 else pair[:1]))
    final = array_of(*[(0, head) for head in range(heads)])
    places = [
        (place, [(head, *home) for (one, head), home in homes.items() if one == place])
        for place in [far, *range(far - 1, -far, -1)]
    ]
    grads_pass, dq_parts, *blocks = owner_grads(
        places, depths, table, got, joint, kv, hidden, grads_query, groups
    )
    sums = [
        travel([blocks[ahead][0], blocks[behind][0]], head)
        for head, (ahead, behind) in enumerate(firsts)
    ]
    ends = [None] * heads
    after = grads_pass
    for distance in range(far - 1, 0, -1):
        for head in range(heads):
            arrived = sums[head]
            if distance == 1:
                ends[head] = arrived[1]
                arrived = arrived[:1]
            added = add_arrived(
                blocks[pairs[distance, head]], arrived, after, f"add_{head}_{distance}"
            )
            after = added[0]
            sums[head] = travel(added, head)
    returned = exchange(dq_parts)
    summed = last_sums(
        blocks[final], [one for head in range(heads) for one in (sums[head][0], ends[head])]
    )
    summed, returned = lax.optimization_barrier((summed, returned))
    question_dq = sum_dq(table, [returned], own_dq)

    share = summed.shape[0] // (peers * cores)
    parts = lax.all_to_all(
        summed.reshape(peers * cores, share, -1),
        ("dp", "tensor"),
        split_axis=0,
        concat_axis=0,
        tiled=True,
    )
    weight_grad = finish_weights(parts.reshape(peers, cores, share, -1))
    question_dkv = jnp.swapaxes(grads_query.reshape(samples, rows, heads, 2, HD), 2, 3)
    question_dkv = question_dkv.reshape(samples, rows, 2, channels)
    passage_dkv = jnp.swapaxes(grads_pass.reshape(slots, slot_len, heads, 2, HD), 2, 3)
    passage_dkv = passage_dkv.reshape(slots, slot_len, 2, channels)
    return (question_dq, question_dkv, passage_dkv, weight_grad)


def solution(mesh):
    in_specs = (
        P(("dp", "pass"), None, "tensor"),
        P(("dp", "pass"), None, "tensor"),
        P(("dp", "pass"), None, None, "tensor"),
        P(("dp", "pass"), None, None, "tensor"),
        P(("dp", "pass"), "tensor", None),
        P(("dp", "pass"), "tensor", None),
        P(None, "pass", None),
        P(None, "pass", None),
    )
    out_specs = (
        P(("dp", "pass"), None, "tensor"),
        P(("dp", "pass"), None, None, "tensor"),
        P(("dp", "pass"), None, None, "tensor"),
        P(("dp", "pass", "tensor"), None, None),
    )
    return jax.shard_map(local, mesh=mesh, in_specs=in_specs, out_specs=out_specs, check_vma=False)
```
